32 devices in a mesh: dp: 8 (over z, y), chan: 4 (over x, core).
Axes of the slice: x: 2, y: 2, z: 4, core: 2. Of those that a mesh axis runs over, the one named last changes fastest.
Arguments:
- inputs: bfloat16 [32768, 1024], P('dp', 'chan'), may hold values from -6 to 6
- resolution: int32 [128], P('dp'), may hold values from 0 to 2, as said below
- reduce_weight: bfloat16 [1024, 256], replicated, may hold values from -0.1875 to 0.1875
- first_gain: float32 [256], P('chan'), may hold values from 0.5 to 1.5
- first_shift: float32 [256], P('chan'), may hold values from -3 to 3
- split_weight: bfloat16 [9, 128, 512], P(None, None, 'chan'), may hold values from -0.1875 to 0.1875
- second_gain: float32 [512], P('chan'), may hold values from 0.5 to 1.5
- second_shift: float32 [512], P('chan'), may hold values from -3 to 3
- gate_down: float32 [256, 128], replicated, may hold values from -0.375 to 0.375
- gate_gain: float32 [128], replicated, may hold values from 0.5 to 1.5
- gate_shift: float32 [128], replicated, may hold values from -3 to 3
- gate_up: float32 [128, 512], replicated, may hold values from -0.5 to 0.5
- gate_bias: float32 [512], replicated, may hold values from -3 to 3
- expand_weight: bfloat16 [256, 1024], P(None, 'chan'), may hold values from -0.375 to 0.375
- third_gain: float32 [1024], P('chan'), may hold values from 0.5 to 1.5
- third_shift: float32 [1024], P('chan'), may hold values from -3 to 3
- cotangent: bfloat16 [32768, 1024], P('dp', 'chan'), may hold values from -6 to 6
Outputs:
- block_out: bfloat16 [32768, 1024], P('dp', 'chan')
- inputs_grad: bfloat16 [32768, 1024], P('dp', 'chan')
- reduce_grad: float32 [1024, 256], P(None, 'chan')
- first_gain_grad: float32 [256], P('chan')
- first_shift_grad: float32 [256], P('chan')
- split_grad: float32 [9, 128, 512], P(None, None, 'chan')
- second_gain_grad: float32 [512], P('chan')
- second_shift_grad: float32 [512], P('chan')
- down_grad: float32 [256, 128], P(None, 'chan')
- gate_gain_grad: float32 [128], P('chan')
- gate_shift_grad: float32 [128], P('chan')
- up_grad: float32 [128, 512], P(None, 'chan')
- bias_grad: float32 [512], P('chan')
- expand_grad: float32 [256, 1024], P(None, 'chan')
- third_gain_grad: float32 [1024], P('chan')
- third_shift_grad: float32 [1024], P('chan')
The draws below stay inside these ranges and needn't reach their ends.
Inputs may be any that keep to these rules, and one draw needn't show every extreme that they name: Image i has side 12 + 2 * resolution[i] pixels inside its 16 x 16 slot; group 2 fills the slot.
All inputs are finite; a program needn't handle non-finite values.
Results may differ from the reference program's by a relative error of at most 0.02.
Values may be sent and summed in bfloat16 or wider, within the bound.
A program may use at most 128 MiB of HBM per device.

```python
import jax
import jax.numpy as jnp
from jax import lax

C = 1024
P_SIZE = 256
A = 128
SIDE = 16
IMG_DEV = 16
IMAGES = 128
ROWS = 32768


def draw_resolution(key, part):
    key = jax.random.fold_in(key, 5)
    key_level, key_pick, key_free = jax.random.split(key, 3)
    devices = IMAGES // IMG_DEV
    level = jax.random.randint(key_level, (devices, 1), 0, 3)
    pick = jax.random.randint(key_pick, (devices, IMG_DEV), 0, 2)
    spread = jax.random.randint(key_free, (devices, IMG_DEV), 0, 3)
    groups = jnp.where(pick == 0, level, spread).reshape(IMAGES)
    groups = groups.at[0].set(2).at[1].set(0)
    return groups.astype(jnp.int32)


def levels(stream_key, dims, cuts, low, high):
    factor_of = 1.0
    for axis_at, blocks in cuts:
        steps = jax.random.uniform(jax.random.fold_in(jax.random.fold_in(stream_key, 6), axis_at), (blocks,), jnp.float32, low / len(cuts), high / len(cuts))
        factor_of = factor_of * jnp.repeat(jnp.exp(steps), dims[axis_at] // blocks).reshape((-1,) + (1,) * (len(dims) - 1 - axis_at))
    return factor_of


def gaussian(stream_key, shape, scale, limit, cuts=(), dtype=jnp.bfloat16):
    level = levels(stream_key, shape, cuts, -0.22, 0.18) if cuts else 1.0
    drawn = jax.random.normal(stream_key, shape, jnp.float32) * scale * level
    return jnp.minimum(jnp.maximum(drawn, -limit), limit).astype(dtype)


def setup_inputs(seed: int = 0) -> dict:
    key_of = jax.random.split(jax.random.key(seed), 18)
    inputs = gaussian(key_of[0], (ROWS, C), 1.0, 6.0, ((0, 8), (1, 4)))
    resolution = draw_resolution(jax.random.fold_in(key_of[17], 71), 0)
    reduce_weight = gaussian(key_of[2], (C, P_SIZE), C ** -0.5, 0.1875)
    first_gain = jnp.clip(1.0 + 0.1 * jax.random.normal(key_of[3], (P_SIZE,), jnp.float32), 0.5, 1.5)
    first_shift = gaussian(key_of[4], (P_SIZE,), 0.5, 3.0, ((0, 4),), jnp.float32)
    split_weight = gaussian(key_of[5], (9, P_SIZE // 2, 2 * P_SIZE), (9 * P_SIZE // 2) ** -0.5, 0.1875, ((2, 4),))
    second_gain = jnp.clip(1.0 + 0.1 * jax.random.normal(key_of[6], (2 * P_SIZE,), jnp.float32), 0.5, 1.5)
    second_shift = gaussian(key_of[7], (2 * P_SIZE,), 0.5, 3.0, ((0, 4),), jnp.float32)
    gate_down = gaussian(key_of[8], (P_SIZE, A), P_SIZE ** -0.5, 0.375, (), jnp.float32)
    gate_gain = jnp.clip(1.0 + 0.1 * jax.random.normal(key_of[9], (A,), jnp.float32), 0.5, 1.5)
    gate_shift = gaussian(key_of[10], (A,), 0.5, 3.0, (), jnp.float32)
    gate_up = gaussian(key_of[11], (A, 2 * P_SIZE), A ** -0.5, 0.5, (), jnp.float32)
    gate_bias = gaussian(key_of[12], (2 * P_SIZE,), 0.5, 3.0, (), jnp.float32)
    expand_weight = gaussian(key_of[13], (P_SIZE, C), P_SIZE ** -0.5, 0.375, ((1, 4),))
    third_gain = jnp.clip(1.0 + 0.1 * jax.random.normal(key_of[14], (C,), jnp.float32), 0.5, 1.5)
    third_shift = gaussian(key_of[15], (C,), 0.5, 3.0, ((0, 4),), jnp.float32)
    cotangent = gaussian(key_of[16], (ROWS, C), 1.0, 6.0, ((0, 8), (1, 4)))
    return dict(inputs=inputs, resolution=resolution, reduce_weight=reduce_weight, first_gain=first_gain, first_shift=first_shift, split_weight=split_weight, second_gain=second_gain, second_shift=second_shift, gate_down=gate_down, gate_gain=gate_gain, gate_shift=gate_shift, gate_up=gate_up, gate_bias=gate_bias, expand_weight=expand_weight, third_gain=third_gain, third_shift=third_shift, cotangent=cotangent)


eps = 1e-05
highest = lax.Precision.HIGHEST

@jax.custom_vjp
def low(v):
    return lax.optimization_barrier(v.astype(jnp.bfloat16)).astype(jnp.float32)

@jax.custom_vjp
def low_back(v):
    return v

def low_keep(v):
    return (low(v), None)

def low_pass(kept, grad):
    return (grad,)

def back_keep(v):
    return (v, None)

def back_low(kept, grad):
    return (low(grad),)
low.defvjp(low_keep, low_pass)
low_back.defvjp(back_keep, back_low)

def batch_norm(values, weight, gain, shift):
    count = jnp.sum(weight)
    mean = lax.optimization_barrier(jnp.sum(weight * values, 0)) / count
    spread = lax.optimization_barrier(jnp.sum(weight * (values - mean) ** 2, 0)) / count
    return gain * (values - mean) * lax.rsqrt(spread + eps) + shift

def radix_weights(logits, width):
    first = logits[:, :width]
    second = logits[:, width:]
    top = jnp.maximum(first, second)
    upper = jnp.exp(first - top)
    lower = jnp.exp(second - top)
    total = upper + lower
    return jnp.concatenate([upper / total, lower / total], 1)

def reference(inputs, resolution, reduce_weight, first_gain, first_shift, split_weight, second_gain, second_shift, gate_down, gate_gain, gate_shift, gate_up, gate_bias, expand_weight, third_gain, third_shift, cotangent):
    images = resolution.shape[0]
    width = reduce_weight.shape[1]
    rows = inputs.shape[0]
    sides = 12 + 2 * resolution
    places = jnp.arange(SIDE)
    valid = ((places[None, :, None] < sides[:, None, None]) & (places[None, None, :] < sides[:, None, None])).astype(jnp.float32)
    pixel_mask = valid.reshape(rows, 1)
    pixels = (sides * sides).astype(jnp.float32)
    image_ones = jnp.ones((images, 1), jnp.float32)

    def forward(features, reduce_w, gain_one, shift_one, split_w, gain_two, shift_two, down_w, gain_gate, shift_gate, up_w, bias_up, expand_w, gain_three, shift_three):
        reduced = low_back(jnp.dot(features, reduce_w, precision=highest))
        first_act = low(pixel_mask * jax.nn.silu(batch_norm(reduced, pixel_mask, gain_one, shift_one)))
        kernel = split_w.reshape(3, 3, width // 2, 2 * width)
        splits = lax.conv_general_dilated(first_act.reshape(images, SIDE, SIDE, width), kernel, (1, 1), 'SAME', dimension_numbers=('NHWC', 'HWIO', 'NHWC'), feature_group_count=2, precision=highest)
        splits = low_back(splits.reshape(rows, 2 * width))
        second_act = pixel_mask * jax.nn.silu(batch_norm(splits, pixel_mask, gain_two, shift_two))
        per_image = second_act.reshape(images, SIDE * SIDE, 2 * width)
        pooled = lax.optimization_barrier(jnp.sum(per_image, 1)) / pixels[:, None]
        summary = pooled[:, :width] + pooled[:, width:]
        squeezed = jnp.dot(summary, down_w, precision=highest)
        squeezed = jax.nn.silu(batch_norm(squeezed, image_ones, gain_gate, shift_gate))
        logits = jnp.dot(squeezed, up_w, precision=highest) + bias_up
        attention = radix_weights(logits, width)
        weighted = low((per_image * attention[:, None, :]).reshape(rows, 2 * width))
        merged = low(weighted[:, :width] + weighted[:, width:])
        expanded = low_back(jnp.dot(merged, expand_w, precision=highest))
        return pixel_mask * jax.nn.silu(batch_norm(expanded, pixel_mask, gain_three, shift_three) + features)
    block_out, pullback = jax.vjp(forward, inputs.astype(jnp.float32), reduce_weight.astype(jnp.float32), first_gain, first_shift, split_weight.astype(jnp.float32), second_gain, second_shift, gate_down, gate_gain, gate_shift, gate_up, gate_bias, expand_weight.astype(jnp.float32), third_gain, third_shift)
    grads = pullback(cotangent.astype(jnp.float32))
    return (block_out.astype(jnp.bfloat16), grads[0].astype(jnp.bfloat16), grads[1], grads[2], grads[3], grads[4], grads[5], grads[6], grads[7], grads[8], grads[9], grads[10], grads[11], grads[12], grads[13], grads[14])
```

```python
import functools
import types

import jax
import jax.numpy as jnp
from jax import lax
from jax.experimental import pallas as pl
from jax.experimental.pallas import tpu as pltpu
from jax.sharding import PartitionSpec as P

SIDE = 16
CELLS = SIDE * SIDE
TALL = CELLS + 2 * SIDE
LANES = 128
EPS = 1e-05
HIGHEST = lax.Precision.HIGHEST
F32 = jnp.float32
BF16 = jnp.bfloat16
MESH = pl.DeviceIdType.MESH
STRIP = 32


def wide(mask, width):
    return mask if width == LANES else jnp.concatenate([mask] * (width // LANES), axis=1)


def fold(values):
    return jnp.sum(values.reshape(values.shape[0] // 8, 8, values.shape[1]), axis=0)


def total(values):
    return jnp.sum(values, axis=0, keepdims=True)


def sigmoid(values):
    return 0.5 * jnp.tanh(0.5 * values) + 0.5


def dot(left, right):
    return jnp.dot(left, right, preferred_element_type=F32)


def exact(left, right):
    return jnp.dot(left, right, precision=HIGHEST, preferred_element_type=F32)


def exact_nt(left, right):
    return lax.dot_general(
        left, right, (((1,), (1,)), ((), ())), precision=HIGHEST, preferred_element_type=F32
    )


def exact_tn(left, right):
    return lax.dot_general(
        left, right, (((0,), (0,)), ((), ())), precision=HIGHEST, preferred_element_type=F32
    )


def flip(values):
    return values.astype(F32).T.astype(values.dtype)


def put(ref, row, vector):
    for part in range(vector.shape[1] // LANES):
        ref[0, row + part : row + part + 1, :] = vector[:, part * LANES : (part + 1) * LANES]


def get(block, row, width):
    parts = [block[row + q : row + q + 1, :] for q in range(width // LANES)]
    return parts[0] if len(parts) == 1 else jnp.concatenate(parts, axis=1)


def kernel(c, names, *refs):
    r = types.SimpleNamespace(**dict(zip(names, refs)))
    DP, CH, X, D, ipd, images = c.DP, c.CH, c.X, c.D, c.ipd, c.images
    width, cw, inner, m1, m2, mg = c.width, c.cw, c.inner, c.m1, c.m2, c.mg
    half, two = width // 2, 2 * width
    own_rows = ipd * CELLS
    taps = 9 * half
    dp = lax.axis_index("dp")
    ch = lax.axis_index("chan")
    core = ch % 2
    chip = ch // 2
    mate = (dp, ch + 1 - 2 * core)
    f0 = ((0, 0), (0, 0))

    def remote(src, dst, send, recv, device):
        return pltpu.make_async_remote_copy(
            src_ref=src, dst_ref=dst, send_sem=send, recv_sem=recv, device_id=device, device_id_type=MESH
        )

    def drain(ref, sem):
        pltpu.make_async_copy(ref, ref, sem).wait()

    def loop(count, body):
        def step(i, carry):
            body(i)
            return carry

        lax.fori_loop(0, count, step, 0)

    def peer(t):
        return (dp, ((chip + t) % X) * 2 + core)

    def across(d):
        return ((dp + d) % DP, ch)

    def block_of(t, same):
        return ((chip + t) % X) * 2 + (core if same else 1 - core)

    def rows_of(b, i):
        return pl.ds(pl.multiple_of((b * ipd + i) * CELLS, CELLS), CELLS)

    def block_rows(b):
        return pl.ds(pl.multiple_of(b * own_rows, own_rows), own_rows)

    def image(i):
        return pl.ds(pl.multiple_of(i * CELLS, CELLS), CELLS)

    def strips(base, body, carry, size=STRIP):
        def step(k, state):
            return body(pl.ds(pl.multiple_of(base + k * size, size), size), k, state)

        return lax.fori_loop(0, CELLS // size, step, carry)

    def everyone(buf, k, message=None):
        message = buf.at[0] if message is None else message

        def one(j, carry):
            d, q = j // CH, j % CH
            slot = ((DP - d) % DP) * CH + (CH - q) % CH
            remote(buf.at[0], buf.at[slot], r.all_send.at[k], r.all_recv.at[k], ((dp + d) % DP, (ch + q) % CH)).start()
            return carry

        lax.fori_loop(1, D, one, 0)

    def everyone_wait(buf, k):
        drain(buf.at[pl.ds(1, D - 1)], r.all_recv.at[k])

    def everyone_done(buf, k):
        drain(buf.at[pl.ds(1, D - 1)], r.all_send.at[k])

    def column(buf, k):
        for d in range(1, DP):
            remote(buf.at[0], buf.at[DP - d], r.col_send.at[k], r.col_recv.at[k], across(d)).start()

    def column_wait(buf, k):
        drain(buf.at[pl.ds(1, DP - 1)], r.col_recv.at[k])

    def column_done(buf, k):
        drain(buf.at[pl.ds(1, DP - 1)], r.col_send.at[k])

    class Scatter:
        def __init__(self, k, stage, inward, outward, landed, keep):
            self.k, self.stage, self.inward = k, stage, inward
            self.outward, self.landed, self.keep = outward, landed, keep

        def compute_mate(self, t, part):
            def body(i):
                self.stage[t, i] = part(block_of(t, False), i).astype(BF16)

            loop(ipd, body)

        def send_mate(self, t):
            def body(i):
                remote(
                    self.stage.at[t, i], self.inward.at[t, i],
                    r.rs_core_send.at[self.k], r.rs_core_recv.at[self.k, t, i], mate,
                ).start()

            loop(ipd, body)

        def to_mate(self, t, part):
            def body(i):
                self.stage[t, i] = part(block_of(t, False), i).astype(BF16)
                remote(
                    self.stage.at[t, i], self.inward.at[t, i],
                    r.rs_core_send.at[self.k], r.rs_core_recv.at[self.k, t, i], mate,
                ).start()

            loop(ipd, body)

        def to_peer(self, t, part):
            def body(i):
                value = part(block_of(t, True), i)
                drain(self.inward.at[t, i], r.rs_core_recv.at[self.k, t, i])
                self.outward[t - 1, i] = (value + self.inward[t, i].astype(F32)).astype(BF16)
                remote(
                    self.outward.at[t - 1, i], self.landed.at[X - t - 1, i],
                    r.rs_chip_send.at[self.k], r.rs_chip_recv.at[self.k, X - t, i], peer(t),
                ).start()

            loop(ipd, body)

        def own(self, part):
            def body(i):
                value = part(ch, i)
                drain(self.inward.at[0, i], r.rs_core_recv.at[self.k, 0, i])
                self.keep[image(i), :] = value + self.inward[0, i].astype(F32)

            loop(ipd, body)

        def arrive(self, i):
            for t in range(1, X):
                drain(self.landed.at[t - 1, i], r.rs_chip_recv.at[self.k, t, i])

        def extra(self, i, at, lanes):
            value = self.landed[0, i, at, lanes].astype(F32)
            for t in range(2, X):
                value = value + self.landed[t - 1, i, at, lanes].astype(F32)
            return value

        def done(self):
            drain(self.stage, r.rs_core_send.at[self.k])
            drain(self.outward, r.rs_chip_send.at[self.k])

    class Gather:
        def __init__(self, k, place, whole, pieces):
            self.k, self.place, self.whole, self.pieces = k, place, whole, pieces

        def send(self, i):
            src = self.place(ch, i)
            remote(src, src, r.ag_core_send.at[self.k], r.ag_core_recv.at[self.k, i], mate).start()
            for t in range(1, X):
                remote(src, src, r.ag_chip_send.at[self.k, t], r.ag_chip_recv.at[self.k, X - t, i], peer(t)).start()

        def from_mate(self, i):
            drain(self.place(block_of(0, False), i), r.ag_core_recv.at[self.k, i])

        def from_peer(self, t, i):
            ref = self.place(block_of(t, True), i)
            drain(ref, r.ag_chip_recv.at[self.k, t, i])
            remote(ref, ref, r.ag_pass_send.at[self.k, t], r.ag_pass_recv.at[self.k, t, i], mate).start()

        def from_pass(self, t, i):
            drain(self.place(block_of(t, False), i), r.ag_pass_recv.at[self.k, t, i])

        def done(self):
            drain(self.whole(ch), r.ag_core_send.at[self.k])
            for t in range(1, X):
                drain(self.whole(ch), r.ag_chip_send.at[self.k, t])
                drain(self.whole(block_of(t, True)), r.ag_pass_send.at[self.k, t])

    barrier = pltpu.get_barrier_semaphore()

    def greet(j, carry):
        pl.semaphore_signal(
            barrier, inc=1, device_id=((dp + j // CH) % DP, (ch + j % CH) % CH), device_id_type=MESH
        )
        return carry

    lax.fori_loop(1, D, greet, 0)

    load_w = pltpu.make_async_copy(
        r.reduce_weight.at[pl.ds(pl.multiple_of(ch * cw, cw), cw)], r.wr, r.load.at[0]
    )
    load_w.start()
    order = []
    for t in list(range(1, X)) + [0]:
        order += [block_of(t, False), block_of(t, True)]
    loads = []
    for k, b in enumerate(order):
        at = pl.ds(pl.multiple_of(b * own_rows, own_rows), own_rows)
        loads.append(pltpu.make_async_copy(r.inputs.at[at], r.xv.at[at], r.load.at[2 + k]))
        loads[-1].start()
    load_c = pltpu.make_async_copy(r.cotangent, r.cv, r.load.at[1])
    load_c.start()

    row_at = lax.broadcasted_iota(jnp.int32, (CELLS, LANES), 0)
    spot_r = lax.shift_right_logical(row_at, 4)
    spot_c = lax.bitwise_and(row_at, 15)

    def make_mask(j):
        side = 12 + 2 * r.resolution[j]
        mask = jnp.where(jnp.logical_and(spot_r < side, spot_c < side), 1.0, 0.0)
        r.area[pl.ds(j, 1), :] = jnp.full((1, LANES), side * side, jnp.int32).astype(F32)
        r.maskf[image(j), :] = mask
        r.maskb[image(j), :] = mask.astype(BF16)

    loop(images, make_mask)

    def selector(parts, mine):
        row = lax.broadcasted_iota(jnp.int32, (mine, mine * parts), 0)
        col = lax.broadcasted_iota(jnp.int32, (mine, mine * parts), 1)
        return jnp.where(col == row + ch * mine, 1.0, 0.0)

    pick1 = selector(CH, m1)
    pick2 = selector(CH, m2)
    pickg = selector(CH, mg)
    r.pbuf[0, 0:1, 0:width] = exact(r.first_gain[...], pick1)
    r.pbuf[0, 1:2, 0:width] = exact(r.first_shift[...], pick1)
    r.pbuf[0, 2:3, :] = exact(r.second_gain[...], pick2)
    r.pbuf[0, 3:4, :] = exact(r.second_shift[...], pick2)

    def part_reduce(b, i):
        at = rows_of(b, i)
        x = r.xv[at, :] * wide(r.maskb[at, :], cw)
        r.xv[at, :] = x
        return dot(x, r.wr[...])

    load_w.wait()
    rs1 = Scatter(0, r.stage, r.inward, r.outward, r.landed, r.red)
    loads[0].wait()
    rs1.compute_mate(1, part_reduce)
    pl.semaphore_wait(barrier, D - 1)
    rs1.send_mate(1)
    for t in range(1, X):
        if t > 1:
            loads[2 * t - 2].wait()
            rs1.to_mate(t, part_reduce)
        loads[2 * t - 1].wait()
        rs1.to_peer(t, part_reduce)
    loads[2 * X - 2].wait()
    rs1.to_mate(0, part_reduce)
    loads[2 * X - 1].wait()
    rs1.own(part_reduce)

    for q in range(1, CH):
        remote(r.pbuf.at[0], r.pbuf.at[CH - q], r.par_send.at[0], r.par_recv.at[CH - q], (dp, (ch + q) % CH)).start()
    r.wg[ch] = r.split_weight[...]
    gw = Gather(3, lambda b, i: r.wg.at[b], lambda b: r.wg.at[b], 1)
    gw.send(0)

    r.wrt[...] = flip(r.wr[...])
    r.wet[...] = flip(r.expand_weight[...])

    def turn_x(j):
        r.xt[j] = flip(r.xv[image(j), :])

    loop(images, turn_x)
    for g in range(2):
        for i in range(ipd):
            r.act[g, i, 0:SIDE, :] = jnp.zeros((SIDE, 3 * half), BF16)
            r.act[g, i, CELLS + SIDE : TALL, :] = jnp.zeros((SIDE, 3 * half), BF16)
            r.dsh[g, i, 0:SIDE, :] = jnp.zeros((SIDE, 3 * width), BF16)
            r.dsh[g, i, CELLS + SIDE : TALL, :] = jnp.zeros((SIDE, 3 * width), BF16)

    def finish_reduce(i, state):
        rs1.arrive(i)

        def body(at, k, state):
            first, second = state
            value = r.red[at, :] + rs1.extra(i, pl.ds(pl.multiple_of(k * STRIP, STRIP), STRIP), slice(None))
            r.red[at, :] = value
            return (first + fold(value), second + fold(value * value))

        return strips(i * CELLS, body, state)

    zero8 = jnp.zeros((8, width), F32)
    first, second = lax.fori_loop(0, ipd, finish_reduce, (zero8, zero8))

    pixels = lax.fori_loop(
        0, ipd, lambda i, count: count + r.area[pl.ds(ch * ipd + i, 1), :], jnp.zeros((1, LANES), F32)
    )
    r.g1[0] = jnp.zeros((8, LANES), F32)
    put(r.g1, 0, total(first))
    put(r.g1, width // LANES, total(second))
    r.g1[0, 6:7, :] = pixels
    everyone(r.g1, 0)

    everyone_wait(r.g1, 0)
    sums = jnp.sum(r.g1[...], axis=0)
    count = sums[6:7, 0:1]
    inverse = 1.0 / count
    params = r.pbuf[0]
    for q in range(1, CH):
        drain(r.pbuf.at[q], r.par_recv.at[q])
        params = params + r.pbuf[q]
    gain1, shift1 = params[0:1, 0:width], params[1:2, 0:width]
    gain2, shift2 = params[2:3, :], params[3:4, :]
    for t in range(1, X):
        gw.from_peer(t, 0)

    def moments(first, second):
        mean = first * inverse
        return mean, lax.rsqrt(second * inverse - mean * mean + EPS)

    mean1, scale1 = moments(get(sums, 0, width), get(sums, width // LANES, width))

    place_x = lambda b, i: r.xh1.at[rows_of(b, i)]
    gx = Gather(0, place_x, lambda b: r.xh1.at[block_rows(b)], ipd)

    strip_c = lax.bitwise_and(lax.broadcasted_iota(jnp.int32, (STRIP, LANES), 0), 15)
    not_first = strip_c != 0
    not_last = strip_c != 15

    def first_act(i):
        def body(at, k, carry):
            there = pl.ds(pl.multiple_of((ch * ipd + i) * CELLS + k * STRIP, STRIP), STRIP)
            put_at = pl.ds(pl.multiple_of(SIDE + k * STRIP, SIDE), STRIP)
            mask = r.maskf[there, :]
            for g in range(2):
                lanes = slice(g * half, (g + 1) * half)
                xh = (r.red[at, lanes] - mean1[:, lanes]) * scale1[:, lanes]
                h = gain1[:, lanes] * xh + shift1[:, lanes]
                s = sigmoid(h)
                y = h * s
                r.red[at, lanes] = xh
                r.xh1[there, lanes] = xh.astype(BF16)
                r.slope1[at, lanes] = mask * (s + y - y * s)
                a = mask * y
                before = jnp.where(not_first, pltpu.roll(a, 1, 0), 0.0)
                after = jnp.where(not_last, pltpu.roll(a, STRIP - 1, 0), 0.0)
                r.act[g, i, put_at, 0:half] = before.astype(BF16)
                r.act[g, i, put_at, half : 2 * half] = a.astype(BF16)
                r.act[g, i, put_at, 2 * half : 3 * half] = after.astype(BF16)
            return carry

        strips(i * CELLS, body, 0)
        gx.send(i)

    loop(ipd, first_act)

    gw.from_mate(0)
    for t in range(1, X):
        gw.from_pass(t, 0)
    for g in range(2):
        for q in range(CH // 2):
            r.wf[g, :, q * m2 : (q + 1) * m2] = r.wg[g * (CH // 2) + q]

    def conv(i, state):
        there = rows_of(ch, i)
        out = []
        for g in range(2):
            lanes = slice(g * width, (g + 1) * width)
            left = jnp.concatenate(
                [r.act[g, i, k * SIDE : k * SIDE + CELLS, :] for k in range(3)], axis=1
            )
            value = dot(left, r.wf[g]) * wide(r.maskf[there, :], width)
            r.sp[image(i), lanes] = value
            out.append((state[g][0] + fold(value), state[g][1] + fold(value * value)))
        return tuple(out)

    state = lax.fori_loop(0, ipd, conv, ((zero8, zero8), (zero8, zero8)))
    for g in range(2):
        put(r.g2, g * (width // LANES), total(state[g][0]))
        put(r.g2, (2 + g) * (width // LANES), total(state[g][1]))
    everyone(r.g2, 1)

    for g in range(2):
        for tap in range(9):
            r.wt[g, tap * width : (tap + 1) * width, :] = flip(r.wf[g, tap * half : (tap + 1) * half, :])

    everyone_wait(r.g2, 1)
    sums = jnp.sum(r.g2[...], axis=0)
    mean2, scale2 = moments(get(sums, 0, two), get(sums, two // LANES, two))

    r.g3[0] = jnp.zeros((8, LANES), F32)

    def second_act(i):
        def body(at, k, state):
            there = pl.ds(pl.multiple_of((ch * ipd + i) * CELLS + k * STRIP, STRIP), STRIP)
            mask = r.maskf[there, :]
            new = []
            for q in range(two // LANES):
                lanes = slice(q * LANES, (q + 1) * LANES)
                xh = (r.sp[at, lanes] - mean2[:, lanes]) * scale2[:, lanes]
                h = gain2[:, lanes] * xh + shift2[:, lanes]
                s = sigmoid(h)
                y = h * s
                r.sp[at, lanes] = xh
                r.slope2[at, lanes] = mask * (s + y - y * s)
                a = mask * y
                r.act2[at, lanes] = a
                new.append(state[q] + fold(a))
            return tuple(new)

        zero = jnp.zeros((8, LANES), F32)
        pooled = strips(i * CELLS, body, (zero,) * (two // LANES))
        share = 1.0 / r.area[pl.ds(ch * ipd + i, 1), :]
        r.share[pl.ds(i, 1), :] = share
        n = width // LANES
        for q in range(n):
            r.g3[0, pl.ds(4 * q + i, 1), :] = total(pooled[q] + pooled[n + q]) * share

    loop(ipd, second_act)
    everyone(r.g3, 2)

    gate_rows = min(D * 8, 2 * LANES)
    gate_blocks = D * 8 // gate_rows
    gate_at = lax.broadcasted_iota(jnp.int32, (gate_rows, LANES), 0)
    valid = lax.bitwise_and(gate_at, 7) < ipd
    every = 1.0 / (D * ipd)

    def gate_block(n):
        return pl.ds(pl.multiple_of(n * gate_rows, gate_rows), gate_rows)

    def lower_upper(buf, n):
        slots = gate_rows // 8
        both = buf[pl.ds(n * slots, slots)].reshape(gate_rows, LANES)
        return jnp.where(valid, both, 0.0), jnp.where(valid, pltpu.roll(both, gate_rows - 4, 0), 0.0)

    def gate_in(n, state):
        sum_lo, sum_hi = lower_upper(r.g3, n)
        pre = exact(sum_lo, r.gate_down[0:LANES, :]) + exact(sum_hi, r.gate_down[LANES:, :])
        r.gate_x[gate_block(n), :] = pre
        return state[0] + total(pre), state[1] + total(pre * pre)

    everyone_wait(r.g3, 2)
    zero1 = jnp.zeros((1, LANES), F32)
    first, second = lax.fori_loop(0, gate_blocks, gate_in, (zero1, zero1))
    gate_mean = first * every
    gate_scale = lax.rsqrt(second * every - gate_mean * gate_mean + EPS)

    def gate_out(n):
        at = gate_block(n)
        x = (r.gate_x[at, :] - gate_mean) * gate_scale
        h = r.gate_gain[...] * x + r.gate_shift[...]
        s = sigmoid(h)
        y = h * s
        r.gate_x[at, :] = x
        r.squeezed[at, :] = y
        r.gate_slope[at, :] = s + y - y * s

    loop(gate_blocks, gate_out)
    logits = exact(r.squeezed[0:8, :], r.gate_up[...]) + r.gate_bias[...]
    top = jnp.maximum(logits[:, :width], logits[:, width:])
    upper = jnp.exp(logits[:, :width] - top)
    lower = jnp.exp(logits[:, width:] - top)
    both = upper + lower
    r.att[:, 0:width] = upper / both
    r.att[:, width:two] = lower / both

    gm = Gather(1, lambda b, i: r.merged.at[rows_of(b, i)], lambda b: r.merged.at[block_rows(b)], ipd)

    def merge(i):
        att = r.att[pl.ds(i, 1), :]

        def body(at, k, carry):
            there = pl.ds(pl.multiple_of((ch * ipd + i) * CELLS + k * STRIP, STRIP), STRIP)
            left = (r.act2[at, 0:width] * att[:, 0:width]).astype(BF16)
            right = (r.act2[at, width:two] * att[:, width:two]).astype(BF16)
            r.merged[there, :] = (left.astype(F32) + right.astype(F32)).astype(BF16)
            return carry

        strips(i * CELLS, body, 0)
        gm.send(i)

    loop(ipd, merge)

    r.acc[...] = jnp.zeros((16, cw), F32)

    def expand(b, i):
        at = rows_of(b, i)
        value = dot(r.merged[at, :], r.expand_weight[...])
        r.ex[at, :] = value
        r.acc[0:8, :] += fold(value)
        r.acc[8:16, :] += fold(value * value)

    loop(ipd, lambda i: expand(ch, i))

    def expand_mate(i):
        gm.from_mate(i)
        expand(block_of(0, False), i)

    loop(ipd, expand_mate)
    for t in range(1, X):

        def expand_peer(i):
            gm.from_peer(t, i)
            expand(block_of(t, True), i)

        loop(ipd, expand_peer)
    for t in range(1, X):

        def expand_pass(i):
            gm.from_pass(t, i)
            expand(block_of(t, False), i)

        loop(ipd, expand_pass)
    put(r.c1, 0, total(r.acc[0:8, :]))
    put(r.c1, cw // LANES, total(r.acc[8:16, :]))
    column(r.c1, 0)
    load_c.wait()

    def turn_m(j):
        r.mt[j] = flip(r.merged[image(j), :])

    loop(images, turn_m)
    column_wait(r.c1, 0)
    sums = jnp.sum(r.c1[...], axis=0)
    mean3, scale3 = moments(get(sums, 0, cw), get(sums, cw // LANES, cw))
    gain3, shift3 = r.third_gain[...], r.third_shift[...]

    def outputs(j, state):
        def body(at, k, state):
            shift, cross = state
            mask = wide(r.maskf[at, :], cw)
            xh = (r.ex[at, :] - mean3) * scale3
            h = gain3 * xh + shift3 + r.xv[at, :].astype(F32)
            s = sigmoid(h)
            y = h * s
            d = r.cv[at, :].astype(F32) * mask * (s + y - y * s)
            r.cv[at, :] = (mask * y).astype(BF16)
            r.dpre[at, :] = d
            r.ex[at, :] = xh
            return (shift + fold(d), cross + fold(d * xh))

        state = strips(j * CELLS, body, state)
        pltpu.make_async_copy(r.cv.at[image(j)], r.block_out.at[image(j)], r.store.at[0]).start()
        return state

    zero_c = jnp.zeros((8, cw), F32)
    shift, cross = lax.fori_loop(0, images, outputs, (zero_c, zero_c))
    put(r.c2, 0, total(shift))
    put(r.c2, cw // LANES, total(cross))
    column(r.c2, 1)
    column_wait(r.c2, 1)
    sums = jnp.sum(r.c2[...], axis=0)
    shift_grad, gain_grad = get(sums, 0, cw), get(sums, cw // LANES, cw)
    r.third_gain_grad[...] = gain_grad
    r.third_shift_grad[...] = shift_grad
    lead3, base3, slant3 = gain3 * scale3, shift_grad * inverse, gain_grad * inverse

    def part_merged(b, i):
        def body(at, k, carry):
            mask = wide(r.maskf[at, :], cw)
            d = mask * lead3 * (r.dpre[at, :] - base3 - r.ex[at, :] * slant3)
            r.de[at, :] = d.astype(BF16)
            return carry

        strips((b * ipd + i) * CELLS, body, 0)
        return dot(r.de[rows_of(b, i), :], r.wet[...])

    rs1.done()
    rs2 = Scatter(1, r.stage, r.inward2, r.outward, r.landed2, r.dm)
    for t in range(1, X):
        rs2.to_mate(t, part_merged)
        rs2.to_peer(t, part_merged)
    rs2.to_mate(0, part_merged)
    rs2.own(part_merged)

    def grow(j):
        r.eg[...] += dot(r.mt[j], r.de[image(j), :])

    r.eg[...] = dot(r.mt[0], r.de[image(0), :])
    lax.fori_loop(1, images, lambda j, carry: (grow(j), carry)[1], 0)
    piece = width // DP
    et = r.es.dtype
    r.es[...] = r.eg[...].astype(et)

    def piece_rows(d):
        return pl.ds(pl.multiple_of(((dp + d) % DP) * piece, piece), piece)

    for d in range(1, DP):
        remote(r.es.at[piece_rows(d)], r.ebuf.at[DP - d], r.eg_send.at[0], r.eg_recv.at[0], across(d)).start()

    r.g4[0] = jnp.zeros((8, LANES), F32)

    def finish_merged(i):
        rs2.arrive(i)

        def body(at, k, state):
            here = pl.ds(pl.multiple_of(k * STRIP, STRIP), STRIP)
            value = r.dm[at, :] + rs2.extra(i, here, slice(None))
            r.dm[at, :] = value
            return state + fold(value * (r.act2[at, 0:width] - r.act2[at, width:two]))

        gap = total(strips(i * CELLS, body, zero8))
        att = r.att[pl.ds(i, 1), :]
        grad = att[:, 0:width] * att[:, width:two] * gap
        for q in range(width // LANES):
            r.g4[0, pl.ds(4 * q + i, 1), :] = grad[:, q * LANES : (q + 1) * LANES]

    loop(ipd, finish_merged)
    everyone(r.g4, 3)

    drain(r.ebuf.at[pl.ds(1, DP - 1)], r.eg_recv.at[0])
    value = r.eg[piece_rows(0), :]
    for d in range(1, DP):
        value = value + r.ebuf[d].astype(F32)
    r.eo[0] = value.astype(et)
    for d in range(1, DP):
        remote(r.eo.at[0], r.eo.at[DP - d], r.eg_send.at[1], r.eg_recv.at[1], across(d)).start()

    everyone_wait(r.g4, 3)
    up_gap = r.gate_up[:, 0:width] - r.gate_up[:, width:two]

    def gate_back(n, state):
        at = gate_block(n)
        grad_lo, grad_hi = lower_upper(r.g4, n)
        grad = exact_nt(grad_lo, up_gap[:, 0:LANES]) + exact_nt(grad_hi, up_gap[:, LANES:width])
        grad = grad * r.gate_slope[at, :]
        r.grad_down[at, :] = grad
        return state[0] + total(grad), state[1] + total(grad * r.gate_x[at, :])

    gate_shift_all, gate_gain_all = lax.fori_loop(0, gate_blocks, gate_back, (zero1, zero1))
    lead = r.gate_gain[...] * gate_scale

    def gate_norm_back(n):
        at = gate_block(n)
        grad = r.grad_down[at, :] - gate_shift_all * every - r.gate_x[at, :] * (gate_gain_all * every)
        r.grad_down[at, :] = jnp.where(valid, lead * grad, 0.0)

    loop(gate_blocks, gate_norm_back)
    r.grad_summary[...] = exact_nt(r.grad_down[0:8, :], r.gate_down[...])

    def second_back(i, state):
        att = r.att[pl.ds(i, 1), :]
        flat = r.grad_summary[pl.ds(i, 1), :] * wide(r.share[pl.ds(i, 1), :], width)

        def body(at, k, state):
            d = r.dm[at, :]
            new = []
            for g in range(2):
                lanes = slice(g * width, (g + 1) * width)
                value = (d * att[:, lanes] + flat) * r.slope2[at, lanes]
                r.act2[at, lanes] = value
                new.append((state[g][0] + fold(value), state[g][1] + fold(value * r.sp[at, lanes])))
            return tuple(new)

        return strips(i * CELLS, body, state, 16)

    state = lax.fori_loop(0, ipd, second_back, ((zero8, zero8), (zero8, zero8)))
    for g in range(2):
        put(r.g5, g * (width // LANES), total(state[g][0]))
        put(r.g5, (2 + g) * (width // LANES), total(state[g][1]))
    everyone(r.g5, 4)

    r.gate_gain_grad[...] = exact_nt(gate_gain_all, pickg)
    r.gate_shift_grad[...] = exact_nt(gate_shift_all, pickg)

    def gate_grads(n, state):
        at = gate_block(n)
        sum_lo, sum_hi = lower_upper(r.g3, n)
        grad_lo, grad_hi = lower_upper(r.g4, n)
        picked = exact_nt(r.grad_down[at, :], pickg)
        down = jnp.concatenate([exact_tn(sum_lo, picked), exact_tn(sum_hi, picked)], axis=0)
        squeezed = r.squeezed[at, :]
        up = jnp.concatenate([exact_tn(squeezed, grad_lo), exact_tn(squeezed, grad_hi)], axis=1)
        bias = jnp.concatenate([total(grad_lo), total(grad_hi)], axis=1)
        return state[0] + down, state[1] + up, state[2] + bias

    down, up, bias = lax.fori_loop(
        0, gate_blocks, gate_grads,
        (jnp.zeros((width, mg), F32), jnp.zeros((inner, width), F32), jnp.zeros((1, width), F32)),
    )
    r.down_grad[...] = down
    r.up_grad[...] = exact_nt(jnp.concatenate([up, -up], axis=1), pick2)
    r.bias_grad[...] = exact_nt(jnp.concatenate([bias, -bias], axis=1), pick2)

    everyone_wait(r.g5, 4)
    sums = jnp.sum(r.g5[...], axis=0)
    shift_grad, gain_grad = get(sums, 0, two), get(sums, two // LANES, two)
    r.second_gain_grad[...] = exact_nt(gain_grad, pick2)
    r.second_shift_grad[...] = exact_nt(shift_grad, pick2)
    lead2, base2, slant2 = gain2 * scale2, shift_grad * inverse, gain_grad * inverse

    def splits_back(i):
        def body(at, k, carry):
            there = pl.ds(pl.multiple_of((ch * ipd + i) * CELLS + k * STRIP, STRIP), STRIP)
            put_at = pl.ds(pl.multiple_of(SIDE + k * STRIP, SIDE), STRIP)
            mask = r.maskf[there, :]
            for q in range(two // LANES):
                g, p = q // (width // LANES), q % (width // LANES)
                lanes = slice(q * LANES, (q + 1) * LANES)
                d = mask * lead2[:, lanes] * (
                    r.act2[at, lanes] - base2[:, lanes] - r.sp[at, lanes] * slant2[:, lanes]
                )
                r.act2[at, lanes] = d
                before = jnp.where(not_first, pltpu.roll(d, 1, 0), 0.0)
                after = jnp.where(not_last, pltpu.roll(d, STRIP - 1, 0), 0.0)
                for n, value in enumerate((after, d, before)):
                    start = n * width + p * LANES
                    r.dsh[g, i, put_at, start : start + LANES] = value.astype(BF16)
            return carry

        strips(i * CELLS, body, 0)

    loop(ipd, splits_back)

    def first_back(i, state):
        out = []
        for g in range(2):
            lanes = slice(g * half, (g + 1) * half)
            left = jnp.concatenate(
                [r.dsh[g, i, (2 - k) * SIDE : (2 - k) * SIDE + CELLS, :] for k in range(3)], axis=1
            )
            value = dot(left, r.wt[g]) * r.slope1[image(i), lanes]
            r.dh1[rows_of(ch, i), lanes] = value.astype(BF16)
            out.append((state[g][0] + fold(value), state[g][1] + fold(value * r.red[image(i), lanes])))
        return tuple(out)

    zero_h = jnp.zeros((8, half), F32)
    state = lax.fori_loop(0, ipd, first_back, ((zero_h, zero_h), (zero_h, zero_h)))
    r.g6[0] = jnp.zeros((8, LANES), F32)
    for g in range(2):
        r.g6[0, g : g + 1, :] = total(state[g][0])
        r.g6[0, 2 + g : 3 + g, :] = total(state[g][1])
    everyone(r.g6, 5)
    gd = Gather(2, lambda b, i: r.dh1.at[rows_of(b, i)], lambda b: r.dh1.at[block_rows(b)], ipd)
    loop(ipd, gd.send)

    def pass_x(i):
        for t in range(1, X):
            gx.from_peer(t, i)

    loop(ipd, pass_x)

    def turn_d(i):
        for g in range(2):
            r.dst[g, :, image(i)] = r.act2[image(i), g * width : (g + 1) * width].T.astype(BF16)

    loop(ipd, turn_d)
    per = CH // 2
    for g in range(2):
        for k in range(3):
            lanes = slice(3 * k * half, 3 * (k + 1) * half)
            right = r.act[g, :, k * SIDE : k * SIDE + CELLS, :].reshape(own_rows, 3 * half)
            value = dot(r.dst[g], right)
            if c.split_inside:
                for q in range(per):
                    b = g * per + q
                    r.ss[b // 2, b % 2, :, lanes] = value[q * m2 : (q + 1) * m2, :].astype(BF16)
            else:
                r.split_part[g * width : (g + 1) * width, lanes] = value
    if c.split_inside:
        remote(r.ss.at[:, 1 - core], r.sin, r.sg_send.at[0], r.sg_recv.at[0], mate).start()

    everyone_wait(r.g6, 5)
    sums = jnp.sum(r.g6[...], axis=0)
    shift_grad, gain_grad = get(sums, 0, width), get(sums, 2, width)
    r.first_gain_grad[...] = exact_nt(gain_grad, pick1)
    r.first_shift_grad[...] = exact_nt(shift_grad, pick1)
    lead1, base1, slant1 = gain1 * scale1, shift_grad * inverse, gain_grad * inverse

    if c.split_inside:
        drain(r.sin, r.sg_recv.at[0])
        slab = m2 // DP

        def slab_rows(d):
            return pl.ds(pl.multiple_of(((dp + d) % DP) * slab, slab), slab)

        for t in range(X):
            r.sc[t] = (r.ss[t, core].astype(F32) + r.sin[t].astype(F32)).astype(BF16)
        for d in range(1, DP):
            for t in range(X):
                remote(
                    r.sc.at[t, slab_rows(d)], r.sp1.at[DP - d, t], r.sg_send.at[1], r.sg_recv.at[1], across(d)
                ).start()

    r.rg[...] = jnp.zeros((cw, width), F32)

    def from_x(i):
        gx.from_mate(i)
        for t in range(1, X):
            gx.from_pass(t, i)

    loop(ipd, from_x)
    gx.done()

    def reduced_back(b, i):
        def body(at, k, carry):
            mask = wide(r.maskf[at, :], width)
            d = mask * lead1 * (r.dh1[at, :].astype(F32) - base1 - r.xh1[at, :].astype(F32) * slant1)
            r.xh1[at, :] = d.astype(BF16)
            return carry

        strips((b * ipd + i) * CELLS, body, 0)
        r.rg[...] += dot(r.xt[b * ipd + i], r.xh1[rows_of(b, i), :])

    def input_back(b, i):
        at = rows_of(b, i)
        r.xv[at, :] = (r.dpre[at, :] + dot(r.xh1[at, :], r.wrt[...])).astype(BF16)
        pltpu.make_async_copy(r.xv.at[at], r.inputs_grad.at[at], r.store.at[1]).start()

    loop(ipd, lambda i: reduced_back(ch, i))

    def from_mate(i):
        gd.from_mate(i)
        reduced_back(block_of(0, False), i)

    loop(ipd, from_mate)
    loop(ipd, lambda i: input_back(ch, i))
    loop(ipd, lambda i: input_back(block_of(0, False), i))
    for t in range(1, X):

        def from_peer(i):
            gd.from_peer(t, i)
            reduced_back(block_of(t, True), i)

        loop(ipd, from_peer)
    for t in range(1, X):

        def from_pass(i):
            gd.from_pass(t, i)
            reduced_back(block_of(t, False), i)

        loop(ipd, from_pass)

    if c.reduce_inside:
        r.rs[...] = r.rg[...].T.astype(r.rs.dtype)
        for d in range(1, DP):
            remote(r.rs.at[piece_rows(d)], r.rbuf.at[DP - d], r.rg_send.at[0], r.rg_recv.at[0], across(d)).start()
    else:
        r.reduce_part[...] = r.rg[...].T
    if c.split_inside:
        drain(r.sp1.at[pl.ds(1, DP - 1)], r.sg_recv.at[1])
        for t in range(X):
            value = r.sc[(chip + t) % X, slab_rows(0), :].astype(F32)
            for d in range(1, DP):
                value = value + r.sp1[d, (chip + t) % X].astype(F32)
            r.sx[t] = value.astype(BF16)
            if t:
                remote(r.sx.at[t], r.sxin.at[X - t], r.sg_send.at[2], r.sg_recv.at[2], peer(t)).start()
    for t in range(1, X):
        loop(ipd, lambda i: input_back(block_of(t, True), i))
    if c.reduce_inside:
        groups = DP // CH
        goal = dp // groups
        drain(r.rbuf.at[pl.ds(1, DP - 1)], r.rg_recv.at[0])
        value = r.rs[piece_rows(0), :].astype(F32)
        for d in range(1, DP):
            value = value + r.rbuf[d].astype(F32)
        r.rsum[...] = value.astype(r.rsum.dtype)
        slot = r.rall.at[dp % groups, ch]
        for d in range(1, DP):
            remote(r.rsum, slot, r.rg_send.at[1], r.rg_recv.at[1], ((dp + d) % DP, goal)).start()

        @pl.when(goal == ch)
        def _():
            pltpu.make_async_copy(r.rsum, slot, r.rg_recv.at[1]).start()

        @pl.when(goal != ch)
        def _():
            remote(r.rsum, slot, r.rg_send.at[2], r.rg_recv.at[1], (dp, goal)).start()

    if c.split_inside:
        drain(r.sxin.at[pl.ds(1, X - 1)], r.sg_recv.at[2])
        value = r.sx[0].astype(F32)
        for t in range(1, X):
            value = value + r.sxin[t].astype(F32)
        r.so[0] = value.astype(BF16)
        for d in range(1, DP):
            remote(r.so.at[0], r.so.at[DP - d], r.sg_send.at[3], r.sg_recv.at[3], across(d)).start()
    for t in range(1, X):
        loop(ipd, lambda i: input_back(block_of(t, False), i))

    drain(r.eo.at[pl.ds(1, DP - 1)], r.eg_recv.at[1])
    for d in range(DP):
        r.expand_grad[piece_rows(d), :] = r.eo[d].astype(F32)
    if c.reduce_inside:
        drain(r.rall, r.rg_recv.at[1])
        r.tall[...] = jnp.zeros((LANES, CH * cw), F32)
        for s in range(groups):
            for q in range(CH):
                r.tall[s * piece : (s + 1) * piece, q * cw : (q + 1) * cw] = r.rall[s, q].astype(F32)
        for q in range(CH * cw // LANES):
            at = slice(q * LANES, (q + 1) * LANES)
            r.reduce_grad[at, :] = r.tall[:, at].T[:, 0:m1]
    if c.split_inside:
        drain(r.so.at[pl.ds(1, DP - 1)], r.sg_recv.at[3])
        for tap in range(9):
            at = slice(tap * half, (tap + 1) * half)
            block = jnp.concatenate([r.so[(d - dp + DP) % DP, :, at].astype(F32) for d in range(DP)], axis=0)
            r.split_grad[tap] = block.T

    for k, buf in enumerate((r.g1, r.g2, r.g3, r.g4, r.g5, r.g6)):
        everyone_done(buf, k)
    column_done(r.c1, 0)
    column_done(r.c2, 1)
    rs2.done()
    for gather in (gm, gd, gw):
        gather.done()
    drain(r.pbuf.at[pl.ds(1, CH - 1)], r.par_send.at[0])
    drain(r.ebuf.at[pl.ds(1, DP - 1)], r.eg_send.at[0])
    drain(r.ebuf.at[pl.ds(1, DP - 1)], r.eg_send.at[1])
    if c.reduce_inside:
        drain(r.rbuf.at[pl.ds(1, DP - 1)], r.rg_send.at[0])
        drain(r.rbuf.at[pl.ds(1, DP - 1)], r.rg_send.at[1])

        @pl.when(goal != ch)
        def _():
            drain(r.rsum, r.rg_send.at[2])

    if c.split_inside:
        drain(r.sin, r.sg_send.at[0])
        drain(r.sp1.at[pl.ds(1, DP - 1)], r.sg_send.at[1])
        drain(r.sxin.at[pl.ds(1, X - 1)], r.sg_send.at[2])
        drain(r.so.at[pl.ds(1, DP - 1)], r.sg_send.at[3])
    drain(r.cv, r.store.at[0])
    drain(r.xv, r.store.at[1])


ARGS = (
    "inputs", "resolution", "reduce_weight", "first_gain", "first_shift", "split_weight", "second_gain",
    "second_shift", "gate_down", "gate_gain", "gate_shift", "gate_up", "gate_bias", "expand_weight",
    "third_gain", "third_shift", "cotangent",
)


def per_device(*arrays):
    a = dict(zip(ARGS, arrays))
    c = types.SimpleNamespace()
    c.DP, c.CH = lax.axis_size("dp"), lax.axis_size("chan")
    c.X, c.D = c.CH // 2, c.DP * c.CH
    c.images = a["resolution"].shape[0]
    c.ipd = c.images // c.CH
    rows, c.cw = a["inputs"].shape
    c.width = a["reduce_weight"].shape[1]
    c.inner = a["gate_down"].shape[1]
    c.m1, c.m2, c.mg = c.width // c.CH, 2 * c.width // c.CH, c.inner // c.CH
    half, two = c.width // 2, 2 * c.width
    taps = 9 * half
    piece = c.width // c.DP
    piece_type = BF16 if piece % 16 == 0 else F32
    c.reduce_inside = c.DP % c.CH == 0 and piece % 8 == 0
    c.split_inside = c.m2 % (16 * c.DP) == 0
    own = c.ipd * CELLS
    DP, CH, X, D, ipd, cw, width = c.DP, c.CH, c.X, c.D, c.ipd, c.cw, c.width
    for name in ARGS:
        if a[name].ndim == 1 and name != "resolution":
            a[name] = a[name].reshape(1, -1)
    a["split_weight"] = a["split_weight"].reshape(taps, c.m2)
    sds = jax.ShapeDtypeStruct
    outs = dict(
        block_out=sds((rows, cw), BF16),
        inputs_grad=sds((rows, cw), BF16),
        first_gain_grad=sds((1, c.m1), F32),
        first_shift_grad=sds((1, c.m1), F32),
        second_gain_grad=sds((1, c.m2), F32),
        second_shift_grad=sds((1, c.m2), F32),
        down_grad=sds((width, c.mg), F32),
        gate_gain_grad=sds((1, c.mg), F32),
        gate_shift_grad=sds((1, c.mg), F32),
        up_grad=sds((c.inner, c.m2), F32),
        bias_grad=sds((1, c.m2), F32),
        expand_grad=sds((width, cw), F32),
        third_gain_grad=sds((1, cw), F32),
        third_shift_grad=sds((1, cw), F32),
    )
    if c.reduce_inside:
        outs["reduce_grad"] = sds((CH * cw, c.m1), F32)
    else:
        outs["reduce_part"] = sds((width, cw), F32)
    if c.split_inside:
        outs["split_grad"] = sds((9, half, c.m2), F32)
    else:
        outs["split_part"] = sds((two, taps), F32)
    V = pltpu.VMEM
    dma = lambda *shape: pltpu.SemaphoreType.DMA(shape)
    scratch = dict(
        xv=V((rows, cw), BF16), cv=V((rows, cw), BF16), wr=V((cw, width), BF16), wrt=V((width, cw), BF16),
        wet=V((cw, width), BF16), xt=V((c.images, cw, CELLS), BF16), mt=V((c.images, width, CELLS), BF16),
        maskf=V((rows, LANES), F32), area=V((c.images, LANES), F32), maskb=V((rows, LANES), BF16), pbuf=V((CH, 8, two), F32),
        red=V((own, width), F32), slope1=V((own, width), F32), xh1=V((rows, width), BF16),
        act=V((2, ipd, TALL, 3 * half), BF16), dsh=V((2, ipd, TALL, 3 * width), BF16),
        wg=V((CH, taps, c.m2), BF16), wf=V((2, taps, width), BF16), wt=V((2, 9 * width, half), BF16),
        sp=V((own, two), F32), slope2=V((own, two), F32), act2=V((own, two), F32), share=V((8, LANES), F32),
        gate_x=V((D * 8, LANES), F32), squeezed=V((D * 8, LANES), F32), gate_slope=V((D * 8, LANES), F32),
        grad_down=V((D * 8, LANES), F32), grad_summary=V((8, width), F32), att=V((8, two), F32),
        merged=V((rows, width), BF16), ex=V((rows, cw), F32), acc=V((16, cw), F32),
        dpre=V((rows, cw), F32), de=V((rows, cw), BF16), dm=V((own, width), F32), dh1=V((rows, width), BF16),

        dst=V((2, width, own), BF16),
        eg=V((width, cw), F32), es=V((width, cw), piece_type), ebuf=V((DP, piece, cw), piece_type),
        eo=V((DP, piece, cw), piece_type), rg=V((cw, width), F32),
        all_send=dma(6), all_recv=dma(6), col_send=dma(2), col_recv=dma(2),
        rs_core_send=dma(2), rs_core_recv=dma(2, X, ipd), rs_chip_send=dma(2), rs_chip_recv=dma(2, X, ipd),
        ag_core_send=dma(4), ag_core_recv=dma(4, ipd), ag_chip_send=dma(4, X), ag_chip_recv=dma(4, X, ipd),
        ag_pass_send=dma(4, X), ag_pass_recv=dma(4, X, ipd), par_send=dma(1), par_recv=dma(CH),
        eg_send=dma(2), eg_recv=dma(2), rg_send=dma(3), rg_recv=dma(2), sg_send=dma(4), sg_recv=dma(4),
        load=dma(2 + 2 * X), store=dma(2),
    )
    for name, count in (
        ("stage", X), ("inward", X), ("outward", X - 1), ("landed", X - 1), ("inward2", X), ("landed2", X - 1)
    ):
        scratch[name] = V((count, ipd, CELLS, width), BF16)
    for k in range(1, 7):
        scratch[f"g{k}"] = V((D, 8, LANES), F32)
    for k in range(1, 3):
        scratch[f"c{k}"] = V((DP, 8, LANES), F32)
    if c.reduce_inside:
        scratch.update(
            rs=V((width, cw), piece_type), rbuf=V((DP, piece, cw), piece_type), rsum=V((piece, cw), piece_type),
            rall=V((DP // CH, CH, piece, cw), piece_type), tall=V((LANES, CH * cw), F32),
        )
    if c.split_inside:
        slab = c.m2 // DP
        scratch.update(
            ss=V((X, 2, c.m2, taps), BF16), sin=V((X, c.m2, taps), BF16), sc=V((X, c.m2, taps), BF16),
            sp1=V((DP, X, slab, taps), BF16), sx=V((X, slab, taps), BF16), sxin=V((X, slab, taps), BF16),
            so=V((DP, slab, taps), BF16),
        )
    anywhere = pl.BlockSpec(memory_space=pl.ANY)
    vmem = pl.BlockSpec(memory_space=pltpu.VMEM)
    spec = dict(
        inputs=anywhere, cotangent=anywhere, reduce_weight=anywhere, block_out=anywhere, inputs_grad=anywhere,
        resolution=pl.BlockSpec(memory_space=pltpu.SMEM),
    )
    names = tuple(ARGS) + tuple(outs) + tuple(scratch)
    results = pl.pallas_call(
        functools.partial(kernel, c, names),
        out_shape=tuple(outs.values()),
        in_specs=[spec.get(name, vmem) for name in ARGS],
        out_specs=tuple(spec.get(name, vmem) for name in outs),
        scratch_shapes=list(scratch.values()),
        compiler_params=pltpu.CompilerParams(
            collective_id=0, has_side_effects=True, vmem_limit_bytes=62 * 2**20
        ),
        name="block",
    )(*[a[name] for name in ARGS])
    o = dict(zip(outs, results))
    if not c.reduce_inside:
        place = lax.axis_index("chan")
        part = lax.psum(o["reduce_part"], "dp")
        part = lax.all_gather(part, "chan", axis=1, tiled=True)
        o["reduce_grad"] = lax.dynamic_slice_in_dim(part, place * c.m1, c.m1, 0).T
    if not c.split_inside:
        place = lax.axis_index("chan")
        part = lax.psum(o["split_part"], ("dp", "chan"))
        part = lax.dynamic_slice_in_dim(part, place * c.m2, c.m2, 0)
        o["split_grad"] = part.T.reshape(9, half, c.m2)
    flat = lambda name: o[name].reshape(-1)
    return (
        o["block_out"], o["inputs_grad"], o["reduce_grad"], flat("first_gain_grad"), flat("first_shift_grad"),
        o["split_grad"], flat("second_gain_grad"), flat("second_shift_grad"), o["down_grad"],
        flat("gate_gain_grad"), flat("gate_shift_grad"), o["up_grad"], flat("bias_grad"), o["expand_grad"],
        flat("third_gain_grad"), flat("third_shift_grad"),
    )


def solution(mesh):
    placed = (
        P("dp", "chan"), P("dp"), P(), P("chan"), P("chan"), P(None, None, "chan"), P("chan"), P("chan"),
        P(), P(), P(), P(), P(), P(None, "chan"), P("chan"), P("chan"), P("dp", "chan"),
    )
    return jax.shard_map(
        per_device,
        mesh=mesh,
        in_specs=placed,
        out_specs=(
            P("dp", "chan"), P("dp", "chan"), P(None, "chan"), P("chan"), P("chan"), P(None, None, "chan"),
            P("chan"), P("chan"), P(None, "chan"), P("chan"), P("chan"), P(None, "chan"), P("chan"),
            P(None, "chan"), P("chan"), P("chan"),
        ),
        check_vma=False,
    )
```

```python
import functools
import types

import jax
import jax.numpy as jnp
from jax import lax
from jax.experimental import pallas as pl
from jax.experimental.pallas import tpu as pltpu
from jax.sharding import PartitionSpec as P

SIDE = 16
CELLS = SIDE * SIDE
TALL = CELLS + 2 * SIDE
LANES = 128
EPS = 1e-05
HIGHEST = lax.Precision.HIGHEST
F32 = jnp.float32
BF16 = jnp.bfloat16
MESH = pl.DeviceIdType.MESH
STRIP = 32


def wide(mask, width):
    return mask if width == LANES else jnp.concatenate([mask] * (width // LANES), axis=1)


def fold(values):
    return jnp.sum(values.reshape(values.shape[0] // 8, 8, values.shape[1]), axis=0)


def total(values):
    return jnp.sum(values, axis=0, keepdims=True)


def sigmoid(values):
    return 0.5 * jnp.tanh(0.5 * values) + 0.5


def dot(left, right):
    return jnp.dot(left, right, preferred_element_type=F32)


def exact(left, right):
    return jnp.dot(left, right, precision=HIGHEST, preferred_element_type=F32)


def exact_nt(left, right):
    return lax.dot_general(
        left, right, (((1,), (1,)), ((), ())), precision=HIGHEST, preferred_element_type=F32
    )


def exact_tn(left, right):
    return lax.dot_general(
        left, right, (((0,), (0,)), ((), ())), precision=HIGHEST, preferred_element_type=F32
    )


def flip(values):
    return values.astype(F32).T.astype(values.dtype)


def put(ref, row, vector):
    for part in range(vector.shape[1] // LANES):
        ref[0, row + part : row + part + 1, :] = vector[:, part * LANES : (part + 1) * LANES]


def get(block, row, width):
    parts = [block[row + q : row + q + 1, :] for q in range(width // LANES)]
    return parts[0] if len(parts) == 1 else jnp.concatenate(parts, axis=1)


def kernel(c, names, *refs):
    r = types.SimpleNamespace(**dict(zip(names, refs)))
    DP, CH, X, D, ipd, images = c.DP, c.CH, c.X, c.D, c.ipd, c.images
    width, cw, inner, m1, m2, mg = c.width, c.cw, c.inner, c.m1, c.m2, c.mg
    half, two = width // 2, 2 * width
    own_rows = ipd * CELLS
    taps = 9 * half
    dp = lax.axis_index("dp")
    ch = lax.axis_index("chan")
    core = ch % 2
    chip = ch // 2
    mate = (dp, ch + 1 - 2 * core)
    f0 = ((0, 0), (0, 0))

    def remote(src, dst, send, recv, device):
        return pltpu.make_async_remote_copy(
            src_ref=src, dst_ref=dst, send_sem=send, recv_sem=recv, device_id=device, device_id_type=MESH
        )

    def drain(ref, sem):
        pltpu.make_async_copy(ref, ref, sem).wait()

    def loop(count, body):
        def step(i, carry):
            body(i)
            return carry

        lax.fori_loop(0, count, step, 0)

    def peer(t):
        return (dp, ((chip + t) % X) * 2 + core)

    def across(d):
        return ((dp + d) % DP, ch)

    def block_of(t, same):
        return ((chip + t) % X) * 2 + (core if same else 1 - core)

    def rows_of(b, i):
        return pl.ds(pl.multiple_of((b * ipd + i) * CELLS, CELLS), CELLS)

    def block_rows(b):
        return pl.ds(pl.multiple_of(b * own_rows, own_rows), own_rows)

    def image(i):
        return pl.ds(pl.multiple_of(i * CELLS, CELLS), CELLS)

    def strips(base, body, carry, size=STRIP):
        def step(k, state):
            return body(pl.ds(pl.multiple_of(base + k * size, size), size), k, state)

        return lax.fori_loop(0, CELLS // size, step, carry)

    def everyone(buf, k, message=None):
        message = buf.at[0] if message is None else message

        def one(j, carry):
            d, q = j // CH, j % CH
            slot = ((DP - d) % DP) * CH + (CH - q) % CH
            remote(buf.at[0], buf.at[slot], r.all_send.at[k], r.all_recv.at[k], ((dp + d) % DP, (ch + q) % CH)).start()
            return carry

        lax.fori_loop(1, D, one, 0)

    def everyone_wait(buf, k):
        drain(buf.at[pl.ds(1, D - 1)], r.all_recv.at[k])

    def everyone_done(buf, k):
        drain(buf.at[pl.ds(1, D - 1)], r.all_send.at[k])

    def column(buf, k):
        for d in range(1, DP):
            remote(buf.at[0], buf.at[DP - d], r.col_send.at[k], r.col_recv.at[k], across(d)).start()

    def row(buf, k, source=None):
        for q in range(1, CH):
            src = buf.at[0] if source is None else source.at[(ch + q) % CH]
            remote(src, buf.at[CH - q], r.row_send.at[k], r.row_recv.at[k], (dp, (ch + q) % CH)).start()

    def row_sum(buf, k, column_buf):
        drain(buf.at[pl.ds(1, CH - 1)], r.row_recv.at[k])
        column_buf[0] = jnp.sum(buf[...], axis=0)

    def row_done(buf, k):
        drain(buf.at[pl.ds(1, CH - 1)], r.row_send.at[k])

    def column_wait(buf, k):
        drain(buf.at[pl.ds(1, DP - 1)], r.col_recv.at[k])

    def column_done(buf, k):
        drain(buf.at[pl.ds(1, DP - 1)], r.col_send.at[k])

    class Scatter:
        def __init__(self, k, stage, inward, outward, landed, keep):
            self.k, self.stage, self.inward = k, stage, inward
            self.outward, self.landed, self.keep = outward, landed, keep

        def compute_mate(self, t, part):
            def body(i):
                self.stage[t, i] = part(block_of(t, False), i).astype(BF16)

            loop(ipd, body)

        def send_mate(self, t):
            def body(i):
                remote(
                    self.stage.at[t, i], self.inward.at[t, i],
                    r.rs_core_send.at[self.k], r.rs_core_recv.at[self.k, t, i], mate,
                ).start()

            loop(ipd, body)

        def to_mate(self, t, part):
            def body(i):
                self.stage[t, i] = part(block_of(t, False), i).astype(BF16)
                remote(
                    self.stage.at[t, i], self.inward.at[t, i],
                    r.rs_core_send.at[self.k], r.rs_core_recv.at[self.k, t, i], mate,
                ).start()

            loop(ipd, body)

        def to_peer(self, t, part):
            def body(i):
                value = part(block_of(t, True), i)
                drain(self.inward.at[t, i], r.rs_core_recv.at[self.k, t, i])
                self.outward[t - 1, i] = (value + self.inward[t, i].astype(F32)).astype(BF16)
                remote(
                    self.outward.at[t - 1, i], self.landed.at[X - t - 1, i],
                    r.rs_chip_send.at[self.k], r.rs_chip_recv.at[self.k, X - t, i], peer(t),
                ).start()

            loop(ipd, body)

        def own(self, part):
            def body(i):
                value = part(ch, i)
                drain(self.inward.at[0, i], r.rs_core_recv.at[self.k, 0, i])
                self.keep[image(i), :] = value + self.inward[0, i].astype(F32)

            loop(ipd, body)

        def arrive(self, i):
            for t in range(1, X):
                drain(self.landed.at[t - 1, i], r.rs_chip_recv.at[self.k, t, i])

        def extra(self, i, at, lanes):
            value = self.landed[0, i, at, lanes].astype(F32)
            for t in range(2, X):
                value = value + self.landed[t - 1, i, at, lanes].astype(F32)
            return value

        def done(self):
            drain(self.stage, r.rs_core_send.at[self.k])
            drain(self.outward, r.rs_chip_send.at[self.k])

    class Gather:
        def __init__(self, k, place, whole, pieces):
            self.k, self.place, self.whole, self.pieces = k, place, whole, pieces

        def send(self, i):
            src = self.place(ch, i)
            remote(src, src, r.ag_core_send.at[self.k], r.ag_core_recv.at[self.k, i], mate).start()
            for t in range(1, X):
                remote(src, src, r.ag_chip_send.at[self.k, t], r.ag_chip_recv.at[self.k, X - t, i], peer(t)).start()

        def from_mate(self, i):
            drain(self.place(block_of(0, False), i), r.ag_core_recv.at[self.k, i])

        def from_peer(self, t, i):
            ref = self.place(block_of(t, True), i)
            drain(ref, r.ag_chip_recv.at[self.k, t, i])
            remote(ref, ref, r.ag_pass_send.at[self.k, t], r.ag_pass_recv.at[self.k, t, i], mate).start()

        def from_pass(self, t, i):
            drain(self.place(block_of(t, False), i), r.ag_pass_recv.at[self.k, t, i])

        def done(self):
            drain(self.whole(ch), r.ag_core_send.at[self.k])
            for t in range(1, X):
                drain(self.whole(ch), r.ag_chip_send.at[self.k, t])
                drain(self.whole(block_of(t, True)), r.ag_pass_send.at[self.k, t])

    class Share:
        def __init__(self, k, blocks, rows):
            self.k, self.blocks, self.piece = k, blocks, rows // DP

        def part(self, b, d):
            at = pl.ds(pl.multiple_of(((dp + d) % DP) * self.piece, self.piece), self.piece)
            return self.blocks.at[b, at]

        def send(self):
            own = self.blocks.at[ch]
            remote(own, own, r.sh_core_send.at[self.k], r.sh_core_recv.at[self.k], mate).start()
            for t in range(1, X):
                src = self.part(ch, 0) if c.share else own
                remote(src, src, r.sh_chip_send.at[self.k, t], r.sh_chip_recv.at[self.k, X - t], peer(t)).start()

        def spread(self):
            for t in range(1, X):
                b = block_of(t, True)
                src = self.part(b, 0) if c.share else self.blocks.at[b]
                drain(src, r.sh_chip_recv.at[self.k, t])
                if c.share:
                    for d in range(1, DP):
                        remote(src, src, r.sh_col_send.at[self.k, t], r.sh_col_recv.at[self.k, t, DP - d], across(d)).start()

        def hand(self):
            for t in range(1, X):
                b = block_of(t, True)
                if c.share:
                    for d in range(1, DP):
                        drain(self.part(b, d), r.sh_col_recv.at[self.k, t, d])
                whole = self.blocks.at[b]
                remote(whole, whole, r.sh_pass_send.at[self.k, t], r.sh_pass_recv.at[self.k, t], mate).start()

        def take(self):
            drain(self.blocks.at[block_of(0, False)], r.sh_core_recv.at[self.k])
            for t in range(1, X):
                drain(self.blocks.at[block_of(t, False)], r.sh_pass_recv.at[self.k, t])

        def done(self):
            own = self.blocks.at[ch]
            drain(own, r.sh_core_send.at[self.k])
            for t in range(1, X):
                whole = self.blocks.at[block_of(t, True)]
                drain(self.part(ch, 0) if c.share else own, r.sh_chip_send.at[self.k, t])
                drain(whole, r.sh_pass_send.at[self.k, t])
                if c.share:
                    for d in range(1, DP):
                        drain(self.part(block_of(t, True), 0), r.sh_col_send.at[self.k, t])

    barrier = pltpu.get_barrier_semaphore()

    def greet(j, carry):
        pl.semaphore_signal(
            barrier, inc=1, device_id=((dp + j // CH) % DP, (ch + j % CH) % CH), device_id_type=MESH
        )
        return carry

    lax.fori_loop(1, D, greet, 0)

    load_w = pltpu.make_async_copy(
        r.reduce_weight.at[pl.ds(pl.multiple_of(ch * cw, cw), cw)], r.wr, r.load.at[0]
    )
    load_w.start()
    order = []
    for t in list(range(1, X)) + [0]:
        order += [block_of(t, False), block_of(t, True)]
    loads = []
    for k, b in enumerate(order):
        at = pl.ds(pl.multiple_of(b * own_rows, own_rows), own_rows)
        loads.append(pltpu.make_async_copy(r.inputs.at[at], r.xv.at[at], r.load.at[2 + k]))
        loads[-1].start()
    load_c = pltpu.make_async_copy(r.cotangent, r.cv, r.load.at[1])
    load_c.start()

    row_at = lax.broadcasted_iota(jnp.int32, (CELLS, LANES), 0)
    spot_r = lax.shift_right_logical(row_at, 4)
    spot_c = lax.bitwise_and(row_at, 15)

    def make_mask(j):
        side = 12 + 2 * r.resolution[j]
        mask = jnp.where(jnp.logical_and(spot_r < side, spot_c < side), 1.0, 0.0)
        r.area[pl.ds(j, 1), :] = jnp.full((1, LANES), side * side, jnp.int32).astype(F32)
        r.maskf[image(j), :] = mask
        r.maskb[image(j), :] = mask.astype(BF16)

    loop(images, make_mask)

    def part_reduce(b, i):
        at = rows_of(b, i)
        x = r.xv[at, :] * wide(r.maskb[at, :], cw)
        r.xv[at, :] = x
        return dot(x, r.wr[...])

    r.wg[ch] = r.split_weight[...]
    r.wx[ch] = r.expand_weight[...]
    shares = (Share(0, r.wg, taps), Share(1, r.wx, width))

    load_w.wait()
    rs1 = Scatter(0, r.stage, r.inward, r.outward, r.landed, r.red)
    loads[0].wait()
    rs1.compute_mate(1, part_reduce)
    pl.semaphore_wait(barrier, D - 1)
    rs1.send_mate(1)
    for share in shares:
        share.send()
    for t in range(1, X):
        if t > 1:
            loads[2 * t - 2].wait()
            rs1.to_mate(t, part_reduce)
        loads[2 * t - 1].wait()
        rs1.to_peer(t, part_reduce)
    for share in shares:
        share.spread()
    loads[2 * X - 2].wait()
    rs1.to_mate(0, part_reduce)
    loads[2 * X - 1].wait()
    rs1.own(part_reduce)

    def selector(parts, mine):
        row = lax.broadcasted_iota(jnp.int32, (mine, mine * parts), 0)
        col = lax.broadcasted_iota(jnp.int32, (mine, mine * parts), 1)
        return jnp.where(col == row + ch * mine, 1.0, 0.0)

    pick1 = selector(CH, m1)
    pick2 = selector(CH, m2)
    pickg = selector(CH, mg)
    r.pbuf[0, 0:1, 0:width] = exact(r.first_gain[...], pick1)
    r.pbuf[0, 1:2, 0:width] = exact(r.first_shift[...], pick1)
    r.pbuf[0, 2:3, :] = exact(r.second_gain[...], pick2)
    r.pbuf[0, 3:4, :] = exact(r.second_shift[...], pick2)

    for q in range(1, CH):
        remote(r.pbuf.at[0], r.pbuf.at[CH - q], r.par_send.at[0], r.par_recv.at[CH - q], (dp, (ch + q) % CH)).start()

    r.wrt[...] = flip(r.wr[...])
    r.wet[...] = flip(r.expand_weight[...])

    def turn_x(j):
        r.xt[j] = flip(r.xv[image(j), :])

    loop(images, turn_x)
    for g in range(2):
        for i in range(ipd):
            r.act[g, i, 0:SIDE, :] = jnp.zeros((SIDE, 3 * half), BF16)
            r.act[g, i, CELLS + SIDE : TALL, :] = jnp.zeros((SIDE, 3 * half), BF16)
            r.dsh[g, i, 0:SIDE, :] = jnp.zeros((SIDE, 3 * width), BF16)
            r.dsh[g, i, CELLS + SIDE : TALL, :] = jnp.zeros((SIDE, 3 * width), BF16)

    def finish_reduce(i, state):
        rs1.arrive(i)

        def body(at, k, state):
            first, second = state
            value = r.red[at, :] + rs1.extra(i, pl.ds(pl.multiple_of(k * STRIP, STRIP), STRIP), slice(None))
            r.red[at, :] = value
            return (first + fold(value), second + fold(value * value))

        return strips(i * CELLS, body, state)

    zero8 = jnp.zeros((8, width), F32)
    first, second = lax.fori_loop(0, ipd, finish_reduce, (zero8, zero8))

    pixels = lax.fori_loop(
        0, ipd, lambda i, count: count + r.area[pl.ds(ch * ipd + i, 1), :], jnp.zeros((1, LANES), F32)
    )
    r.g1[0] = jnp.zeros((8, LANES), F32)
    put(r.g1, 0, total(first))
    put(r.g1, width // LANES, total(second))
    r.g1[0, 6:7, :] = pixels
    everyone(r.g1, 0)
    for share in shares:
        share.hand()
    everyone_wait(r.g1, 0)
    sums = jnp.sum(r.g1[...], axis=0)
    count = sums[6:7, 0:1]
    inverse = 1.0 / count
    params = r.pbuf[0]
    for q in range(1, CH):
        drain(r.pbuf.at[q], r.par_recv.at[q])
        params = params + r.pbuf[q]
    gain1, shift1 = params[0:1, 0:width], params[1:2, 0:width]
    gain2, shift2 = params[2:3, :], params[3:4, :]

    def moments(first, second):
        mean = first * inverse
        return mean, lax.rsqrt(second * inverse - mean * mean + EPS)

    mean1, scale1 = moments(get(sums, 0, width), get(sums, width // LANES, width))

    place_x = lambda b, i: r.xh1.at[rows_of(b, i)]
    gx = Gather(0, place_x, lambda b: r.xh1.at[block_rows(b)], ipd)

    strip_c = lax.bitwise_and(lax.broadcasted_iota(jnp.int32, (STRIP, LANES), 0), 15)
    not_first = strip_c != 0
    not_last = strip_c != 15

    def first_act(i):
        def body(at, k, carry):
            there = pl.ds(pl.multiple_of((ch * ipd + i) * CELLS + k * STRIP, STRIP), STRIP)
            put_at = pl.ds(pl.multiple_of(SIDE + k * STRIP, SIDE), STRIP)
            mask = r.maskf[there, :]
            for g in range(2):
                lanes = slice(g * half, (g + 1) * half)
                xh = (r.red[at, lanes] - mean1[:, lanes]) * scale1[:, lanes]
                h = gain1[:, lanes] * xh + shift1[:, lanes]
                s = sigmoid(h)
                y = h * s
                r.red[at, lanes] = xh
                r.xh1[there, lanes] = xh.astype(BF16)
                r.slope1[at, lanes] = mask * (s + y - y * s)
                a = mask * y
                before = jnp.where(not_first, pltpu.roll(a, 1, 0), 0.0)
                after = jnp.where(not_last, pltpu.roll(a, STRIP - 1, 0), 0.0)
                r.act[g, i, put_at, 0:half] = before.astype(BF16)
                r.act[g, i, put_at, half : 2 * half] = a.astype(BF16)
                r.act[g, i, put_at, 2 * half : 3 * half] = after.astype(BF16)
            return carry

        strips(i * CELLS, body, 0)

    loop(ipd, first_act)

    for share in shares:
        share.take()
    for g in range(2):
        for q in range(CH // 2):
            r.wf[g, :, q * m2 : (q + 1) * m2] = r.wg[g * (CH // 2) + q]

    def conv(i, state):
        there = rows_of(ch, i)
        out = []
        for g in range(2):
            lanes = slice(g * width, (g + 1) * width)
            left = jnp.concatenate(
                [r.act[g, i, k * SIDE : k * SIDE + CELLS, :] for k in range(3)], axis=1
            )
            value = dot(left, r.wf[g]) * wide(r.maskf[there, :], width)
            r.sp[image(i), lanes] = value
            out.append((state[g][0] + fold(value), state[g][1] + fold(value * value)))
        return tuple(out)

    state = lax.fori_loop(0, ipd, conv, ((zero8, zero8), (zero8, zero8)))
    for g in range(2):
        put(r.g2, g * (width // LANES), total(state[g][0]))
        put(r.g2, (2 + g) * (width // LANES), total(state[g][1]))
    everyone(r.g2, 1)

    for g in range(2):
        for tap in range(9):
            r.wt[g, tap * width : (tap + 1) * width, :] = flip(r.wf[g, tap * half : (tap + 1) * half, :])

    everyone_wait(r.g2, 1)
    sums = jnp.sum(r.g2[...], axis=0)
    mean2, scale2 = moments(get(sums, 0, two), get(sums, two // LANES, two))

    r.g3[0] = jnp.zeros((8, LANES), F32)

    def second_act(i):
        def body(at, k, state):
            there = pl.ds(pl.multiple_of((ch * ipd + i) * CELLS + k * STRIP, STRIP), STRIP)
            mask = r.maskf[there, :]
            new = []
            for q in range(two // LANES):
                lanes = slice(q * LANES, (q + 1) * LANES)
                xh = (r.sp[at, lanes] - mean2[:, lanes]) * scale2[:, lanes]
                h = gain2[:, lanes] * xh + shift2[:, lanes]
                s = sigmoid(h)
                y = h * s
                r.sp[at, lanes] = xh
                r.slope2[at, lanes] = mask * (s + y - y * s)
                a = mask * y
                r.act2[at, lanes] = a
                new.append(state[q] + fold(a))
            return tuple(new)

        zero = jnp.zeros((8, LANES), F32)
        pooled = strips(i * CELLS, body, (zero,) * (two // LANES))
        share = 1.0 / r.area[pl.ds(ch * ipd + i, 1), :]
        r.share[pl.ds(i, 1), :] = share
        n = width // LANES
        for q in range(n):
            r.g3[0, pl.ds(4 * q + i, 1), :] = total(pooled[q] + pooled[n + q]) * share

    loop(ipd, second_act)
    everyone(r.g3, 2)

    gate_rows = min(D * 8, 2 * LANES)
    gate_blocks = D * 8 // gate_rows
    gate_at = lax.broadcasted_iota(jnp.int32, (gate_rows, LANES), 0)
    valid = lax.bitwise_and(gate_at, 7) < ipd
    every = 1.0 / (D * ipd)

    def gate_block(n):
        return pl.ds(pl.multiple_of(n * gate_rows, gate_rows), gate_rows)

    def lower_upper(buf, n):
        slots = gate_rows // 8
        both = buf[pl.ds(n * slots, slots)].reshape(gate_rows, LANES)
        return jnp.where(valid, both, 0.0), jnp.where(valid, pltpu.roll(both, gate_rows - 4, 0), 0.0)

    def gate_in(n, state):
        sum_lo, sum_hi = lower_upper(r.g3, n)
        pre = exact(sum_lo, r.gate_down[0:LANES, :]) + exact(sum_hi, r.gate_down[LANES:, :])
        r.gate_x[gate_block(n), :] = pre
        return state[0] + total(pre), state[1] + total(pre * pre)

    everyone_wait(r.g3, 2)
    zero1 = jnp.zeros((1, LANES), F32)
    first, second = lax.fori_loop(0, gate_blocks, gate_in, (zero1, zero1))
    gate_mean = first * every
    gate_scale = lax.rsqrt(second * every - gate_mean * gate_mean + EPS)

    def gate_out(n):
        at = gate_block(n)
        x = (r.gate_x[at, :] - gate_mean) * gate_scale
        h = r.gate_gain[...] * x + r.gate_shift[...]
        s = sigmoid(h)
        y = h * s
        r.gate_x[at, :] = x
        r.squeezed[at, :] = y
        r.gate_slope[at, :] = s + y - y * s

    loop(gate_blocks, gate_out)
    logits = exact(r.squeezed[0:8, :], r.gate_up[...]) + r.gate_bias[...]
    top = jnp.maximum(logits[:, :width], logits[:, width:])
    upper = jnp.exp(logits[:, :width] - top)
    lower = jnp.exp(logits[:, width:] - top)
    both = upper + lower
    r.att[:, 0:width] = upper / both
    r.att[:, width:two] = lower / both

    gm = Gather(1, lambda b, i: r.merged.at[rows_of(b, i)], lambda b: r.merged.at[block_rows(b)], ipd)

    def merge(i):
        att = r.att[pl.ds(i, 1), :]

        def body(at, k, carry):
            there = pl.ds(pl.multiple_of((ch * ipd + i) * CELLS + k * STRIP, STRIP), STRIP)
            left = (r.act2[at, 0:width] * att[:, 0:width]).astype(BF16)
            right = (r.act2[at, width:two] * att[:, width:two]).astype(BF16)
            r.merged[there, :] = (left.astype(F32) + right.astype(F32)).astype(BF16)
            return carry

        strips(i * CELLS, body, 0)

    merge(0)
    gm.send(0)
    lax.fori_loop(1, ipd, lambda i, carry: (merge(i), carry)[1], 0)

    def expand_sums(k):
        def body(i, state):
            value = dot(r.merged[rows_of(ch, i), :], r.wx[k])
            return (state[0] + fold(value), state[1] + fold(value * value))

        first, second = lax.fori_loop(0, ipd, body, (zero_c, zero_c))
        put(r.sums3.at[pl.ds(k, 1)], 0, total(first))
        put(r.sums3.at[pl.ds(k, 1)], cw // LANES, total(second))

    zero_c = jnp.zeros((8, cw), F32)
    loop(CH, expand_sums)
    r.r1[0] = r.sums3[ch]
    row(r.r1, 0, r.sums3)
    lax.fori_loop(1, ipd, lambda i, carry: (gm.send(i), carry)[1], 0)
    load_c.wait()
    r.acc[...] = jnp.zeros((16, cw), F32)
    row_sum(r.r1, 0, r.c1)
    column(r.c1, 0)

    def turn_own(j):
        r.mt[ch * ipd + j] = flip(r.merged[rows_of(ch, j), :])

    loop(ipd, turn_own)
    column_wait(r.c1, 0)
    sums = jnp.sum(r.c1[...], axis=0)
    mean3, scale3 = moments(get(sums, 0, cw), get(sums, cw // LANES, cw))
    gain3, shift3 = r.third_gain[...], r.third_shift[...]

    def outputs(b, i):
        r.ex[rows_of(b, i), :] = dot(r.merged[rows_of(b, i), :], r.expand_weight[...])

        def body(at, k, state):
            shift, cross = state
            mask = wide(r.maskf[at, :], cw)
            xh = (r.ex[at, :] - mean3) * scale3
            h = gain3 * xh + shift3 + r.xv[at, :].astype(F32)
            s = sigmoid(h)
            y = h * s
            d = r.cv[at, :].astype(F32) * mask * (s + y - y * s)
            r.cv[at, :] = (mask * y).astype(BF16)
            r.dpre[at, :] = d
            r.ex[at, :] = xh
            return (shift + fold(d), cross + fold(d * xh))

        shift, cross = strips((b * ipd + i) * CELLS, body, (zero_c, zero_c))
        r.acc[0:8, :] += shift
        r.acc[8:16, :] += cross
        at = rows_of(b, i)
        pltpu.make_async_copy(r.cv.at[at], r.block_out.at[at], r.store.at[0]).start()

    loop(ipd, lambda i: outputs(ch, i))

    def outputs_mate(i):
        gm.from_mate(i)
        outputs(block_of(0, False), i)

    loop(ipd, outputs_mate)
    for t in range(1, X):

        def outputs_peer(i):
            gm.from_peer(t, i)
            outputs(block_of(t, True), i)

        loop(ipd, outputs_peer)
    lax.fori_loop(1, ipd, lambda i, carry: (gx.send(i), carry)[1], 0)
    for t in range(1, X):

        def outputs_pass(i):
            gm.from_pass(t, i)
            outputs(block_of(t, False), i)

        loop(ipd, outputs_pass)
    put(r.c2, 0, total(r.acc[0:8, :]))
    put(r.c2, cw // LANES, total(r.acc[8:16, :]))
    column(r.c2, 1)

    def turn_other(j):
        b = j // ipd
        b = jnp.where(b < ch, b, b + 1)
        at = b * ipd + j % ipd
        r.mt[at] = flip(r.merged[image(at), :])

    loop(images - ipd, turn_other)
    column_wait(r.c2, 1)
    sums = jnp.sum(r.c2[...], axis=0)
    shift_grad, gain_grad = get(sums, 0, cw), get(sums, cw // LANES, cw)
    r.third_gain_grad[...] = gain_grad
    r.third_shift_grad[...] = shift_grad
    lead3, base3, slant3 = gain3 * scale3, shift_grad * inverse, gain_grad * inverse

    def part_merged(b, i):
        def body(at, k, carry):
            mask = wide(r.maskf[at, :], cw)
            d = mask * lead3 * (r.dpre[at, :] - base3 - r.ex[at, :] * slant3)
            r.de[at, :] = d.astype(BF16)
            return carry

        strips((b * ipd + i) * CELLS, body, 0)
        return dot(r.de[rows_of(b, i), :], r.wet[...])

    rs1.done()
    rs2 = Scatter(1, r.stage, r.inward2, r.outward, r.landed2, r.dm)
    for t in range(1, X):
        rs2.to_mate(t, part_merged)
        rs2.to_peer(t, part_merged)
    rs2.to_mate(0, part_merged)
    rs2.own(part_merged)
    gx.send(0)

    def grow(j):
        r.eg[...] += dot(r.mt[j], r.de[image(j), :])

    r.eg[...] = dot(r.mt[0], r.de[image(0), :])
    lax.fori_loop(1, images, lambda j, carry: (grow(j), carry)[1], 0)
    piece = width // DP
    et = r.es.dtype
    r.es[...] = r.eg[...].astype(et)

    def piece_rows(d):
        return pl.ds(pl.multiple_of(((dp + d) % DP) * piece, piece), piece)

    for d in range(1, DP):
        remote(r.es.at[piece_rows(d)], r.ebuf.at[DP - d], r.eg_send.at[0], r.eg_recv.at[0], across(d)).start()

    r.g4[0] = jnp.zeros((8, LANES), F32)

    def finish_merged(i):
        rs2.arrive(i)

        def body(at, k, state):
            here = pl.ds(pl.multiple_of(k * STRIP, STRIP), STRIP)
            value = r.dm[at, :] + rs2.extra(i, here, slice(None))
            r.dm[at, :] = value
            return state + fold(value * (r.act2[at, 0:width] - r.act2[at, width:two]))

        gap = total(strips(i * CELLS, body, zero8))
        att = r.att[pl.ds(i, 1), :]
        grad = att[:, 0:width] * att[:, width:two] * gap
        for q in range(width // LANES):
            r.g4[0, pl.ds(4 * q + i, 1), :] = grad[:, q * LANES : (q + 1) * LANES]

    loop(ipd, finish_merged)
    everyone(r.g4, 3)

    drain(r.ebuf.at[pl.ds(1, DP - 1)], r.eg_recv.at[0])
    value = r.eg[piece_rows(0), :]
    for d in range(1, DP):
        value = value + r.ebuf[d].astype(F32)
    r.eo[0] = value.astype(et)
    for d in range(1, DP):
        remote(r.eo.at[0], r.eo.at[DP - d], r.eg_send.at[1], r.eg_recv.at[1], across(d)).start()

    everyone_wait(r.g4, 3)
    up_gap = r.gate_up[:, 0:width] - r.gate_up[:, width:two]

    def gate_back(n, state):
        at = gate_block(n)
        grad_lo, grad_hi = lower_upper(r.g4, n)
        grad = exact_nt(grad_lo, up_gap[:, 0:LANES]) + exact_nt(grad_hi, up_gap[:, LANES:width])
        grad = grad * r.gate_slope[at, :]
        r.grad_down[at, :] = grad
        return state[0] + total(grad), state[1] + total(grad * r.gate_x[at, :])

    gate_shift_all, gate_gain_all = lax.fori_loop(0, gate_blocks, gate_back, (zero1, zero1))
    lead = r.gate_gain[...] * gate_scale

    def gate_norm_back(n):
        at = gate_block(n)
        grad = r.grad_down[at, :] - gate_shift_all * every - r.gate_x[at, :] * (gate_gain_all * every)
        r.grad_down[at, :] = jnp.where(valid, lead * grad, 0.0)

    loop(gate_blocks, gate_norm_back)
    r.grad_summary[...] = exact_nt(r.grad_down[0:8, :], r.gate_down[...])

    def second_back(i, state):
        att = r.att[pl.ds(i, 1), :]
        flat = r.grad_summary[pl.ds(i, 1), :] * wide(r.share[pl.ds(i, 1), :], width)

        def body(at, k, state):
            d = r.dm[at, :]
            new = []
            for g in range(2):
                lanes = slice(g * width, (g + 1) * width)
                value = (d * att[:, lanes] + flat) * r.slope2[at, lanes]
                r.act2[at, lanes] = value
                new.append((state[g][0] + fold(value), state[g][1] + fold(value * r.sp[at, lanes])))
            return tuple(new)

        return strips(i * CELLS, body, state, 16)

    state = lax.fori_loop(0, ipd, second_back, ((zero8, zero8), (zero8, zero8)))
    for g in range(2):
        put(r.g5, g * (width // LANES), total(state[g][0]))
        put(r.g5, (2 + g) * (width // LANES), total(state[g][1]))
    everyone(r.g5, 4)

    r.gate_gain_grad[...] = exact_nt(gate_gain_all, pickg)
    r.gate_shift_grad[...] = exact_nt(gate_shift_all, pickg)

    def gate_grads(n, state):
        at = gate_block(n)
        sum_lo, sum_hi = lower_upper(r.g3, n)
        grad_lo, grad_hi = lower_upper(r.g4, n)
        picked = exact_nt(r.grad_down[at, :], pickg)
        down = jnp.concatenate([exact_tn(picked, sum_lo), exact_tn(picked, sum_hi)], axis=1)
        squeezed = r.squeezed[at, :]
        up = jnp.concatenate([exact_tn(squeezed, grad_lo), exact_tn(squeezed, grad_hi)], axis=1)
        bias = jnp.concatenate([total(grad_lo), total(grad_hi)], axis=1)
        return state[0] + down, state[1] + up, state[2] + bias

    down, up, bias = lax.fori_loop(
        0, gate_blocks, gate_grads,
        (jnp.zeros((mg, width), F32), jnp.zeros((inner, width), F32), jnp.zeros((1, width), F32)),
    )
    r.down_grad[...] = down
    r.up_grad[...] = exact_nt(jnp.concatenate([up, -up], axis=1), pick2)
    r.bias_grad[...] = exact_nt(jnp.concatenate([bias, -bias], axis=1), pick2)

    everyone_wait(r.g5, 4)
    sums = jnp.sum(r.g5[...], axis=0)
    shift_grad, gain_grad = get(sums, 0, two), get(sums, two // LANES, two)
    r.second_gain_grad[...] = exact_nt(gain_grad, pick2)
    r.second_shift_grad[...] = exact_nt(shift_grad, pick2)
    lead2, base2, slant2 = gain2 * scale2, shift_grad * inverse, gain_grad * inverse

    def splits_back(i):
        def body(at, k, carry):
            there = pl.ds(pl.multiple_of((ch * ipd + i) * CELLS + k * STRIP, STRIP), STRIP)
            put_at = pl.ds(pl.multiple_of(SIDE + k * STRIP, SIDE), STRIP)
            mask = r.maskf[there, :]
            for q in range(two // LANES):
                g, p = q // (width // LANES), q % (width // LANES)
                lanes = slice(q * LANES, (q + 1) * LANES)
                d = mask * lead2[:, lanes] * (
                    r.act2[at, lanes] - base2[:, lanes] - r.sp[at, lanes] * slant2[:, lanes]
                )
                r.act2[at, lanes] = d
                before = jnp.where(not_first, pltpu.roll(d, 1, 0), 0.0)
                after = jnp.where(not_last, pltpu.roll(d, STRIP - 1, 0), 0.0)
                for n, value in enumerate((after, d, before)):
                    start = n * width + p * LANES
                    r.dsh[g, i, put_at, start : start + LANES] = value.astype(BF16)
            return carry

        strips(i * CELLS, body, 0)

    loop(ipd, splits_back)

    def first_back(i, state):
        out = []
        for g in range(2):
            lanes = slice(g * half, (g + 1) * half)
            left = jnp.concatenate(
                [r.dsh[g, i, (2 - k) * SIDE : (2 - k) * SIDE + CELLS, :] for k in range(3)], axis=1
            )
            value = dot(left, r.wt[g]) * r.slope1[image(i), lanes]
            r.dh1[rows_of(ch, i), lanes] = value.astype(BF16)
            out.append((state[g][0] + fold(value), state[g][1] + fold(value * r.red[image(i), lanes])))
        return tuple(out)

    zero_h = jnp.zeros((8, half), F32)
    state = lax.fori_loop(0, ipd, first_back, ((zero_h, zero_h), (zero_h, zero_h)))
    for g in range(2):
        r.r3[0, g : g + 1, :] = total(state[g][0])
        r.r3[0, 2 + g : 3 + g, :] = total(state[g][1])
    row(r.r3, 1)
    gd = Gather(2, lambda b, i: r.dh1.at[rows_of(b, i)], lambda b: r.dh1.at[block_rows(b)], ipd)
    loop(ipd, gd.send)

    def pass_x(i):
        for t in range(1, X):
            gx.from_peer(t, i)

    loop(ipd, pass_x)

    def turn_d(i):
        for g in range(2):
            r.dst[g, :, image(i)] = r.act2[image(i), g * width : (g + 1) * width].T.astype(BF16)

    loop(ipd, turn_d)
    per = CH // 2
    wide3 = 3 * half
    for k in range(3):
        for g in range(2):
            right = r.act[g, :, k * SIDE : k * SIDE + CELLS, :].reshape(own_rows, wide3)
            value = dot(r.dst[g], right)
            if c.split_inside:
                for q in range(per):
                    b = g * per + q
                    r.ss[k, b % 2, b // 2] = value[q * m2 : (q + 1) * m2, :].astype(BF16)
            else:
                r.split_part[g * width : (g + 1) * width, k * wide3 : (k + 1) * wide3] = value
        if c.split_inside:
            remote(r.ss.at[k, 1 - core], r.sin.at[k], r.sg_send.at[0, k], r.sg_recv.at[0, k], mate).start()
    row_sum(r.r3, 1, r.c3)
    column(r.c3, 2)
    slab = m2 // DP

    def split_spread(k):
        drain(r.sin.at[k], r.sg_recv.at[0, k])
        for t in range(X):
            value = (r.ss[k, core, t].astype(F32) + r.sin[k, t].astype(F32)).astype(BF16)
            r.sc[k, :, t] = value.reshape(DP, slab, wide3)
        for d in range(1, DP):
            remote(
                r.sc.at[k, (dp + d) % DP], r.sp1.at[k, DP - d], r.sg_send.at[1, k], r.sg_recv.at[1, k], across(d)
            ).start()

    def split_chips(k):
        drain(r.sp1.at[k, pl.ds(1, DP - 1)], r.sg_recv.at[1, k])
        for t in range(X):
            there = (chip + t) % X
            value = r.sc[k, dp, there].astype(F32)
            for d in range(1, DP):
                value = value + r.sp1[k, d, there].astype(F32)
            r.sx[k, t] = value.astype(BF16)
            if t:
                remote(r.sx.at[k, t], r.sxin.at[k, X - t], r.sg_send.at[2, k], r.sg_recv.at[2, k], peer(t)).start()

    def split_out(k):
        drain(r.sxin.at[k, pl.ds(1, X - 1)], r.sg_recv.at[2, k])
        value = r.sx[k, 0].astype(F32)
        for t in range(1, X):
            value = value + r.sxin[k, t].astype(F32)
        r.so[k, 0] = value.astype(BF16)
        for d in range(1, DP):
            remote(r.so.at[k, 0], r.so.at[k, DP - d], r.sg_send.at[3, k], r.sg_recv.at[3, k], across(d)).start()

    def split_step(step, k):
        if c.split_inside:
            step(k)

    for k in range(3):
        split_step(split_spread, k)
    column_wait(r.c3, 2)
    sums = jnp.sum(r.c3[...], axis=0)
    shift_grad, gain_grad = get(sums, 0, width), get(sums, 2, width)
    lead1, base1, slant1 = gain1 * scale1, shift_grad * inverse, gain_grad * inverse

    r.rg[...] = jnp.zeros((cw, width), F32)

    def from_x(i):
        gx.from_mate(i)
        for t in range(1, X):
            gx.from_pass(t, i)

    loop(ipd, from_x)
    gx.done()

    def reduced_back(b, i):
        def body(at, k, carry):
            mask = wide(r.maskf[at, :], width)
            d = mask * lead1 * (r.dh1[at, :].astype(F32) - base1 - r.xh1[at, :].astype(F32) * slant1)
            r.xh1[at, :] = d.astype(BF16)
            return carry

        strips((b * ipd + i) * CELLS, body, 0)
        r.rg[...] += dot(r.xt[b * ipd + i], r.xh1[rows_of(b, i), :])

    def input_back(b, i):
        at = rows_of(b, i)
        r.xv[at, :] = (r.dpre[at, :] + dot(r.xh1[at, :], r.wrt[...])).astype(BF16)
        pltpu.make_async_copy(r.xv.at[at], r.inputs_grad.at[at], r.store.at[1]).start()

    loop(ipd, lambda i: reduced_back(ch, i))

    def from_mate(i):
        gd.from_mate(i)
        reduced_back(block_of(0, False), i)

    loop(ipd, from_mate)
    loop(ipd, lambda i: input_back(ch, i))
    loop(ipd, lambda i: input_back(block_of(0, False), i))
    for t in range(1, X):

        def from_peer(i):
            gd.from_peer(t, i)
            reduced_back(block_of(t, True), i)

        loop(ipd, from_peer)
    split_step(split_chips, 0)
    for t in range(1, X):

        def from_pass(i):
            gd.from_pass(t, i)
            reduced_back(block_of(t, False), i)

        loop(ipd, from_pass)

    if c.reduce_inside:
        r.rs[...] = r.rg[...].T.astype(r.rs.dtype)
        for d in range(1, DP):
            remote(r.rs.at[piece_rows(d)], r.rbuf.at[DP - d], r.rg_send.at[0], r.rg_recv.at[0], across(d)).start()
    else:
        r.reduce_part[...] = r.rg[...].T
    split_step(split_chips, 1)
    for t in range(1, X):
        loop(ipd, lambda i: input_back(block_of(t, True), i))
    split_step(split_out, 0)
    if c.reduce_inside:
        groups = DP // CH
        goal = dp // groups
        drain(r.rbuf.at[pl.ds(1, DP - 1)], r.rg_recv.at[0])
        value = r.rs[piece_rows(0), :].astype(F32)
        for d in range(1, DP):
            value = value + r.rbuf[d].astype(F32)
        r.rsum[...] = value.astype(r.rsum.dtype)
        slot = r.rall.at[dp % groups, ch]
        for d in range(1, DP):
            remote(r.rsum, slot, r.rg_send.at[1], r.rg_recv.at[1], ((dp + d) % DP, goal)).start()

        @pl.when(goal == ch)
        def _():
            pltpu.make_async_copy(r.rsum, slot, r.rg_recv.at[1]).start()

        @pl.when(goal != ch)
        def _():
            remote(r.rsum, slot, r.rg_send.at[2], r.rg_recv.at[1], (dp, goal)).start()

    split_step(split_chips, 2)
    split_step(split_out, 1)
    for t in range(1, X):
        loop(ipd, lambda i: input_back(block_of(t, False), i))
    r.first_gain_grad[...] = exact_nt(gain_grad, pick1)
    r.first_shift_grad[...] = exact_nt(shift_grad, pick1)
    split_step(split_out, 2)

    drain(r.eo.at[pl.ds(1, DP - 1)], r.eg_recv.at[1])
    for d in range(DP):
        r.expand_grad[piece_rows(d), :] = r.eo[d].astype(F32)
    if c.reduce_inside:
        drain(r.rall, r.rg_recv.at[1])
        for s in range(groups):
            for q in range(CH):
                r.reduce_grad[s * piece : (s + 1) * piece, q * cw : (q + 1) * cw] = r.rall[s, q].astype(F32)
    if c.split_inside:
        for k in range(3):
            drain(r.so.at[k, pl.ds(1, DP - 1)], r.sg_recv.at[3, k])
            for p in range(3):
                at = slice(p * half, (p + 1) * half)
                block = jnp.concatenate(
                    [r.so[k, (d - dp + DP) % DP, :, at].astype(F32) for d in range(DP)], axis=0
                )
                r.split_grad[3 * k + p] = block.T

    for k, buf in enumerate((r.g1, r.g2, r.g3, r.g4, r.g5)):
        everyone_done(buf, k)
    column_done(r.c1, 0)
    column_done(r.c3, 2)
    row_done(r.r1, 0)
    row_done(r.r3, 1)
    column_done(r.c2, 1)
    rs2.done()
    for gather in (gm, gd) + shares:
        gather.done()
    drain(r.pbuf.at[pl.ds(1, CH - 1)], r.par_send.at[0])
    drain(r.ebuf.at[pl.ds(1, DP - 1)], r.eg_send.at[0])
    drain(r.ebuf.at[pl.ds(1, DP - 1)], r.eg_send.at[1])
    if c.reduce_inside:
        drain(r.rbuf.at[pl.ds(1, DP - 1)], r.rg_send.at[0])
        drain(r.rbuf.at[pl.ds(1, DP - 1)], r.rg_send.at[1])

        @pl.when(goal != ch)
        def _():
            drain(r.rsum, r.rg_send.at[2])

    if c.split_inside:
        for k in range(3):
            drain(r.sin.at[k], r.sg_send.at[0, k])
            drain(r.sp1.at[k, pl.ds(1, DP - 1)], r.sg_send.at[1, k])
            drain(r.sxin.at[k, pl.ds(1, X - 1)], r.sg_send.at[2, k])
            drain(r.so.at[k, pl.ds(1, DP - 1)], r.sg_send.at[3, k])
    drain(r.cv, r.store.at[0])
    drain(r.xv, r.store.at[1])


def hand_over(*refs):
    count = (len(refs) - 1) // 3
    sources, results, places, sems = refs[:count], refs[count : 2 * count], refs[2 * count : -1], refs[-1]
    copies = []
    for source, result, place in zip(sources, results, places):
        rows = source.shape[0]
        parts = 2 if rows >= 1024 else 1
        for p in range(parts):
            at = pl.ds(p * (rows // parts), rows // parts)
            k = len(copies)
            inward = pltpu.make_async_copy(source.at[at], place.at[at], sems.at[k, 0])
            copies.append((inward, pltpu.make_async_copy(place.at[at], result.at[at], sems.at[k, 1])))
            inward.start()
    for inward, outward in copies:
        inward.wait()
        outward.start()
    for inward, outward in copies:
        outward.wait()


ARGS = (
    "inputs", "resolution", "reduce_weight", "first_gain", "first_shift", "split_weight", "second_gain",
    "second_shift", "gate_down", "gate_gain", "gate_shift", "gate_up", "gate_bias", "expand_weight",
    "third_gain", "third_shift", "cotangent",
)


def per_device(*arrays):
    a = dict(zip(ARGS, arrays))
    c = types.SimpleNamespace()
    c.DP, c.CH = lax.axis_size("dp"), lax.axis_size("chan")
    c.X, c.D = c.CH // 2, c.DP * c.CH
    c.images = a["resolution"].shape[0]
    c.ipd = c.images // c.CH
    rows, c.cw = a["inputs"].shape
    c.width = a["reduce_weight"].shape[1]
    c.inner = a["gate_down"].shape[1]
    c.m1, c.m2, c.mg = c.width // c.CH, 2 * c.width // c.CH, c.inner // c.CH
    half, two = c.width // 2, 2 * c.width
    taps = 9 * half
    piece = c.width // c.DP
    piece_type = BF16 if piece % 16 == 0 else F32
    c.reduce_inside = c.DP % c.CH == 0 and piece % 8 == 0
    c.share = taps % (16 * c.DP) == 0 and c.width % (16 * c.DP) == 0
    c.split_inside = c.m2 % (16 * c.DP) == 0
    own = c.ipd * CELLS
    DP, CH, X, D, ipd, cw, width = c.DP, c.CH, c.X, c.D, c.ipd, c.cw, c.width
    for name in ARGS:
        if a[name].ndim == 1 and name != "resolution":
            a[name] = a[name].reshape(1, -1)
    a["split_weight"] = a["split_weight"].reshape(taps, c.m2)
    sds = jax.ShapeDtypeStruct
    outs = dict(
        block_out=sds((rows, cw), BF16),
        inputs_grad=sds((rows, cw), BF16),
        first_gain_grad=sds((1, c.m1), F32),
        first_shift_grad=sds((1, c.m1), F32),
        second_gain_grad=sds((1, c.m2), F32),
        second_shift_grad=sds((1, c.m2), F32),
        down_grad=sds((c.mg, width), F32),
        gate_gain_grad=sds((1, c.mg), F32),
        gate_shift_grad=sds((1, c.mg), F32),
        up_grad=sds((c.inner, c.m2), F32),
        bias_grad=sds((1, c.m2), F32),
        expand_grad=sds((width, cw), F32),
        third_gain_grad=sds((1, cw), F32),
        third_shift_grad=sds((1, cw), F32),
    )
    if c.reduce_inside:
        outs["reduce_grad"] = sds((c.m1, CH * cw), F32)
    else:
        outs["reduce_part"] = sds((width, cw), F32)
    if c.split_inside:
        outs["split_grad"] = sds((9, half, c.m2), F32)
    else:
        outs["split_part"] = sds((two, taps), F32)
    V = pltpu.VMEM
    dma = lambda *shape: pltpu.SemaphoreType.DMA(shape)
    scratch = dict(
        xv=V((rows, cw), BF16), cv=V((rows, cw), BF16), wr=V((cw, width), BF16), wrt=V((width, cw), BF16),
        wet=V((cw, width), BF16), xt=V((c.images, cw, CELLS), BF16), mt=V((c.images, width, CELLS), BF16),
        maskf=V((rows, LANES), F32), area=V((c.images, LANES), F32), maskb=V((rows, LANES), BF16), pbuf=V((CH, 8, two), F32),
        red=V((own, width), F32), slope1=V((own, width), F32), xh1=V((rows, width), BF16),
        act=V((2, ipd, TALL, 3 * half), BF16), dsh=V((2, ipd, TALL, 3 * width), BF16),
        wg=V((CH, taps, c.m2), BF16), wx=V((CH, width, cw), BF16), wf=V((2, taps, width), BF16), wt=V((2, 9 * width, half), BF16),
        sp=V((own, two), F32), slope2=V((own, two), F32), act2=V((own, two), F32), share=V((8, LANES), F32),
        gate_x=V((D * 8, LANES), F32), squeezed=V((D * 8, LANES), F32), gate_slope=V((D * 8, LANES), F32),
        grad_down=V((D * 8, LANES), F32), grad_summary=V((8, width), F32), att=V((8, two), F32),
        merged=V((rows, width), BF16), ex=V((rows, cw), F32), acc=V((16, cw), F32),
        dpre=V((rows, cw), F32), de=V((rows, cw), BF16), dm=V((own, width), F32), dh1=V((rows, width), BF16),

        dst=V((2, width, own), BF16),
        eg=V((width, cw), F32), es=V((width, cw), piece_type), ebuf=V((DP, piece, cw), piece_type),
        eo=V((DP, piece, cw), piece_type), rg=V((cw, width), F32),
        all_send=dma(5), all_recv=dma(5), col_send=dma(3), col_recv=dma(3), row_send=dma(2), row_recv=dma(2),
        rs_core_send=dma(2), rs_core_recv=dma(2, X, ipd), rs_chip_send=dma(2), rs_chip_recv=dma(2, X, ipd),
        ag_core_send=dma(3), ag_core_recv=dma(3, ipd), ag_chip_send=dma(3, X), ag_chip_recv=dma(3, X, ipd),
        ag_pass_send=dma(3, X), ag_pass_recv=dma(3, X, ipd), sh_core_send=dma(2), sh_core_recv=dma(2),
        sh_chip_send=dma(2, X), sh_chip_recv=dma(2, X), sh_col_send=dma(2, X), sh_col_recv=dma(2, X, DP),
        sh_pass_send=dma(2, X), sh_pass_recv=dma(2, X), par_send=dma(1), par_recv=dma(CH),
        eg_send=dma(2), eg_recv=dma(2), rg_send=dma(3), rg_recv=dma(2), sg_send=dma(4, 3), sg_recv=dma(4, 3),
        load=dma(2 + 2 * X), store=dma(2),
    )
    for name, count in (
        ("stage", X), ("inward", X), ("outward", X - 1), ("landed", X - 1), ("inward2", X), ("landed2", X - 1)
    ):
        scratch[name] = V((count, ipd, CELLS, width), BF16)
    for k in range(1, 6):
        scratch[f"g{k}"] = V((D, 8, LANES), F32)
    scratch["sums3"] = V((CH, 4, LANES), F32)
    for k in range(1, 4):
        scratch[f"c{k}"] = V((DP, 4, LANES), F32)
    scratch["r1"] = V((CH, 4, LANES), F32)
    scratch["r3"] = V((CH, 4, LANES), F32)
    if c.reduce_inside:
        scratch.update(
            rs=V((width, cw), piece_type), rbuf=V((DP, piece, cw), piece_type), rsum=V((piece, cw), piece_type),
            rall=V((DP // CH, CH, piece, cw), piece_type),
        )
    if c.split_inside:
        slab = c.m2 // DP
        scratch.update(
            ss=V((3, 2, X, c.m2, 3 * half), BF16), sin=V((3, X, c.m2, 3 * half), BF16),
            sc=V((3, DP, X, slab, 3 * half), BF16), sp1=V((3, DP, X, slab, 3 * half), BF16),
            sx=V((3, X, slab, 3 * half), BF16), sxin=V((3, X, slab, 3 * half), BF16),
            so=V((3, DP, slab, 3 * half), BF16),
        )
    anywhere = pl.BlockSpec(memory_space=pl.ANY)
    vmem = pl.BlockSpec(memory_space=pltpu.VMEM)
    spec = dict(
        inputs=anywhere, cotangent=anywhere, reduce_weight=anywhere, block_out=anywhere, inputs_grad=anywhere,
        resolution=pl.BlockSpec(memory_space=pltpu.SMEM),
    )
    names = tuple(ARGS) + tuple(outs) + tuple(scratch)
    results = pl.pallas_call(
        functools.partial(kernel, c, names),
        out_shape=tuple(outs.values()),
        in_specs=[spec.get(name, vmem) for name in ARGS],
        out_specs=tuple(spec.get(name, vmem) for name in outs),
        scratch_shapes=list(scratch.values()),
        compiler_params=pltpu.CompilerParams(
            collective_id=0, has_side_effects=True, vmem_limit_bytes=62 * 2**20
        ),
        name="block",
    )(*[a[name] for name in ARGS])
    results = pl.pallas_call(
        hand_over,
        out_shape=tuple(outs.values()),
        in_specs=[anywhere] * len(outs),
        out_specs=tuple(anywhere for _ in outs),
        scratch_shapes=[V(v.shape, v.dtype) for v in outs.values()] + [dma(4 * len(outs), 2)],
        compiler_params=pltpu.CompilerParams(vmem_limit_bytes=62 * 2**20),
        name="results",
    )(*results)
    o = dict(zip(outs, results))
    if not c.reduce_inside:
        place = lax.axis_index("chan")
        part = lax.psum(o["reduce_part"], "dp")
        part = lax.all_gather(part, "chan", axis=1, tiled=True)
        o["reduce_grad"] = lax.dynamic_slice_in_dim(part, place * c.m1, c.m1, 0)
    if not c.split_inside:
        place = lax.axis_index("chan")
        part = lax.psum(o["split_part"], ("dp", "chan"))
        part = lax.dynamic_slice_in_dim(part, place * c.m2, c.m2, 0)
        o["split_grad"] = part.T.reshape(9, half, c.m2)
    flat = lambda name: o[name].reshape(-1)
    return (
        o["block_out"], o["inputs_grad"], o["reduce_grad"].T, flat("first_gain_grad"), flat("first_shift_grad"),
        o["split_grad"], flat("second_gain_grad"), flat("second_shift_grad"), o["down_grad"].T,
        flat("gate_gain_grad"), flat("gate_shift_grad"), o["up_grad"], flat("bias_grad"), o["expand_grad"],
        flat("third_gain_grad"), flat("third_shift_grad"),
    )


def solution(mesh):
    placed = (
        P("dp", "chan"), P("dp"), P(), P("chan"), P("chan"), P(None, None, "chan"), P("chan"), P("chan"),
        P(), P(), P(), P(), P(), P(None, "chan"), P("chan"), P("chan"), P("dp", "chan"),
    )
    return jax.shard_map(
        per_device,
        mesh=mesh,
        in_specs=placed,
        out_specs=(
            P("dp", "chan"), P("dp", "chan"), P(None, "chan"), P("chan"), P("chan"), P(None, None, "chan"),
            P("chan"), P("chan"), P(None, "chan"), P("chan"), P("chan"), P(None, "chan"), P("chan"),
            P(None, "chan"), P("chan"), P("chan"),
        ),
        check_vma=False,
    )
```

```python
import functools
import types

import jax
import jax.numpy as jnp
from jax import lax
from jax.experimental import pallas as pl
from jax.experimental.pallas import tpu as pltpu
from jax.sharding import PartitionSpec as P

SIDE = 16
CELLS = SIDE * SIDE
TALL = CELLS + 2 * SIDE
LANES = 128
EPS = 1e-05
HIGHEST = lax.Precision.HIGHEST
F32 = jnp.float32
BF16 = jnp.bfloat16
MESH = pl.DeviceIdType.MESH
STRIP = 32


def wide(mask, width):
    return mask if width == LANES else jnp.concatenate([mask] * (width // LANES), axis=1)


def fold(values):
    return jnp.sum(values.reshape(values.shape[0] // 8, 8, values.shape[1]), axis=0)


def total(values):
    return jnp.sum(values, axis=0, keepdims=True)


def sigmoid(values):
    return 0.5 * jnp.tanh(0.5 * values) + 0.5


def dot(left, right):
    return jnp.dot(left, right, preferred_element_type=F32)


def exact(left, right):
    return jnp.dot(left, right, precision=HIGHEST, preferred_element_type=F32)


def exact_nt(left, right):
    return lax.dot_general(
        left, right, (((1,), (1,)), ((), ())), precision=HIGHEST, preferred_element_type=F32
    )


def exact_tn(left, right):
    return lax.dot_general(
        left, right, (((0,), (0,)), ((), ())), precision=HIGHEST, preferred_element_type=F32
    )


def flip(values):
    return values.astype(F32).T.astype(values.dtype)


def put(ref, row, vector):
    for part in range(vector.shape[1] // LANES):
        ref[0, row + part : row + part + 1, :] = vector[:, part * LANES : (part + 1) * LANES]


def get(block, row, width):
    parts = [block[row + q : row + q + 1, :] for q in range(width // LANES)]
    return parts[0] if len(parts) == 1 else jnp.concatenate(parts, axis=1)


def kernel(c, names, *refs):
    r = types.SimpleNamespace(**dict(zip(names, refs)))
    DP, CH, X, D, ipd, images = c.DP, c.CH, c.X, c.D, c.ipd, c.images
    width, cw, inner, m1, m2, mg = c.width, c.cw, c.inner, c.m1, c.m2, c.mg
    half, two = width // 2, 2 * width
    own_rows = ipd * CELLS
    taps = 9 * half
    dp = lax.axis_index("dp")
    ch = lax.axis_index("chan")
    core = ch % 2
    chip = ch // 2
    mate = (dp, ch + 1 - 2 * core)
    f0 = ((0, 0), (0, 0))

    def remote(src, dst, send, recv, device):
        return pltpu.make_async_remote_copy(
            src_ref=src, dst_ref=dst, send_sem=send, recv_sem=recv, device_id=device, device_id_type=MESH
        )

    def drain(ref, sem):
        pltpu.make_async_copy(ref, ref, sem).wait()

    def loop(count, body):
        def step(i, carry):
            body(i)
            return carry

        lax.fori_loop(0, count, step, 0)

    def peer(t):
        return (dp, ((chip + t) % X) * 2 + core)

    def across(d):
        return ((dp + d) % DP, ch)

    def block_of(t, same):
        return ((chip + t) % X) * 2 + (core if same else 1 - core)

    def rows_of(b, i):
        return pl.ds(pl.multiple_of((b * ipd + i) * CELLS, CELLS), CELLS)

    def block_rows(b):
        return pl.ds(pl.multiple_of(b * own_rows, own_rows), own_rows)

    def image(i):
        return pl.ds(pl.multiple_of(i * CELLS, CELLS), CELLS)

    def strips(base, body, carry, size=STRIP):
        def step(k, state):
            return body(pl.ds(pl.multiple_of(base + k * size, size), size), k, state)

        return lax.fori_loop(0, CELLS // size, step, carry)

    def everyone(buf, k, message=None):
        message = buf.at[0] if message is None else message

        def one(j, carry):
            d, q = j // CH, j % CH
            slot = ((DP - d) % DP) * CH + (CH - q) % CH
            remote(buf.at[0], buf.at[slot], r.all_send.at[k], r.all_recv.at[k], ((dp + d) % DP, (ch + q) % CH)).start()
            return carry

        lax.fori_loop(1, D, one, 0)

    def everyone_wait(buf, k):
        drain(buf.at[pl.ds(1, D - 1)], r.all_recv.at[k])

    def everyone_wait_on(buf, sem):
        drain(buf.at[pl.ds(1, D - 1)], sem)

    def everyone_done(buf, k):
        drain(buf.at[pl.ds(1, D - 1)], r.all_send.at[k])

    def column(buf, k):
        for d in range(1, DP):
            remote(buf.at[0], buf.at[DP - d], r.col_send.at[k], r.col_recv.at[k], across(d)).start()

    def row(buf, k, source=None):
        for q in range(1, CH):
            src = buf.at[0] if source is None else source.at[(ch + q) % CH]
            remote(src, buf.at[CH - q], r.row_send.at[k], r.row_recv.at[k], (dp, (ch + q) % CH)).start()

    def row_sum(buf, k, column_buf):
        drain(buf.at[pl.ds(1, CH - 1)], r.row_recv.at[k])
        column_buf[0] = jnp.sum(buf[...], axis=0)

    def row_done(buf, k):
        drain(buf.at[pl.ds(1, CH - 1)], r.row_send.at[k])

    def column_wait(buf, k):
        drain(buf.at[pl.ds(1, DP - 1)], r.col_recv.at[k])

    def column_done(buf, k):
        drain(buf.at[pl.ds(1, DP - 1)], r.col_send.at[k])

    class Scatter:
        def __init__(self, k, stage, inward, outward, landed, keep):
            self.k, self.stage, self.inward = k, stage, inward
            self.outward, self.landed, self.keep = outward, landed, keep

        def compute_mate(self, t, part):
            def body(i):
                self.stage[t, i] = part(block_of(t, False), i).astype(BF16)

            loop(ipd, body)

        def send_mate(self, t):
            def body(i):
                remote(
                    self.stage.at[t, i], self.inward.at[t, i],
                    r.rs_core_send.at[self.k], r.rs_core_recv.at[self.k, t, i], mate,
                ).start()

            loop(ipd, body)

        def mate_one(self, t, i, part):
            self.stage[t, i] = part(block_of(t, False), i).astype(BF16)
            remote(
                self.stage.at[t, i], self.inward.at[t, i],
                r.rs_core_send.at[self.k], r.rs_core_recv.at[self.k, t, i], mate,
            ).start()

        def to_mate(self, t, part):
            loop(ipd, lambda i: self.mate_one(t, i, part))

        def peer_one(self, t, i, part):
            value = part(block_of(t, True), i)
            drain(self.inward.at[t, i], r.rs_core_recv.at[self.k, t, i])
            self.outward[t - 1, i] = (value + self.inward[t, i].astype(F32)).astype(BF16)
            remote(
                self.outward.at[t - 1, i], self.landed.at[X - t - 1, i],
                r.rs_chip_send.at[self.k], r.rs_chip_recv.at[self.k, X - t, i], peer(t),
            ).start()

        def to_peer(self, t, part):
            loop(ipd, lambda i: self.peer_one(t, i, part))

        def both(self, t, part):
            self.mate_one(t, 0, part)

            def body(i, carry):
                self.mate_one(t, i, part)
                self.peer_one(t, i - 1, part)
                return carry

            lax.fori_loop(1, ipd, body, 0)
            self.peer_one(t, ipd - 1, part)

        def own(self, part):
            def body(i):
                value = part(ch, i)
                drain(self.inward.at[0, i], r.rs_core_recv.at[self.k, 0, i])
                self.keep[image(i), :] = value + self.inward[0, i].astype(F32)

            loop(ipd, body)

        def arrive(self, i):
            for t in range(1, X):
                drain(self.landed.at[t - 1, i], r.rs_chip_recv.at[self.k, t, i])

        def extra(self, i, at, lanes):
            value = self.landed[0, i, at, lanes].astype(F32)
            for t in range(2, X):
                value = value + self.landed[t - 1, i, at, lanes].astype(F32)
            return value

        def done(self):
            drain(self.stage, r.rs_core_send.at[self.k])
            drain(self.outward, r.rs_chip_send.at[self.k])

    class Gather:
        def __init__(self, k, place, whole, pieces):
            self.k, self.place, self.whole, self.pieces = k, place, whole, pieces

        def send(self, i):
            src = self.place(ch, i)
            remote(src, src, r.ag_core_send.at[self.k], r.ag_core_recv.at[self.k, i], mate).start()
            for t in range(1, X):
                remote(src, src, r.ag_chip_send.at[self.k, t], r.ag_chip_recv.at[self.k, X - t, i], peer(t)).start()

        def from_mate(self, i):
            drain(self.place(block_of(0, False), i), r.ag_core_recv.at[self.k, i])

        def from_peer(self, t, i):
            ref = self.place(block_of(t, True), i)
            drain(ref, r.ag_chip_recv.at[self.k, t, i])
            remote(ref, ref, r.ag_pass_send.at[self.k, t], r.ag_pass_recv.at[self.k, t, i], mate).start()

        def from_pass(self, t, i):
            drain(self.place(block_of(t, False), i), r.ag_pass_recv.at[self.k, t, i])

        def done(self):
            drain(self.whole(ch), r.ag_core_send.at[self.k])
            for t in range(1, X):
                drain(self.whole(ch), r.ag_chip_send.at[self.k, t])
                drain(self.whole(block_of(t, True)), r.ag_pass_send.at[self.k, t])

    class Share:
        def __init__(self, k, blocks, rows):
            self.k, self.blocks, self.piece = k, blocks, rows // DP

        def part(self, b, d):
            at = pl.ds(pl.multiple_of(((dp + d) % DP) * self.piece, self.piece), self.piece)
            return self.blocks.at[b, at]

        def send(self):
            own = self.blocks.at[ch]
            remote(own, own, r.sh_core_send.at[self.k], r.sh_core_recv.at[self.k], mate).start()
            for t in range(1, X):
                src = self.part(ch, 0) if c.share else own
                remote(src, src, r.sh_chip_send.at[self.k, t], r.sh_chip_recv.at[self.k, X - t], peer(t)).start()

        def spread(self):
            for t in range(1, X):
                b = block_of(t, True)
                src = self.part(b, 0) if c.share else self.blocks.at[b]
                drain(src, r.sh_chip_recv.at[self.k, t])
                if c.share:
                    for d in range(1, DP):
                        remote(src, src, r.sh_col_send.at[self.k, t], r.sh_col_recv.at[self.k, t, DP - d], across(d)).start()

        def hand(self):
            for t in range(1, X):
                b = block_of(t, True)
                if c.share:
                    for d in range(1, DP):
                        drain(self.part(b, d), r.sh_col_recv.at[self.k, t, d])
                whole = self.blocks.at[b]
                remote(whole, whole, r.sh_pass_send.at[self.k, t], r.sh_pass_recv.at[self.k, t], mate).start()

        def take(self):
            drain(self.blocks.at[block_of(0, False)], r.sh_core_recv.at[self.k])
            for t in range(1, X):
                drain(self.blocks.at[block_of(t, False)], r.sh_pass_recv.at[self.k, t])

        def done(self):
            own = self.blocks.at[ch]
            drain(own, r.sh_core_send.at[self.k])
            for t in range(1, X):
                whole = self.blocks.at[block_of(t, True)]
                drain(self.part(ch, 0) if c.share else own, r.sh_chip_send.at[self.k, t])
                drain(whole, r.sh_pass_send.at[self.k, t])
                if c.share:
                    for d in range(1, DP):
                        drain(self.part(block_of(t, True), 0), r.sh_col_send.at[self.k, t])

    barrier = pltpu.get_barrier_semaphore()

    def greet(j, carry):
        pl.semaphore_signal(
            barrier, inc=1, device_id=((dp + j // CH) % DP, (ch + j % CH) % CH), device_id_type=MESH
        )
        return carry

    lax.fori_loop(1, D, greet, 0)

    load_w = pltpu.make_async_copy(
        r.reduce_weight.at[pl.ds(pl.multiple_of(ch * cw, cw), cw)], r.wr, r.load.at[0]
    )
    load_w.start()
    order = []
    for t in list(range(1, X)) + [0]:
        order += [block_of(t, False), block_of(t, True)]
    loads = []
    for k, b in enumerate(order):
        at = pl.ds(pl.multiple_of(b * own_rows, own_rows), own_rows)
        loads.append(pltpu.make_async_copy(r.inputs.at[at], r.xv.at[at], r.load.at[2 + k]))
        loads[-1].start()
    load_c = pltpu.make_async_copy(r.cotangent, r.cv, r.load.at[1])
    load_c.start()

    row_at = lax.broadcasted_iota(jnp.int32, (CELLS, LANES), 0)
    spot_r = lax.shift_right_logical(row_at, 4)
    spot_c = lax.bitwise_and(row_at, 15)

    def make_mask(j):
        side = 12 + 2 * r.resolution[j]
        mask = jnp.where(jnp.logical_and(spot_r < side, spot_c < side), 1.0, 0.0)
        r.area[pl.ds(j, 1), :] = jnp.full((1, LANES), side * side, jnp.int32).astype(F32)
        r.maskf[image(j), :] = mask
        r.maskb[image(j), :] = mask.astype(BF16)

    loop(images, make_mask)

    def part_reduce(b, i):
        at = rows_of(b, i)
        x = r.xv[at, :] * wide(r.maskb[at, :], cw)
        r.xv[at, :] = x
        return dot(x, r.wr[...])

    r.wg[ch] = r.split_weight[...]
    r.wx[ch] = r.expand_weight[...]
    shares = (Share(0, r.wg, taps), Share(1, r.wx, width))

    load_w.wait()
    rs1 = Scatter(0, r.stage, r.inward, r.outward, r.landed, r.red)
    loads[0].wait()
    rs1.compute_mate(1, part_reduce)
    pl.semaphore_wait(barrier, D - 1)
    rs1.send_mate(1)
    for share in shares:
        share.send()
    for t in range(1, X):
        if t > 1:
            loads[2 * t - 2].wait()
            rs1.to_mate(t, part_reduce)
        loads[2 * t - 1].wait()
        rs1.to_peer(t, part_reduce)
    for share in shares:
        share.spread()
    loads[2 * X - 2].wait()
    rs1.to_mate(0, part_reduce)
    loads[2 * X - 1].wait()
    rs1.own(part_reduce)

    def selector(parts, mine):
        row = lax.broadcasted_iota(jnp.int32, (mine, mine * parts), 0)
        col = lax.broadcasted_iota(jnp.int32, (mine, mine * parts), 1)
        return jnp.where(col == row + ch * mine, 1.0, 0.0)

    pick1 = selector(CH, m1)
    pick2 = selector(CH, m2)
    pickg = selector(CH, mg)
    r.pbuf[0, 0:1, 0:width] = exact(r.first_gain[...], pick1)
    r.pbuf[0, 1:2, 0:width] = exact(r.first_shift[...], pick1)
    r.pbuf[0, 2:3, :] = exact(r.second_gain[...], pick2)
    r.pbuf[0, 3:4, :] = exact(r.second_shift[...], pick2)

    for q in range(1, CH):
        remote(r.pbuf.at[0], r.pbuf.at[CH - q], r.par_send.at[0], r.par_recv.at[CH - q], (dp, (ch + q) % CH)).start()

    r.wrt[...] = flip(r.wr[...])
    r.wet[...] = flip(r.expand_weight[...])

    def turn_x(j):
        r.xt[j] = flip(r.xv[image(j), :])

    loop(images, turn_x)
    for g in range(2):
        for i in range(ipd):
            r.act[g, i, 0:SIDE, :] = jnp.zeros((SIDE, 3 * half), BF16)
            r.act[g, i, CELLS + SIDE : TALL, :] = jnp.zeros((SIDE, 3 * half), BF16)
            r.dsh[g, i, 0:SIDE, :] = jnp.zeros((SIDE, 3 * width), BF16)
            r.dsh[g, i, CELLS + SIDE : TALL, :] = jnp.zeros((SIDE, 3 * width), BF16)

    def finish_reduce(i, state):
        rs1.arrive(i)

        def body(at, k, state):
            first, second = state
            value = r.red[at, :] + rs1.extra(i, pl.ds(pl.multiple_of(k * STRIP, STRIP), STRIP), slice(None))
            r.red[at, :] = value
            return (first + fold(value), second + fold(value * value))

        return strips(i * CELLS, body, state)

    zero8 = jnp.zeros((8, width), F32)
    first, second = lax.fori_loop(0, ipd, finish_reduce, (zero8, zero8))

    pixels = lax.fori_loop(
        0, ipd, lambda i, count: count + r.area[pl.ds(ch * ipd + i, 1), :], jnp.zeros((1, LANES), F32)
    )
    r.g1[0] = jnp.zeros((8, LANES), F32)
    put(r.g1, 0, total(first))
    put(r.g1, width // LANES, total(second))
    r.g1[0, 6:7, :] = pixels
    everyone(r.g1, 0)
    for share in shares:
        share.hand()
    everyone_wait(r.g1, 0)
    sums = jnp.sum(r.g1[...], axis=0)
    count = sums[6:7, 0:1]
    inverse = 1.0 / count
    params = r.pbuf[0]
    for q in range(1, CH):
        drain(r.pbuf.at[q], r.par_recv.at[q])
        params = params + r.pbuf[q]
    gain1, shift1 = params[0:1, 0:width], params[1:2, 0:width]
    gain2, shift2 = params[2:3, :], params[3:4, :]

    def moments(first, second):
        mean = first * inverse
        return mean, lax.rsqrt(second * inverse - mean * mean + EPS)

    mean1, scale1 = moments(get(sums, 0, width), get(sums, width // LANES, width))

    place_x = lambda b, i: r.xh1.at[rows_of(b, i)]
    gx = Gather(0, place_x, lambda b: r.xh1.at[block_rows(b)], ipd)

    strip_c = lax.bitwise_and(lax.broadcasted_iota(jnp.int32, (STRIP, LANES), 0), 15)
    not_first = strip_c != 0
    not_last = strip_c != 15

    def first_act(i):
        def body(at, k, carry):
            there = pl.ds(pl.multiple_of((ch * ipd + i) * CELLS + k * STRIP, STRIP), STRIP)
            put_at = pl.ds(pl.multiple_of(SIDE + k * STRIP, SIDE), STRIP)
            mask = r.maskf[there, :]
            for g in range(2):
                lanes = slice(g * half, (g + 1) * half)
                xh = (r.red[at, lanes] - mean1[:, lanes]) * scale1[:, lanes]
                h = gain1[:, lanes] * xh + shift1[:, lanes]
                s = sigmoid(h)
                y = h * s
                r.red[at, lanes] = xh
                r.xh1[there, lanes] = xh.astype(BF16)
                r.slope1[at, lanes] = mask * (s + y - y * s)
                a = mask * y
                before = jnp.where(not_first, pltpu.roll(a, 1, 0), 0.0)
                after = jnp.where(not_last, pltpu.roll(a, STRIP - 1, 0), 0.0)
                r.act[g, i, put_at, 0:half] = before.astype(BF16)
                r.act[g, i, put_at, half : 2 * half] = a.astype(BF16)
                r.act[g, i, put_at, 2 * half : 3 * half] = after.astype(BF16)
            return carry

        strips(i * CELLS, body, 0)

    loop(ipd, first_act)

    for share in shares:
        share.take()
    for g in range(2):
        for q in range(CH // 2):
            r.wf[g, :, q * m2 : (q + 1) * m2] = r.wg[g * (CH // 2) + q]

    def conv(i, state):
        there = rows_of(ch, i)
        out = []
        for g in range(2):
            lanes = slice(g * width, (g + 1) * width)
            left = jnp.concatenate(
                [r.act[g, i, k * SIDE : k * SIDE + CELLS, :] for k in range(3)], axis=1
            )
            value = dot(left, r.wf[g]) * wide(r.maskf[there, :], width)
            r.sp[image(i), lanes] = value
            out.append((state[g][0] + fold(value), state[g][1] + fold(value * value)))
        return tuple(out)

    state = lax.fori_loop(0, ipd, conv, ((zero8, zero8), (zero8, zero8)))
    for g in range(2):
        put(r.g2, g * (width // LANES), total(state[g][0]))
        put(r.g2, (2 + g) * (width // LANES), total(state[g][1]))
    everyone(r.g2, 1)
    loop(ipd // 2, gx.send)

    for g in range(2):
        for tap in range(9):
            r.wt[g, tap * width : (tap + 1) * width, :] = flip(r.wf[g, tap * half : (tap + 1) * half, :])

    everyone_wait(r.g2, 1)
    sums = jnp.sum(r.g2[...], axis=0)
    mean2, scale2 = moments(get(sums, 0, two), get(sums, two // LANES, two))

    r.g3[0] = jnp.zeros((8, LANES), F32)

    def second_act(i):
        def body(at, k, state):
            there = pl.ds(pl.multiple_of((ch * ipd + i) * CELLS + k * STRIP, STRIP), STRIP)
            mask = r.maskf[there, :]
            new = []
            for q in range(two // LANES):
                lanes = slice(q * LANES, (q + 1) * LANES)
                xh = (r.sp[at, lanes] - mean2[:, lanes]) * scale2[:, lanes]
                h = gain2[:, lanes] * xh + shift2[:, lanes]
                s = sigmoid(h)
                y = h * s
                r.sp[at, lanes] = xh
                r.slope2[at, lanes] = mask * (s + y - y * s)
                a = mask * y
                r.act2[at, lanes] = a
                new.append(state[q] + fold(a))
            return tuple(new)

        zero = jnp.zeros((8, LANES), F32)
        pooled = strips(i * CELLS, body, (zero,) * (two // LANES))
        share = 1.0 / r.area[pl.ds(ch * ipd + i, 1), :]
        r.share[pl.ds(i, 1), :] = share
        n = width // LANES
        for q in range(n):
            r.g3[0, pl.ds(4 * q + i, 1), :] = total(pooled[q] + pooled[n + q]) * share

    loop(ipd, second_act)
    everyone(r.g3, 2)
    lax.fori_loop(ipd // 2, ipd, lambda i, carry: (gx.send(i), carry)[1], 0)


    gate_rows = min(D * 8, 2 * LANES)
    gate_blocks = D * 8 // gate_rows
    gate_at = lax.broadcasted_iota(jnp.int32, (gate_rows, LANES), 0)
    valid = lax.bitwise_and(gate_at, 7) < ipd
    every = 1.0 / (D * ipd)

    def gate_block(n):
        return pl.ds(pl.multiple_of(n * gate_rows, gate_rows), gate_rows)

    def lower_upper(buf, n):
        slots = gate_rows // 8
        both = buf[pl.ds(n * slots, slots)].reshape(gate_rows, LANES)
        return jnp.where(valid, both, 0.0), jnp.where(valid, pltpu.roll(both, gate_rows - 4, 0), 0.0)

    def gate_in(n, state):
        sum_lo, sum_hi = lower_upper(r.g3, n)
        pre = exact(sum_lo, r.gate_down[0:LANES, :]) + exact(sum_hi, r.gate_down[LANES:, :])
        r.gate_x[gate_block(n), :] = pre
        return state[0] + total(pre), state[1] + total(pre * pre)

    everyone_wait(r.g3, 2)
    zero1 = jnp.zeros((1, LANES), F32)
    first, second = lax.fori_loop(0, gate_blocks, gate_in, (zero1, zero1))
    gate_mean = first * every
    gate_scale = lax.rsqrt(second * every - gate_mean * gate_mean + EPS)

    def gate_out(n):
        at = gate_block(n)
        x = (r.gate_x[at, :] - gate_mean) * gate_scale
        h = r.gate_gain[...] * x + r.gate_shift[...]
        s = sigmoid(h)
        y = h * s
        r.gate_x[at, :] = x
        r.squeezed[at, :] = y
        r.gate_slope[at, :] = s + y - y * s

    loop(gate_blocks, gate_out)
    logits = exact(r.squeezed[0:8, :], r.gate_up[...]) + r.gate_bias[...]
    top = jnp.maximum(logits[:, :width], logits[:, width:])
    upper = jnp.exp(logits[:, :width] - top)
    lower = jnp.exp(logits[:, width:] - top)
    both = upper + lower
    r.att[:, 0:width] = upper / both
    r.att[:, width:two] = lower / both

    gm = Gather(1, lambda b, i: r.merged.at[rows_of(b, i)], lambda b: r.merged.at[block_rows(b)], ipd)

    def merge(i):
        att = r.att[pl.ds(i, 1), :]

        def body(at, k, carry):
            there = pl.ds(pl.multiple_of((ch * ipd + i) * CELLS + k * STRIP, STRIP), STRIP)
            left = (r.act2[at, 0:width] * att[:, 0:width]).astype(BF16)
            right = (r.act2[at, width:two] * att[:, width:two]).astype(BF16)
            r.merged[there, :] = (left.astype(F32) + right.astype(F32)).astype(BF16)
            return carry

        strips(i * CELLS, body, 0)

    merge(0)
    gm.send(0)
    lax.fori_loop(1, ipd, lambda i, carry: (merge(i), carry)[1], 0)

    def expand_sums(k):
        def body(i, state):
            value = dot(r.merged[rows_of(ch, i), :], r.wx[k])
            return (state[0] + fold(value), state[1] + fold(value * value))

        first, second = lax.fori_loop(0, ipd, body, (zero_c, zero_c))
        put(r.sums3.at[pl.ds(k, 1)], 0, total(first))
        put(r.sums3.at[pl.ds(k, 1)], cw // LANES, total(second))

    zero_c = jnp.zeros((8, cw), F32)
    loop(CH, expand_sums)
    r.r1[0] = r.sums3[ch]
    row(r.r1, 0, r.sums3)
    lax.fori_loop(1, ipd, lambda i, carry: (gm.send(i), carry)[1], 0)
    load_c.wait()
    r.acc[...] = jnp.zeros((16, cw), F32)
    row_sum(r.r1, 0, r.c1)
    column(r.c1, 0)

    def slope_guess():
        root = 3.0**0.5
        points = []
        for z in (-root, 0.0, root):
            h = shift2 + z * gain2
            s = sigmoid(h)
            points.append(s + h * s - h * s * s)
        low, mid, high = points
        return (low + 4.0 * mid + high) * (1.0 / 6.0), (high - low) * (root / 6.0)

    guess = slope_guess()

    def slope_sums(i):
        share = r.share[pl.ds(i, 1), :]
        zero = jnp.zeros((8, LANES), F32)
        n = width // LANES

        def body(at, k, state):
            new = []
            for q in range(2 * n):
                lanes = slice(q * LANES, (q + 1) * LANES)
                slope = r.slope2[at, lanes]
                new.append((state[q][0] + fold(slope), state[q][1] + fold(slope * r.sp[at, lanes])))
            return tuple(new)

        state = strips(i * CELLS, body, ((zero, zero),) * (2 * n))
        for q in range(2 * n):
            for stat in range(2):
                row_at = (stat * n + q % n) * 8 + 4 * (q // n)
                r.slopes[pl.ds(row_at + i, 1), :] = (
                    total(state[q][stat]) * share - guess[stat][:, q * LANES : (q + 1) * LANES]
                )

    r.slopes[...] = jnp.zeros_like(r.slopes)
    loop(ipd, slope_sums)
    r.g5[0] = r.slopes[...].astype(BF16)

    def turn_own(j):
        r.mt[ch * ipd + j] = flip(r.merged[rows_of(ch, j), :])

    loop(ipd, turn_own)
    column_wait(r.c1, 0)
    sums = jnp.sum(r.c1[...], axis=0)
    mean3, scale3 = moments(get(sums, 0, cw), get(sums, cw // LANES, cw))
    gain3, shift3 = r.third_gain[...], r.third_shift[...]

    def outputs(b, i):
        r.ex[rows_of(b, i), :] = dot(r.merged[rows_of(b, i), :], r.expand_weight[...])

        def body(at, k, state):
            shift, cross = state
            mask = wide(r.maskf[at, :], cw)
            xh = (r.ex[at, :] - mean3) * scale3
            h = gain3 * xh + shift3 + r.xv[at, :].astype(F32)
            s = sigmoid(h)
            y = h * s
            d = r.cv[at, :].astype(F32) * mask * (s + y - y * s)
            r.cv[at, :] = (mask * y).astype(BF16)
            r.dpre[at, :] = d
            r.ex[at, :] = xh
            return (shift + fold(d), cross + fold(d * xh))

        shift, cross = strips((b * ipd + i) * CELLS, body, (zero_c, zero_c))
        r.acc[0:8, :] += shift
        r.acc[8:16, :] += cross
        at = rows_of(b, i)
        pltpu.make_async_copy(r.cv.at[at], r.block_out.at[at], r.store.at[0]).start()

    loop(ipd, lambda i: outputs(ch, i))

    def outputs_mate(i):
        gm.from_mate(i)
        outputs(block_of(0, False), i)

    loop(ipd, outputs_mate)
    for t in range(1, X):

        def outputs_peer(i):
            gm.from_peer(t, i)
            outputs(block_of(t, True), i)

        loop(ipd, outputs_peer)
    everyone(r.g5, 4)
    for t in range(1, X):

        def outputs_pass(i):
            gm.from_pass(t, i)
            outputs(block_of(t, False), i)

        loop(ipd, outputs_pass)
    put(r.c2, 0, total(r.acc[0:8, :]))
    put(r.c2, cw // LANES, total(r.acc[8:16, :]))
    column(r.c2, 1)

    def turn_other(j):
        b = j // ipd
        b = jnp.where(b < ch, b, b + 1)
        at = b * ipd + j % ipd
        r.mt[at] = flip(r.merged[image(at), :])

    loop(images - ipd, turn_other)
    column_wait(r.c2, 1)
    sums = jnp.sum(r.c2[...], axis=0)
    shift_grad, gain_grad = get(sums, 0, cw), get(sums, cw // LANES, cw)
    r.third_gain_grad[...] = gain_grad
    r.third_shift_grad[...] = shift_grad
    lead3, base3, slant3 = gain3 * scale3, shift_grad * inverse, gain_grad * inverse

    def part_merged(b, i):
        def body(at, k, carry):
            mask = wide(r.maskf[at, :], cw)
            d = mask * lead3 * (r.dpre[at, :] - base3 - r.ex[at, :] * slant3)
            r.de[at, :] = d.astype(BF16)
            return carry

        strips((b * ipd + i) * CELLS, body, 0)
        return dot(r.de[rows_of(b, i), :], r.wet[...])

    rs1.done()
    rs2 = Scatter(1, r.stage, r.inward2, r.outward, r.landed2, r.dm)
    for t in range(1, X):
        rs2.both(t, part_merged)
    rs2.to_mate(0, part_merged)
    rs2.own(part_merged)

    def grow(j):
        r.eg[...] += dot(r.mt[j], r.de[image(j), :])

    r.eg[...] = dot(r.mt[0], r.de[image(0), :])
    lax.fori_loop(1, images, lambda j, carry: (grow(j), carry)[1], 0)
    piece = width // DP
    et = r.es.dtype
    r.es[...] = r.eg[...].astype(et)

    def piece_rows(d):
        return pl.ds(pl.multiple_of(((dp + d) % DP) * piece, piece), piece)

    for d in range(1, DP):
        remote(r.es.at[piece_rows(d)], r.ebuf.at[DP - d], r.eg_send.at[0], r.eg_recv.at[0], across(d)).start()

    r.told[...] = jnp.zeros((16, LANES), F32)

    def finish_merged(i):
        rs2.arrive(i)

        def body(at, k, state):
            here = pl.ds(pl.multiple_of(k * SIDE, SIDE), SIDE)
            value = r.dm[at, :] + rs2.extra(i, here, slice(None))
            r.dm[at, :] = value
            new = [state[0] + fold(value * (r.act2[at, 0:width] - r.act2[at, width:two]))]
            for g in range(2):
                lanes = slice(g * width, (g + 1) * width)
                part = value * r.slope2[at, lanes]
                new += [state[1 + 2 * g] + fold(part), state[2 + 2 * g] + fold(part * r.sp[at, lanes])]
            return tuple(new)

        gap, *parts = strips(i * CELLS, body, (zero8,) * 5, SIDE)
        att = r.att[pl.ds(i, 1), :]
        grad = att[:, 0:width] * att[:, width:two] * total(gap)
        n = width // LANES
        for q in range(n):
            r.told[pl.ds(4 * q + i, 1), :] = grad[:, q * LANES : (q + 1) * LANES]
        for g in range(2):
            for stat in range(2):
                part = total(parts[2 * g + stat]) * att[:, g * width : (g + 1) * width]
                for q in range(n):
                    at = 8 + (2 * stat + g) * n + q
                    r.told[at : at + 1, :] += part[:, q * LANES : (q + 1) * LANES]

    loop(ipd, finish_merged)
    r.r4[0] = r.told[8:16, :]
    row(r.r4, 2)
    r.g4[0] = r.told[0:8, :]
    everyone(r.g4, 3)
    row_sum(r.r4, 2, r.c4)
    column(r.c4, 3)
    everyone_wait(r.g5, 4)
    everyone_wait(r.g4, 3)
    up_gap = r.gate_up[:, 0:width] - r.gate_up[:, width:two]

    def gate_back(n, state):
        at = gate_block(n)
        grad_lo, grad_hi = lower_upper(r.g4, n)
        grad = exact_nt(grad_lo, up_gap[:, 0:LANES]) + exact_nt(grad_hi, up_gap[:, LANES:width])
        grad = grad * r.gate_slope[at, :]
        r.grad_down[at, :] = grad
        return state[0] + total(grad), state[1] + total(grad * r.gate_x[at, :])

    gate_shift_all, gate_gain_all = lax.fori_loop(0, gate_blocks, gate_back, (zero1, zero1))
    lead = r.gate_gain[...] * gate_scale

    def gate_norm_back(n, state):
        at = gate_block(n)
        grad = r.grad_down[at, :] - gate_shift_all * every - r.gate_x[at, :] * (gate_gain_all * every)
        grad = jnp.where(valid, lead * grad, 0.0)
        r.grad_down[at, :] = grad
        summary = exact_nt(grad, r.gate_down[...])
        slots = gate_rows // 8

        @pl.when(n == 0)
        def _():
            r.grad_summary[...] = summary[0:8, :]

        slopes = r.g5[pl.ds(n * slots, slots)].astype(F32)
        new = []
        for stat in range(2):
            for p in range(width // LANES):
                part = summary[:, p * LANES : (p + 1) * LANES]
                part = (part + pltpu.roll(part, 4, 0)).reshape(slots, 8, LANES)
                k = stat * (width // LANES) + p
                new.append(state[k] + jnp.sum(part * slopes[:, 8 * k : 8 * k + 8, :], axis=0))
        new.append(state[-1] + total(summary))
        return tuple(new)

    n_half = width // LANES
    zero = jnp.zeros((8, LANES), F32)
    *flats, summed = lax.fori_loop(
        0, gate_blocks, gate_norm_back, (zero,) * (2 * n_half) + (jnp.zeros((1, width), F32),)
    )
    guess = slope_guess()
    column_wait(r.c4, 3)
    told = jnp.sum(r.c4[...], axis=0)

    def second_sum(stat):
        parts = []
        for q in range(2 * n_half):
            flat = flats[stat * n_half + q % n_half]
            flat = total(flat[4 * (q // n_half) : 4 * (q // n_half) + 4, :])
            at = 2 * n_half * stat + q
            lanes = slice(q % n_half * LANES, (q % n_half + 1) * LANES)
            flat = flat + guess[stat][:, q * LANES : (q + 1) * LANES] * summed[:, lanes]
            parts.append(flat + told[at : at + 1, :])
        return jnp.concatenate(parts, axis=1)

    shift_grad2, gain_grad2 = second_sum(0), second_sum(1)
    lead2, base2, slant2 = gain2 * scale2, shift_grad2 * inverse, gain_grad2 * inverse

    def splits_back(i):
        att = r.att[pl.ds(i, 1), :]
        flat = r.grad_summary[pl.ds(i, 1), :] * wide(r.share[pl.ds(i, 1), :], width)

        def body(at, k, carry):
            there = pl.ds(pl.multiple_of((ch * ipd + i) * CELLS + k * STRIP, STRIP), STRIP)
            put_at = pl.ds(pl.multiple_of(SIDE + k * STRIP, SIDE), STRIP)
            mask = r.maskf[there, :]
            for q in range(two // LANES):
                g, p = q // n_half, q % n_half
                lanes = slice(q * LANES, (q + 1) * LANES)
                here = slice(p * LANES, (p + 1) * LANES)
                d = (r.dm[at, here] * att[:, lanes] + flat[:, here]) * r.slope2[at, lanes]
                d = mask * lead2[:, lanes] * (d - base2[:, lanes] - r.sp[at, lanes] * slant2[:, lanes])
                r.act2[at, lanes] = d
                before = jnp.where(not_first, pltpu.roll(d, 1, 0), 0.0)
                after = jnp.where(not_last, pltpu.roll(d, STRIP - 1, 0), 0.0)
                for n, value in enumerate((after, d, before)):
                    start = n * width + p * LANES
                    r.dsh[g, i, put_at, start : start + LANES] = value.astype(BF16)
            return carry

        strips(i * CELLS, body, 0)

    loop(ipd, splits_back)

    drain(r.ebuf.at[pl.ds(1, DP - 1)], r.eg_recv.at[0])
    value = r.eg[piece_rows(0), :]
    for d in range(1, DP):
        value = value + r.ebuf[d].astype(F32)
    r.eo[0] = value.astype(et)
    for d in range(1, DP):
        remote(r.eo.at[0], r.eo.at[DP - d], r.eg_send.at[1], r.eg_recv.at[1], across(d)).start()

    def first_back(i, state):
        out = []
        for g in range(2):
            lanes = slice(g * half, (g + 1) * half)
            left = jnp.concatenate(
                [r.dsh[g, i, (2 - k) * SIDE : (2 - k) * SIDE + CELLS, :] for k in range(3)], axis=1
            )
            value = dot(left, r.wt[g]) * r.slope1[image(i), lanes]
            r.dh1[rows_of(ch, i), lanes] = value.astype(BF16)
            out.append((state[g][0] + fold(value), state[g][1] + fold(value * r.red[image(i), lanes])))
        return tuple(out)

    zero_h = jnp.zeros((8, half), F32)
    gd = Gather(2, lambda b, i: r.dh1.at[rows_of(b, i)], lambda b: r.dh1.at[block_rows(b)], ipd)

    def first_back_send(i, state):
        state = first_back(i, state)
        gd.send(i)
        return state

    state = lax.fori_loop(0, ipd // 2, first_back_send, ((zero_h, zero_h), (zero_h, zero_h)))
    state = lax.fori_loop(ipd // 2, ipd, first_back, state)
    for g in range(2):
        r.g6[0, g : g + 1, :] = total(state[g][0])
        r.g6[0, 2 + g : 3 + g, :] = total(state[g][1])
    everyone(r.g6, 5)
    lax.fori_loop(ipd // 2, ipd, lambda i, carry: (gd.send(i), carry)[1], 0)

    def pass_x(i):
        for t in range(1, X):
            gx.from_peer(t, i)

    loop(ipd, pass_x)

    def turn_d(i):
        for g in range(2):
            r.dst[g, :, image(i)] = r.act2[image(i), g * width : (g + 1) * width].T.astype(BF16)

    loop(ipd, turn_d)
    per = CH // 2
    wide3 = 3 * half
    for k in range(3):
        for g in range(2):
            right = r.act[g, :, k * SIDE : k * SIDE + CELLS, :].reshape(own_rows, wide3)
            value = dot(r.dst[g], right)
            if c.split_inside:
                for q in range(per):
                    b = g * per + q
                    r.ss[k, b % 2, b // 2] = value[q * m2 : (q + 1) * m2, :].astype(BF16)
            else:
                r.split_part[g * width : (g + 1) * width, k * wide3 : (k + 1) * wide3] = value
        if c.split_inside:
            remote(r.ss.at[k, 1 - core], r.sin.at[k], r.sg_send.at[0, k], r.sg_recv.at[0, k], mate).start()
    slab = m2 // DP
    Z = DP // 2
    turn, side = dp // 2, dp % 2

    def ring(e):
        return (((turn + e) % Z) * 2 + side, ch)

    other = (dp + 1 - 2 * side, ch)

    def split_cores(k):
        drain(r.sin.at[k], r.sg_recv.at[0, k])
        for t in range(X):
            value = (r.ss[k, core, t].astype(F32) + r.sin[k, t].astype(F32)).astype(BF16)
            value = value.reshape(Z, 2, slab, wide3)
            for p in range(2):
                r.sc[k, p, :, t] = value[:, p]
        remote(r.sc.at[k, 1 - side], r.sp1.at[k], r.sg_send.at[1, k], r.sg_recv.at[1, k], other).start()

    def split_pairs(k):
        drain(r.sp1.at[k], r.sg_recv.at[1, k])
        r.sy[k] = (r.sc[k, side].astype(F32) + r.sp1[k].astype(F32)).astype(BF16)
        for e in range(1, Z):
            remote(
                r.sy.at[k, (turn + e) % Z], r.sz.at[k, Z - e], r.sg_send.at[2, k], r.sg_recv.at[2, k], ring(e)
            ).start()

    def split_chips(k):
        drain(r.sz.at[k, pl.ds(1, Z - 1)], r.sg_recv.at[2, k])
        for t in range(X):
            there = (chip + t) % X
            value = r.sy[k, turn, there].astype(F32)
            for e in range(1, Z):
                value = value + r.sz[k, e, there].astype(F32)
            r.sx[k, t] = value.astype(BF16)
            if t:
                remote(r.sx.at[k, t], r.sxin.at[k, X - t], r.sg_send.at[3, k], r.sg_recv.at[3, k], peer(t)).start()

    def split_out(k):
        drain(r.sxin.at[k, pl.ds(1, X - 1)], r.sg_recv.at[3, k])
        value = r.sx[k, 0].astype(F32)
        for t in range(1, X):
            value = value + r.sxin[k, t].astype(F32)
        r.so[k, 0] = value.astype(BF16)
        for d in range(1, DP):
            remote(r.so.at[k, 0], r.so.at[k, DP - d], r.sg_send.at[4, k], r.sg_recv.at[4, k], across(d)).start()

    def split_step(step, k):
        if c.split_inside:
            step(k)

    for k in range(3):
        split_step(split_cores, k)
    everyone_wait(r.g6, 5)
    sums = jnp.sum(r.g6[...], axis=0)
    shift_grad, gain_grad = get(sums, 0, width), get(sums, 2, width)
    lead1, base1, slant1 = gain1 * scale1, shift_grad * inverse, gain_grad * inverse

    r.rg[...] = jnp.zeros((cw, width), F32)

    def from_x(i):
        gx.from_mate(i)
        for t in range(1, X):
            gx.from_pass(t, i)

    loop(ipd, from_x)
    gx.done()

    def reduced_back(b, i):
        def body(at, k, carry):
            mask = wide(r.maskf[at, :], width)
            d = mask * lead1 * (r.dh1[at, :].astype(F32) - base1 - r.xh1[at, :].astype(F32) * slant1)
            r.xh1[at, :] = d.astype(BF16)
            return carry

        strips((b * ipd + i) * CELLS, body, 0)
        r.rg[...] += dot(r.xt[b * ipd + i], r.xh1[rows_of(b, i), :])

    def input_back(b, i):
        at = rows_of(b, i)
        r.xv[at, :] = (r.dpre[at, :] + dot(r.xh1[at, :], r.wrt[...])).astype(BF16)
        pltpu.make_async_copy(r.xv.at[at], r.inputs_grad.at[at], r.store.at[1]).start()

    loop(ipd, lambda i: reduced_back(ch, i))

    def from_mate(i):
        gd.from_mate(i)
        reduced_back(block_of(0, False), i)

    loop(ipd, from_mate)
    split_step(split_pairs, 0)
    for t in range(1, X):

        def from_peer(i):
            gd.from_peer(t, i)
            reduced_back(block_of(t, True), i)

        loop(ipd, from_peer)
    split_step(split_pairs, 1)
    for t in range(1, X):

        def from_pass(i):
            gd.from_pass(t, i)
            reduced_back(block_of(t, False), i)

        loop(ipd, from_pass)

    if c.reduce_inside:
        r.rs[...] = r.rg[...].T.astype(r.rs.dtype)
        for d in range(1, DP):
            remote(r.rs.at[piece_rows(d)], r.rbuf.at[DP - d], r.rg_send.at[0], r.rg_recv.at[0], across(d)).start()
    else:
        r.reduce_part[...] = r.rg[...].T
    split_step(split_pairs, 2)
    split_step(split_chips, 0)
    loop(ipd, lambda i: input_back(ch, i))
    split_step(split_chips, 1)
    loop(ipd, lambda i: input_back(block_of(0, False), i))
    split_step(split_out, 0)
    split_step(split_chips, 2)
    if c.reduce_inside:
        groups = DP // CH
        goal = dp // groups
        drain(r.rbuf.at[pl.ds(1, DP - 1)], r.rg_recv.at[0])
        value = r.rs[piece_rows(0), :].astype(F32)
        for d in range(1, DP):
            value = value + r.rbuf[d].astype(F32)
        r.rsum[...] = value.astype(r.rsum.dtype)
        slot = r.rall.at[dp % groups, ch]
        for d in range(1, DP):
            remote(r.rsum, slot, r.rg_send.at[1], r.rg_recv.at[1], ((dp + d) % DP, goal)).start()

        @pl.when(goal == ch)
        def _():
            pltpu.make_async_copy(r.rsum, slot, r.rg_recv.at[1]).start()

        @pl.when(goal != ch)
        def _():
            remote(r.rsum, slot, r.rg_send.at[2], r.rg_recv.at[1], (dp, goal)).start()

    split_step(split_out, 1)
    for t in range(1, X):
        loop(ipd, lambda i: input_back(block_of(t, True), i))
    split_step(split_out, 2)
    for t in range(1, X):
        loop(ipd, lambda i: input_back(block_of(t, False), i))
    r.second_gain_grad[...] = exact_nt(gain_grad2, pick2)
    r.second_shift_grad[...] = exact_nt(shift_grad2, pick2)
    r.first_gain_grad[...] = exact_nt(gain_grad, pick1)
    r.first_shift_grad[...] = exact_nt(shift_grad, pick1)
    r.gate_gain_grad[...] = exact_nt(gate_gain_all, pickg)
    r.gate_shift_grad[...] = exact_nt(gate_shift_all, pickg)

    def gate_grads(n, state):
        at = gate_block(n)
        sum_lo, sum_hi = lower_upper(r.g3, n)
        grad_lo, grad_hi = lower_upper(r.g4, n)
        picked = exact_nt(r.grad_down[at, :], pickg)
        down = jnp.concatenate([exact_tn(picked, sum_lo), exact_tn(picked, sum_hi)], axis=1)
        squeezed = r.squeezed[at, :]
        up = jnp.concatenate([exact_tn(squeezed, grad_lo), exact_tn(squeezed, grad_hi)], axis=1)
        bias = jnp.concatenate([total(grad_lo), total(grad_hi)], axis=1)
        return state[0] + down, state[1] + up, state[2] + bias

    down, up, bias = lax.fori_loop(
        0, gate_blocks, gate_grads,
        (jnp.zeros((mg, width), F32), jnp.zeros((inner, width), F32), jnp.zeros((1, width), F32)),
    )
    r.down_grad[...] = down
    r.up_grad[...] = exact_nt(jnp.concatenate([up, -up], axis=1), pick2)
    r.bias_grad[...] = exact_nt(jnp.concatenate([bias, -bias], axis=1), pick2)

    drain(r.eo.at[pl.ds(1, DP - 1)], r.eg_recv.at[1])
    for d in range(DP):
        r.expand_grad[piece_rows(d), :] = r.eo[d].astype(F32)
    if c.reduce_inside:
        drain(r.rall, r.rg_recv.at[1])
        for s in range(groups):
            for q in range(CH):
                r.reduce_grad[s * piece : (s + 1) * piece, q * cw : (q + 1) * cw] = r.rall[s, q].astype(F32)
    if c.split_inside:
        for k in range(3):
            drain(r.so.at[k, pl.ds(1, DP - 1)], r.sg_recv.at[4, k])
            for p in range(3):
                at = slice(p * half, (p + 1) * half)
                block = jnp.concatenate(
                    [r.so[k, (d - dp + DP) % DP, :, at].astype(F32) for d in range(DP)], axis=0
                )
                r.split_grad[3 * k + p] = block.T

    for k, buf in enumerate((r.g1, r.g2, r.g3, r.g4, r.g5, r.g6)):
        everyone_done(buf, k)
    column_done(r.c1, 0)
    row_done(r.r1, 0)
    row_done(r.r4, 2)
    column_done(r.c4, 3)
    column_done(r.c2, 1)
    rs2.done()
    for gather in (gm, gd) + shares:
        gather.done()
    drain(r.pbuf.at[pl.ds(1, CH - 1)], r.par_send.at[0])
    drain(r.ebuf.at[pl.ds(1, DP - 1)], r.eg_send.at[0])
    drain(r.ebuf.at[pl.ds(1, DP - 1)], r.eg_send.at[1])
    if c.reduce_inside:
        drain(r.rbuf.at[pl.ds(1, DP - 1)], r.rg_send.at[0])
        drain(r.rbuf.at[pl.ds(1, DP - 1)], r.rg_send.at[1])

        @pl.when(goal != ch)
        def _():
            drain(r.rsum, r.rg_send.at[2])

    if c.split_inside:
        for k in range(3):
            drain(r.sin.at[k], r.sg_send.at[0, k])
            drain(r.sp1.at[k], r.sg_send.at[1, k])
            drain(r.sz.at[k, pl.ds(1, Z - 1)], r.sg_send.at[2, k])
            drain(r.sxin.at[k, pl.ds(1, X - 1)], r.sg_send.at[3, k])
            drain(r.so.at[k, pl.ds(1, DP - 1)], r.sg_send.at[4, k])
    drain(r.cv, r.store.at[0])
    drain(r.xv, r.store.at[1])


def hand_over(*refs):
    count = (len(refs) - 1) // 3
    sources, results, places, sems = refs[:count], refs[count : 2 * count], refs[2 * count : -1], refs[-1]
    copies = []
    for source, result, place in zip(sources, results, places):
        rows = source.shape[0]
        parts = 2 if rows >= 1024 else 1
        for p in range(parts):
            at = pl.ds(p * (rows // parts), rows // parts)
            k = len(copies)
            inward = pltpu.make_async_copy(source.at[at], place.at[at], sems.at[k, 0])
            copies.append((inward, pltpu.make_async_copy(place.at[at], result.at[at], sems.at[k, 1])))
            inward.start()
    for inward, outward in copies:
        inward.wait()
        outward.start()
    for inward, outward in copies:
        outward.wait()


ARGS = (
    "inputs", "resolution", "reduce_weight", "first_gain", "first_shift", "split_weight", "second_gain",
    "second_shift", "gate_down", "gate_gain", "gate_shift", "gate_up", "gate_bias", "expand_weight",
    "third_gain", "third_shift", "cotangent",
)


def per_device(*arrays):
    a = dict(zip(ARGS, arrays))
    c = types.SimpleNamespace()
    c.DP, c.CH = lax.axis_size("dp"), lax.axis_size("chan")
    c.X, c.D = c.CH // 2, c.DP * c.CH
    c.images = a["resolution"].shape[0]
    c.ipd = c.images // c.CH
    rows, c.cw = a["inputs"].shape
    c.width = a["reduce_weight"].shape[1]
    c.inner = a["gate_down"].shape[1]
    c.m1, c.m2, c.mg = c.width // c.CH, 2 * c.width // c.CH, c.inner // c.CH
    half, two = c.width // 2, 2 * c.width
    taps = 9 * half
    piece = c.width // c.DP
    piece_type = BF16 if piece % 16 == 0 else F32
    c.reduce_inside = c.DP % c.CH == 0 and piece % 8 == 0
    c.share = taps % (16 * c.DP) == 0 and c.width % (16 * c.DP) == 0
    c.split_inside = c.m2 % (16 * c.DP) == 0 and c.DP % 2 == 0 and c.DP > 2
    own = c.ipd * CELLS
    DP, CH, X, D, ipd, cw, width = c.DP, c.CH, c.X, c.D, c.ipd, c.cw, c.width
    for name in ARGS:
        if a[name].ndim == 1 and name != "resolution":
            a[name] = a[name].reshape(1, -1)
    a["split_weight"] = a["split_weight"].reshape(taps, c.m2)
    sds = jax.ShapeDtypeStruct
    outs = dict(
        block_out=sds((rows, cw), BF16),
        inputs_grad=sds((rows, cw), BF16),
        first_gain_grad=sds((1, c.m1), F32),
        first_shift_grad=sds((1, c.m1), F32),
        second_gain_grad=sds((1, c.m2), F32),
        second_shift_grad=sds((1, c.m2), F32),
        down_grad=sds((c.mg, width), F32),
        gate_gain_grad=sds((1, c.mg), F32),
        gate_shift_grad=sds((1, c.mg), F32),
        up_grad=sds((c.inner, c.m2), F32),
        bias_grad=sds((1, c.m2), F32),
        expand_grad=sds((width, cw), F32),
        third_gain_grad=sds((1, cw), F32),
        third_shift_grad=sds((1, cw), F32),
    )
    if c.reduce_inside:
        outs["reduce_grad"] = sds((c.m1, CH * cw), F32)
    else:
        outs["reduce_part"] = sds((width, cw), F32)
    if c.split_inside:
        outs["split_grad"] = sds((9, half, c.m2), F32)
    else:
        outs["split_part"] = sds((two, taps), F32)
    V = pltpu.VMEM
    dma = lambda *shape: pltpu.SemaphoreType.DMA(shape)
    scratch = dict(
        xv=V((rows, cw), BF16), cv=V((rows, cw), BF16), wr=V((cw, width), BF16), wrt=V((width, cw), BF16),
        wet=V((cw, width), BF16), xt=V((c.images, cw, CELLS), BF16), mt=V((c.images, width, CELLS), BF16),
        maskf=V((rows, LANES), F32), area=V((c.images, LANES), F32), maskb=V((rows, LANES), BF16), pbuf=V((CH, 8, two), F32),
        red=V((own, width), F32), slope1=V((own, width), F32), xh1=V((rows, width), BF16),
        act=V((2, ipd, TALL, 3 * half), BF16), dsh=V((2, ipd, TALL, 3 * width), BF16),
        wg=V((CH, taps, c.m2), BF16), wx=V((CH, width, cw), BF16), wf=V((2, taps, width), BF16), wt=V((2, 9 * width, half), BF16),
        sp=V((own, two), F32), slope2=V((own, two), F32), act2=V((own, two), F32), share=V((8, LANES), F32),
        gate_x=V((D * 8, LANES), F32), squeezed=V((D * 8, LANES), F32), gate_slope=V((D * 8, LANES), F32),
        grad_down=V((D * 8, LANES), F32), grad_summary=V((8, width), F32), att=V((8, two), F32),
        merged=V((rows, width), BF16), ex=V((rows, cw), F32), acc=V((16, cw), F32),
        dpre=V((rows, cw), F32), de=V((rows, cw), BF16), dm=V((own, width), F32), dh1=V((rows, width), BF16),

        dst=V((2, width, own), BF16),
        eg=V((width, cw), F32), es=V((width, cw), piece_type), ebuf=V((DP, piece, cw), piece_type),
        eo=V((DP, piece, cw), piece_type), rg=V((cw, width), F32),
        all_send=dma(6), all_recv=dma(6), col_send=dma(4), col_recv=dma(4), row_send=dma(3), row_recv=dma(3),
        rs_core_send=dma(2), rs_core_recv=dma(2, X, ipd), rs_chip_send=dma(2), rs_chip_recv=dma(2, X, ipd),
        ag_core_send=dma(3), ag_core_recv=dma(3, ipd), ag_chip_send=dma(3, X), ag_chip_recv=dma(3, X, ipd),
        ag_pass_send=dma(3, X), ag_pass_recv=dma(3, X, ipd), sh_core_send=dma(2), sh_core_recv=dma(2),
        sh_chip_send=dma(2, X), sh_chip_recv=dma(2, X), sh_col_send=dma(2, X), sh_col_recv=dma(2, X, DP),
        sh_pass_send=dma(2, X), sh_pass_recv=dma(2, X), par_send=dma(1), par_recv=dma(CH),
        eg_send=dma(2), eg_recv=dma(2), rg_send=dma(3), rg_recv=dma(2), sg_send=dma(5, 3), sg_recv=dma(5, 3),
        load=dma(2 + 2 * X), store=dma(2),
    )
    for name, count in (
        ("stage", X), ("inward", X), ("outward", X - 1), ("landed", X - 1), ("inward2", X), ("landed2", X - 1)
    ):
        scratch[name] = V((count, ipd, CELLS, width), BF16)
    for k in range(1, 5):
        scratch[f"g{k}"] = V((D, 8, LANES), F32)
    scratch["r4"] = V((CH, 8, LANES), F32)
    scratch["c4"] = V((DP, 8, LANES), F32)
    scratch["g5"] = V((D, 16 * width // LANES, LANES), BF16)
    scratch["told"] = V((16, LANES), F32)
    scratch["slopes"] = V((16 * width // LANES, LANES), F32)
    scratch["sums3"] = V((CH, 4, LANES), F32)
    scratch["c1"] = V((DP, 4, LANES), F32)
    scratch["r1"] = V((CH, 4, LANES), F32)
    scratch["c2"] = V((DP, 4, LANES), F32)
    scratch["g6"] = V((D, 4, LANES), F32)
    if c.reduce_inside:
        scratch.update(
            rs=V((width, cw), piece_type), rbuf=V((DP, piece, cw), piece_type), rsum=V((piece, cw), piece_type),
            rall=V((DP // CH, CH, piece, cw), piece_type),
        )
    if c.split_inside:
        slab = c.m2 // DP
        scratch.update(
            ss=V((3, 2, X, c.m2, 3 * half), BF16), sin=V((3, X, c.m2, 3 * half), BF16),
            sc=V((3, 2, c.DP // 2, X, slab, 3 * half), BF16), sp1=V((3, c.DP // 2, X, slab, 3 * half), BF16),
            sy=V((3, c.DP // 2, X, slab, 3 * half), BF16), sz=V((3, c.DP // 2, X, slab, 3 * half), BF16),
            sx=V((3, X, slab, 3 * half), BF16), sxin=V((3, X, slab, 3 * half), BF16),
            so=V((3, c.DP, slab, 3 * half), BF16),
        )
    anywhere = pl.BlockSpec(memory_space=pl.ANY)
    vmem = pl.BlockSpec(memory_space=pltpu.VMEM)
    spec = dict(
        inputs=anywhere, cotangent=anywhere, reduce_weight=anywhere, block_out=anywhere, inputs_grad=anywhere,
        resolution=pl.BlockSpec(memory_space=pltpu.SMEM),
    )
    names = tuple(ARGS) + tuple(outs) + tuple(scratch)
    results = pl.pallas_call(
        functools.partial(kernel, c, names),
        out_shape=tuple(outs.values()),
        in_specs=[spec.get(name, vmem) for name in ARGS],
        out_specs=tuple(spec.get(name, vmem) for name in outs),
        scratch_shapes=list(scratch.values()),
        compiler_params=pltpu.CompilerParams(
            collective_id=0, has_side_effects=True, vmem_limit_bytes=62 * 2**20
        ),
        name="block",
    )(*[a[name] for name in ARGS])
    results = pl.pallas_call(
        hand_over,
        out_shape=tuple(outs.values()),
        in_specs=[anywhere] * len(outs),
        out_specs=tuple(anywhere for _ in outs),
        scratch_shapes=[V(v.shape, v.dtype) for v in outs.values()] + [dma(4 * len(outs), 2)],
        compiler_params=pltpu.CompilerParams(vmem_limit_bytes=62 * 2**20),
        name="results",
    )(*results)
    o = dict(zip(outs, results))
    if not c.reduce_inside:
        place = lax.axis_index("chan")
        part = lax.psum(o["reduce_part"], "dp")
        part = lax.all_gather(part, "chan", axis=1, tiled=True)
        o["reduce_grad"] = lax.dynamic_slice_in_dim(part, place * c.m1, c.m1, 0)
    if not c.split_inside:
        place = lax.axis_index("chan")
        part = lax.psum(o["split_part"], ("dp", "chan"))
        part = lax.dynamic_slice_in_dim(part, place * c.m2, c.m2, 0)
        o["split_grad"] = part.T.reshape(9, half, c.m2)
    flat = lambda name: o[name].reshape(-1)
    return (
        o["block_out"], o["inputs_grad"], o["reduce_grad"].T, flat("first_gain_grad"), flat("first_shift_grad"),
        o["split_grad"], flat("second_gain_grad"), flat("second_shift_grad"), o["down_grad"].T,
        flat("gate_gain_grad"), flat("gate_shift_grad"), o["up_grad"], flat("bias_grad"), o["expand_grad"],
        flat("third_gain_grad"), flat("third_shift_grad"),
    )


def solution(mesh):
    placed = (
        P("dp", "chan"), P("dp"), P(), P("chan"), P("chan"), P(None, None, "chan"), P("chan"), P("chan"),
        P(), P(), P(), P(), P(), P(None, "chan"), P("chan"), P("chan"), P("dp", "chan"),
    )
    return jax.shard_map(
        per_device,
        mesh=mesh,
        in_specs=placed,
        out_specs=(
            P("dp", "chan"), P("dp", "chan"), P(None, "chan"), P("chan"), P("chan"), P(None, None, "chan"),
            P("chan"), P("chan"), P(None, "chan"), P("chan"), P("chan"), P(None, "chan"), P("chan"),
            P(None, "chan"), P("chan"), P("chan"),
        ),
        check_vma=False,
    )
```

```python
import functools
import types

import jax
import jax.numpy as jnp
from jax import lax
from jax.experimental import pallas as pl
from jax.experimental.pallas import tpu as pltpu
from jax.sharding import PartitionSpec as P

SIDE = 16
CELLS = SIDE * SIDE
TALL = CELLS + 2 * SIDE
LANES = 128
EPS = 1e-05
HIGHEST = lax.Precision.HIGHEST
F32 = jnp.float32
BF16 = jnp.bfloat16
MESH = pl.DeviceIdType.MESH
STRIP = 32


def wide(mask, width):
    return mask if width == LANES else jnp.concatenate([mask] * (width // LANES), axis=1)


def fold(values):
    return jnp.sum(values.reshape(values.shape[0] // 8, 8, values.shape[1]), axis=0)


def total(values):
    return jnp.sum(values, axis=0, keepdims=True)


def sigmoid(values):
    return 0.5 * jnp.tanh(0.5 * values) + 0.5


def dot(left, right):
    return jnp.dot(left, right, preferred_element_type=F32)


def exact(left, right):
    return jnp.dot(left, right, precision=HIGHEST, preferred_element_type=F32)


def exact_nt(left, right):
    return lax.dot_general(
        left, right, (((1,), (1,)), ((), ())), precision=HIGHEST, preferred_element_type=F32
    )


def exact_tn(left, right):
    return lax.dot_general(
        left, right, (((0,), (0,)), ((), ())), precision=HIGHEST, preferred_element_type=F32
    )


def flip(values):
    return values.astype(F32).T.astype(values.dtype)


def put(ref, row, vector):
    for part in range(vector.shape[1] // LANES):
        ref[0, row + part : row + part + 1, :] = vector[:, part * LANES : (part + 1) * LANES]


def get(block, row, width):
    parts = [block[row + q : row + q + 1, :] for q in range(width // LANES)]
    return parts[0] if len(parts) == 1 else jnp.concatenate(parts, axis=1)


def kernel(c, names, *refs):
    r = types.SimpleNamespace(**dict(zip(names, refs)))
    DP, CH, X, D, ipd, images = c.DP, c.CH, c.X, c.D, c.ipd, c.images
    width, cw, inner, m1, m2, mg = c.width, c.cw, c.inner, c.m1, c.m2, c.mg
    half, two = width // 2, 2 * width
    own_rows = ipd * CELLS
    taps = 9 * half
    dp = lax.axis_index("dp")
    ch = lax.axis_index("chan")
    core = ch % 2
    chip = ch // 2
    mate = (dp, ch + 1 - 2 * core)
    f0 = ((0, 0), (0, 0))

    def remote(src, dst, send, recv, device):
        return pltpu.make_async_remote_copy(
            src_ref=src, dst_ref=dst, send_sem=send, recv_sem=recv, device_id=device, device_id_type=MESH
        )

    def drain(ref, sem):
        pltpu.make_async_copy(ref, ref, sem).wait()

    def loop(count, body):
        def step(i, carry):
            body(i)
            return carry

        lax.fori_loop(0, count, step, 0)

    def peer(t):
        return (dp, ((chip + t) % X) * 2 + core)

    def across(d):
        return ((dp + d) % DP, ch)

    def block_of(t, same):
        return ((chip + t) % X) * 2 + (core if same else 1 - core)

    def rows_of(b, i):
        return pl.ds(pl.multiple_of((b * ipd + i) * CELLS, CELLS), CELLS)

    def block_rows(b):
        return pl.ds(pl.multiple_of(b * own_rows, own_rows), own_rows)

    def image(i):
        return pl.ds(pl.multiple_of(i * CELLS, CELLS), CELLS)

    def strips(base, body, carry, size=STRIP):
        def step(k, state):
            return body(pl.ds(pl.multiple_of(base + k * size, size), size), k, state)

        return lax.fori_loop(0, CELLS // size, step, carry)

    def everyone(buf, k, message=None):
        message = buf.at[0] if message is None else message

        def one(j, carry):
            d, q = j // CH, j % CH
            slot = ((DP - d) % DP) * CH + (CH - q) % CH
            remote(buf.at[0], buf.at[slot], r.all_send.at[k], r.all_recv.at[k], ((dp + d) % DP, (ch + q) % CH)).start()
            return carry

        lax.fori_loop(1, D, one, 0)

    def everyone_wait(buf, k):
        drain(buf.at[pl.ds(1, D - 1)], r.all_recv.at[k])

    def everyone_wait_on(buf, sem):
        drain(buf.at[pl.ds(1, D - 1)], sem)

    def everyone_done(buf, k):
        drain(buf.at[pl.ds(1, D - 1)], r.all_send.at[k])

    def column(buf, k):
        for d in range(1, DP):
            remote(buf.at[0], buf.at[DP - d], r.col_send.at[k], r.col_recv.at[k], across(d)).start()

    def row(buf, k, source=None):
        for q in range(1, CH):
            src = buf.at[0] if source is None else source.at[(ch + q) % CH]
            remote(src, buf.at[CH - q], r.row_send.at[k], r.row_recv.at[k], (dp, (ch + q) % CH)).start()

    def row_sum(buf, k, column_buf):
        drain(buf.at[pl.ds(1, CH - 1)], r.row_recv.at[k])
        column_buf[0] = jnp.sum(buf[...], axis=0)

    def row_done(buf, k):
        drain(buf.at[pl.ds(1, CH - 1)], r.row_send.at[k])

    def column_wait(buf, k):
        drain(buf.at[pl.ds(1, DP - 1)], r.col_recv.at[k])

    def column_done(buf, k):
        drain(buf.at[pl.ds(1, DP - 1)], r.col_send.at[k])

    class Scatter:
        def __init__(self, k, stage, inward, outward, landed, keep):
            self.k, self.stage, self.inward = k, stage, inward
            self.outward, self.landed, self.keep = outward, landed, keep

        def compute_mate(self, t, part):
            def body(i):
                self.stage[t, i] = part(block_of(t, False), i).astype(BF16)

            loop(ipd, body)

        def send_mate(self, t):
            def body(i):
                remote(
                    self.stage.at[t, i], self.inward.at[t, i],
                    r.rs_core_send.at[self.k], r.rs_core_recv.at[self.k, t, i], mate,
                ).start()

            loop(ipd, body)

        def mate_one(self, t, i, part):
            self.stage[t, i] = part(block_of(t, False), i).astype(BF16)
            remote(
                self.stage.at[t, i], self.inward.at[t, i],
                r.rs_core_send.at[self.k], r.rs_core_recv.at[self.k, t, i], mate,
            ).start()

        def to_mate(self, t, part):
            loop(ipd, lambda i: self.mate_one(t, i, part))

        def peer_one(self, t, i, part):
            value = part(block_of(t, True), i)
            drain(self.inward.at[t, i], r.rs_core_recv.at[self.k, t, i])
            self.outward[t - 1, i] = (value + self.inward[t, i].astype(F32)).astype(BF16)
            remote(
                self.outward.at[t - 1, i], self.landed.at[X - t - 1, i],
                r.rs_chip_send.at[self.k], r.rs_chip_recv.at[self.k, X - t, i], peer(t),
            ).start()

        def to_peer(self, t, part):
            loop(ipd, lambda i: self.peer_one(t, i, part))

        def both(self, t, part):
            self.mate_one(t, 0, part)

            def body(i, carry):
                self.mate_one(t, i, part)
                self.peer_one(t, i - 1, part)
                return carry

            lax.fori_loop(1, ipd, body, 0)
            self.peer_one(t, ipd - 1, part)

        def own(self, part):
            def body(i):
                value = part(ch, i)
                drain(self.inward.at[0, i], r.rs_core_recv.at[self.k, 0, i])
                self.keep[image(i), :] = value + self.inward[0, i].astype(F32)

            loop(ipd, body)

        def arrive(self, i):
            for t in range(1, X):
                drain(self.landed.at[t - 1, i], r.rs_chip_recv.at[self.k, t, i])

        def extra(self, i, at, lanes):
            value = self.landed[0, i, at, lanes].astype(F32)
            for t in range(2, X):
                value = value + self.landed[t - 1, i, at, lanes].astype(F32)
            return value

        def done(self, stage=True):
            if stage:
                drain(self.stage, r.rs_core_send.at[self.k])
            drain(self.outward, r.rs_chip_send.at[self.k])

    class Gather:
        def __init__(self, k, place, whole, pieces):
            self.k, self.place, self.whole, self.pieces = k, place, whole, pieces

        def send(self, i):
            src = self.place(ch, i)
            remote(src, src, r.ag_core_send.at[self.k], r.ag_core_recv.at[self.k, i], mate).start()
            for t in range(1, X):
                remote(src, src, r.ag_chip_send.at[self.k, t], r.ag_chip_recv.at[self.k, X - t, i], peer(t)).start()

        def from_mate(self, i):
            drain(self.place(block_of(0, False), i), r.ag_core_recv.at[self.k, i])

        def from_peer(self, t, i):
            ref = self.place(block_of(t, True), i)
            drain(ref, r.ag_chip_recv.at[self.k, t, i])
            remote(ref, ref, r.ag_pass_send.at[self.k, t], r.ag_pass_recv.at[self.k, t, i], mate).start()

        def from_pass(self, t, i):
            drain(self.place(block_of(t, False), i), r.ag_pass_recv.at[self.k, t, i])

        def done(self):
            drain(self.whole(ch), r.ag_core_send.at[self.k])
            for t in range(1, X):
                drain(self.whole(ch), r.ag_chip_send.at[self.k, t])
                drain(self.whole(block_of(t, True)), r.ag_pass_send.at[self.k, t])

    class Share:
        def __init__(self, k, blocks, rows):
            self.k, self.blocks, self.piece = k, blocks, rows // DP

        def part(self, b, d):
            at = pl.ds(pl.multiple_of(((dp + d) % DP) * self.piece, self.piece), self.piece)
            return self.blocks.at[b, at]

        def send(self):
            own = self.blocks.at[ch]
            remote(own, own, r.sh_core_send.at[self.k], r.sh_core_recv.at[self.k], mate).start()
            for t in range(1, X):
                src = self.part(ch, 0) if c.share else own
                remote(src, src, r.sh_chip_send.at[self.k, t], r.sh_chip_recv.at[self.k, X - t], peer(t)).start()

        def spread(self):
            for t in range(1, X):
                b = block_of(t, True)
                src = self.part(b, 0) if c.share else self.blocks.at[b]
                drain(src, r.sh_chip_recv.at[self.k, t])
                if c.share:
                    for d in range(1, DP):
                        remote(src, src, r.sh_col_send.at[self.k, t], r.sh_col_recv.at[self.k, t, DP - d], across(d)).start()

        def hand(self):
            for t in range(1, X):
                b = block_of(t, True)
                if c.share:
                    for d in range(1, DP):
                        drain(self.part(b, d), r.sh_col_recv.at[self.k, t, d])
                whole = self.blocks.at[b]
                remote(whole, whole, r.sh_pass_send.at[self.k, t], r.sh_pass_recv.at[self.k, t], mate).start()

        def take(self):
            drain(self.blocks.at[block_of(0, False)], r.sh_core_recv.at[self.k])
            for t in range(1, X):
                drain(self.blocks.at[block_of(t, False)], r.sh_pass_recv.at[self.k, t])

        def done(self):
            own = self.blocks.at[ch]
            drain(own, r.sh_core_send.at[self.k])
            for t in range(1, X):
                whole = self.blocks.at[block_of(t, True)]
                drain(self.part(ch, 0) if c.share else own, r.sh_chip_send.at[self.k, t])
                drain(whole, r.sh_pass_send.at[self.k, t])
                if c.share:
                    for d in range(1, DP):
                        drain(self.part(block_of(t, True), 0), r.sh_col_send.at[self.k, t])

    barrier = pltpu.get_barrier_semaphore()

    def greet(j, carry):
        pl.semaphore_signal(
            barrier, inc=1, device_id=((dp + j // CH) % DP, (ch + j % CH) % CH), device_id_type=MESH
        )
        return carry

    lax.fori_loop(1, D, greet, 0)

    load_w = pltpu.make_async_copy(
        r.reduce_weight.at[pl.ds(pl.multiple_of(ch * cw, cw), cw)], r.wr, r.load.at[0]
    )
    load_w.start()
    order = []
    for t in list(range(1, X)) + [0]:
        order += [block_of(t, False), block_of(t, True)]
    loads = []
    for k, b in enumerate(order):
        at = pl.ds(pl.multiple_of(b * own_rows, own_rows), own_rows)
        loads.append(pltpu.make_async_copy(r.inputs.at[at], r.xv.at[at], r.load.at[2 + k]))
        loads[-1].start()
    load_c = pltpu.make_async_copy(r.cotangent, r.cv, r.load.at[1])
    load_c.start()

    row_at = lax.broadcasted_iota(jnp.int32, (CELLS, LANES), 0)
    spot_r = lax.shift_right_logical(row_at, 4)
    spot_c = lax.bitwise_and(row_at, 15)

    def make_mask(j):
        side = 12 + 2 * r.resolution[j]
        mask = jnp.where(jnp.logical_and(spot_r < side, spot_c < side), 1.0, 0.0)
        r.area[pl.ds(j, 1), :] = jnp.full((1, LANES), side * side, jnp.int32).astype(F32)
        r.maskf[image(j), :] = mask

    loop(images, make_mask)

    def part_reduce(b, i):
        at = rows_of(b, i)
        x = r.xv[at, :] * wide(r.maskf[at, :].astype(BF16), cw)
        r.xv[at, :] = x
        return dot(x, r.wr[...])

    r.wg[ch] = r.split_weight[...]
    r.wx[ch] = r.expand_weight[...]
    shares = (Share(0, r.wg, taps), Share(1, r.wx, width))

    load_w.wait()
    rs1 = Scatter(0, r.stage, r.inward, r.outward, r.landed, r.red)
    loads[0].wait()
    rs1.compute_mate(1, part_reduce)
    pl.semaphore_wait(barrier, D - 1)
    rs1.send_mate(1)
    for share in shares:
        share.send()
    for t in range(1, X):
        if t > 1:
            loads[2 * t - 2].wait()
            rs1.to_mate(t, part_reduce)
        loads[2 * t - 1].wait()
        rs1.to_peer(t, part_reduce)
    for share in shares:
        share.spread()
    loads[2 * X - 2].wait()
    rs1.to_mate(0, part_reduce)
    loads[2 * X - 1].wait()
    rs1.own(part_reduce)

    def selector(parts, mine):
        row = lax.broadcasted_iota(jnp.int32, (mine, mine * parts), 0)
        col = lax.broadcasted_iota(jnp.int32, (mine, mine * parts), 1)
        return jnp.where(col == row + ch * mine, 1.0, 0.0)

    pick1 = selector(CH, m1)
    pick2 = selector(CH, m2)
    pickg = selector(CH, mg)
    r.pbuf[0, 0:1, 0:width] = exact(r.first_gain[...], pick1)
    r.pbuf[0, 1:2, 0:width] = exact(r.first_shift[...], pick1)
    r.pbuf[0, 2:3, :] = exact(r.second_gain[...], pick2)
    r.pbuf[0, 3:4, :] = exact(r.second_shift[...], pick2)

    for q in range(1, CH):
        remote(r.pbuf.at[0], r.pbuf.at[CH - q], r.par_send.at[0], r.par_recv.at[CH - q], (dp, (ch + q) % CH)).start()

    r.wrt[...] = flip(r.wr[...])
    r.wet[...] = flip(r.expand_weight[...])

    def turn_x(j):
        r.xt[j] = flip(r.xv[image(j), :])

    loop(images, turn_x)
    for g in range(2):
        for i in range(ipd):
            r.act[g, i, 0:SIDE, :] = jnp.zeros((SIDE, 3 * half), BF16)
            r.act[g, i, CELLS + SIDE : TALL, :] = jnp.zeros((SIDE, 3 * half), BF16)
            r.dsh[g, i, 0:SIDE, :] = jnp.zeros((SIDE, 3 * width), BF16)
            r.dsh[g, i, CELLS + SIDE : TALL, :] = jnp.zeros((SIDE, 3 * width), BF16)

    def finish_reduce(i, state):
        rs1.arrive(i)

        def body(at, k, state):
            first, second = state
            value = r.red[at, :] + rs1.extra(i, pl.ds(pl.multiple_of(k * STRIP, STRIP), STRIP), slice(None))
            r.red[at, :] = value
            return (first + fold(value), second + fold(value * value))

        return strips(i * CELLS, body, state)

    zero8 = jnp.zeros((8, width), F32)
    first, second = lax.fori_loop(0, ipd, finish_reduce, (zero8, zero8))

    pixels = lax.fori_loop(
        0, ipd, lambda i, count: count + r.area[pl.ds(ch * ipd + i, 1), :], jnp.zeros((1, LANES), F32)
    )
    r.g1[0] = jnp.zeros((8, LANES), F32)
    put(r.g1, 0, total(first))
    put(r.g1, width // LANES, total(second))
    r.g1[0, 6:7, :] = pixels
    everyone(r.g1, 0)
    for share in shares:
        share.hand()
    everyone_wait(r.g1, 0)
    sums = jnp.sum(r.g1[...], axis=0)
    count = sums[6:7, 0:1]
    inverse = 1.0 / count
    params = r.pbuf[0]
    for q in range(1, CH):
        drain(r.pbuf.at[q], r.par_recv.at[q])
        params = params + r.pbuf[q]
    gain1, shift1 = params[0:1, 0:width], params[1:2, 0:width]
    gain2, shift2 = params[2:3, :], params[3:4, :]

    def moments(first, second):
        mean = first * inverse
        return mean, lax.rsqrt(second * inverse - mean * mean + EPS)

    mean1, scale1 = moments(get(sums, 0, width), get(sums, width // LANES, width))

    place_x = lambda b, i: r.xh1.at[rows_of(b, i)]
    gx = Gather(0, place_x, lambda b: r.xh1.at[block_rows(b)], ipd)

    strip_c = lax.bitwise_and(lax.broadcasted_iota(jnp.int32, (STRIP, LANES), 0), 15)
    not_first = strip_c != 0
    not_last = strip_c != 15

    def first_act(i):
        def body(at, k, carry):
            there = pl.ds(pl.multiple_of((ch * ipd + i) * CELLS + k * STRIP, STRIP), STRIP)
            put_at = pl.ds(pl.multiple_of(SIDE + k * STRIP, SIDE), STRIP)
            mask = r.maskf[there, :]
            for g in range(2):
                lanes = slice(g * half, (g + 1) * half)
                xh = (r.red[at, lanes] - mean1[:, lanes]) * scale1[:, lanes]
                h = gain1[:, lanes] * xh + shift1[:, lanes]
                s = sigmoid(h)
                y = h * s
                r.red[at, lanes] = xh
                r.xh1[there, lanes] = xh.astype(BF16)
                r.slope1[at, lanes] = mask * (s + y - y * s)
                a = mask * y
                before = jnp.where(not_first, pltpu.roll(a, 1, 0), 0.0)
                after = jnp.where(not_last, pltpu.roll(a, STRIP - 1, 0), 0.0)
                r.act[g, i, put_at, 0:half] = before.astype(BF16)
                r.act[g, i, put_at, half : 2 * half] = a.astype(BF16)
                r.act[g, i, put_at, 2 * half : 3 * half] = after.astype(BF16)
            return carry

        strips(i * CELLS, body, 0)

    loop(ipd, first_act)

    for share in shares:
        share.take()
    for g in range(2):
        for q in range(CH // 2):
            r.wf[g, :, q * m2 : (q + 1) * m2] = r.wg[g * (CH // 2) + q]

    def two_of(n):
        return pl.ds(pl.multiple_of(n * 2 * CELLS, 2 * CELLS), 2 * CELLS)

    def conv(n, state):
        there = pl.ds(pl.multiple_of((ch * ipd + 2 * n) * CELLS, 2 * CELLS), 2 * CELLS)
        out = []
        for g in range(2):
            lanes = slice(g * width, (g + 1) * width)
            left = jnp.concatenate(
                [
                    r.act[g, pl.ds(2 * n, 2), k * SIDE : k * SIDE + CELLS, :].reshape(2 * CELLS, 3 * half)
                    for k in range(3)
                ],
                axis=1,
            )
            value = dot(left, r.wf[g]) * wide(r.maskf[there, :], width)
            r.sp[two_of(n), lanes] = value
            out.append((state[g][0] + fold(value), state[g][1] + fold(value * value)))
        return tuple(out)

    state = lax.fori_loop(0, ipd // 2, conv, ((zero8, zero8), (zero8, zero8)))
    for g in range(2):
        put(r.g2, g * (width // LANES), total(state[g][0]))
        put(r.g2, (2 + g) * (width // LANES), total(state[g][1]))
    everyone(r.g2, 1)
    loop(ipd // 2, gx.send)

    for g in range(2):
        for tap in range(9):
            r.wt[g, tap * width : (tap + 1) * width, :] = flip(r.wf[g, tap * half : (tap + 1) * half, :])

    everyone_wait(r.g2, 1)
    sums = jnp.sum(r.g2[...], axis=0)
    mean2, scale2 = moments(get(sums, 0, two), get(sums, two // LANES, two))

    r.g3[0] = jnp.zeros((8, LANES), F32)

    def second_act(i):
        def body(at, k, state):
            there = pl.ds(pl.multiple_of((ch * ipd + i) * CELLS + k * STRIP, STRIP), STRIP)
            mask = r.maskf[there, :]
            new = []
            for q in range(two // LANES):
                lanes = slice(q * LANES, (q + 1) * LANES)
                xh = (r.sp[at, lanes] - mean2[:, lanes]) * scale2[:, lanes]
                h = gain2[:, lanes] * xh + shift2[:, lanes]
                s = sigmoid(h)
                y = h * s
                r.sp[at, lanes] = xh
                r.slope2[at, lanes] = mask * (s + y - y * s)
                a = mask * y
                r.act2[at, lanes] = a
                new.append(state[q] + fold(a))
            return tuple(new)

        zero = jnp.zeros((8, LANES), F32)
        pooled = strips(i * CELLS, body, (zero,) * (two // LANES))
        share = 1.0 / r.area[pl.ds(ch * ipd + i, 1), :]
        r.share[pl.ds(i, 1), :] = share
        n = width // LANES
        for q in range(n):
            r.g3[0, pl.ds(4 * q + i, 1), :] = total(pooled[q] + pooled[n + q]) * share

    loop(ipd, second_act)
    everyone(r.g3, 2)

    def slope_guess():
        root = 3.0**0.5
        points = []
        for z in (-root, 0.0, root):
            h = shift2 + z * gain2
            s = sigmoid(h)
            points.append(s + h * s - h * s * s)
        low, mid, high = points
        return (low + 4.0 * mid + high) * (1.0 / 6.0), (high - low) * (root / 6.0)

    guess = slope_guess()

    def slope_sums(i):
        share = r.share[pl.ds(i, 1), :]
        zero = jnp.zeros((8, LANES), F32)
        n = width // LANES

        def body(at, k, state):
            new = []
            for q in range(2 * n):
                lanes = slice(q * LANES, (q + 1) * LANES)
                slope = r.slope2[at, lanes]
                new.append((state[q][0] + fold(slope), state[q][1] + fold(slope * r.sp[at, lanes])))
            return tuple(new)

        state = strips(i * CELLS, body, ((zero, zero),) * (2 * n))
        for q in range(2 * n):
            for stat in range(2):
                row_at = (stat * n + q % n) * 8 + 4 * (q // n)
                r.slopes[pl.ds(row_at + i, 1), :] = (
                    total(state[q][stat]) * share - guess[stat][:, q * LANES : (q + 1) * LANES]
                )

    r.slopes[...] = jnp.zeros_like(r.slopes)
    loop(ipd, slope_sums)
    r.g5[0] = r.slopes[...].astype(BF16)

    everyone(r.g5, 4)


    gate_rows = min(D * 8, 2 * LANES)
    gate_blocks = D * 8 // gate_rows
    gate_at = lax.broadcasted_iota(jnp.int32, (gate_rows, LANES), 0)
    valid = lax.bitwise_and(gate_at, 7) < ipd
    every = 1.0 / (D * ipd)

    def gate_block(n):
        return pl.ds(pl.multiple_of(n * gate_rows, gate_rows), gate_rows)

    def lower_upper(buf, n):
        slots = gate_rows // 8
        both = buf[pl.ds(n * slots, slots)].reshape(gate_rows, LANES)
        return jnp.where(valid, both, 0.0), jnp.where(valid, pltpu.roll(both, gate_rows - 4, 0), 0.0)

    def gate_in(n, state):
        sum_lo, sum_hi = lower_upper(r.g3, n)
        pre = exact(sum_lo, r.gate_down[0:LANES, :]) + exact(sum_hi, r.gate_down[LANES:, :])
        r.gate_x[gate_block(n), :] = pre
        return state[0] + total(pre), state[1] + total(pre * pre)

    everyone_wait(r.g3, 2)
    zero1 = jnp.zeros((1, LANES), F32)
    first, second = lax.fori_loop(0, gate_blocks, gate_in, (zero1, zero1))
    gate_mean = first * every
    gate_scale = lax.rsqrt(second * every - gate_mean * gate_mean + EPS)

    def gate_out(n):
        at = gate_block(n)
        x = (r.gate_x[at, :] - gate_mean) * gate_scale
        h = r.gate_gain[...] * x + r.gate_shift[...]
        s = sigmoid(h)
        y = h * s
        r.gate_x[at, :] = x
        r.squeezed[at, :] = y
        r.gate_slope[at, :] = s + y - y * s

    loop(gate_blocks, gate_out)
    logits = exact(r.squeezed[0:8, :], r.gate_up[...]) + r.gate_bias[...]
    top = jnp.maximum(logits[:, :width], logits[:, width:])
    upper = jnp.exp(logits[:, :width] - top)
    lower = jnp.exp(logits[:, width:] - top)
    both = upper + lower
    r.att[:, 0:width] = upper / both
    r.att[:, width:two] = lower / both

    gm = Gather(1, lambda b, i: r.merged.at[rows_of(b, i)], lambda b: r.merged.at[block_rows(b)], ipd)

    def merge(i):
        att = r.att[pl.ds(i, 1), :]

        def body(at, k, carry):
            there = pl.ds(pl.multiple_of((ch * ipd + i) * CELLS + k * STRIP, STRIP), STRIP)
            left = (r.act2[at, 0:width] * att[:, 0:width]).astype(BF16)
            right = (r.act2[at, width:two] * att[:, width:two]).astype(BF16)
            r.merged[there, :] = (left.astype(F32) + right.astype(F32)).astype(BF16)
            return carry

        strips(i * CELLS, body, 0)

    merge(0)
    gm.send(0)
    lax.fori_loop(1, ipd, lambda i, carry: (merge(i), carry)[1], 0)

    def expand_sums(k):
        def body(i, state):
            value = dot(r.merged[rows_of(ch, i), :], r.wx[k])
            return (state[0] + fold(value), state[1] + fold(value * value))

        first, second = lax.fori_loop(0, ipd, body, (zero_c, zero_c))
        put(r.sums3.at[pl.ds(k, 1)], 0, total(first))
        put(r.sums3.at[pl.ds(k, 1)], cw // LANES, total(second))

    zero_c = jnp.zeros((8, cw), F32)
    loop(CH, expand_sums)
    r.r1[0] = r.sums3[ch]
    row(r.r1, 1, r.sums3)
    lax.fori_loop(1, ipd, lambda i, carry: (gm.send(i), carry)[1], 0)
    load_c.wait()
    r.acc[...] = jnp.zeros((16, cw), F32)
    row_sum(r.r1, 1, r.c1)
    column(r.c1, 0)

    for t in range(1, X):
        loop(2, lambda i: gm.from_peer(t, i))
    def turn_own(j):
        r.mt[:, rows_of(ch, j)] = flip(r.merged[rows_of(ch, j), :])

    loop(ipd, turn_own)

    def turn_w(k):
        r.wxt[k] = flip(r.wx[k])

    loop(CH, turn_w)
    column_wait(r.c1, 0)
    sums = jnp.sum(r.c1[...], axis=0)
    mean3, scale3 = moments(get(sums, 0, cw), get(sums, cw // LANES, cw))
    gain3, shift3 = r.third_gain[...], r.third_shift[...]
    lead3 = gain3 * scale3
    lift3 = shift3 - mean3 * lead3
    per3 = cw // LANES
    put(r.r2, 0, lead3 * scale3)
    put(r.r2, per3, lead3)
    put(r.r2, 2 * per3, lead3 * scale3 * mean3)
    row(r.r2, 0)

    def outputs(b, i):
        r.ex[rows_of(b, i), :] = dot(r.merged[rows_of(b, i), :], r.expand_weight[...])

        def body(at, k, state):
            shift, cross = state
            mask = wide(r.maskf[at, :], cw)
            x = r.ex[at, :]
            h = lead3 * x + lift3 + r.xv[at, :].astype(F32)
            s = sigmoid(h)
            y = h * s
            d = r.cv[at, :].astype(F32) * mask * (s + y - y * s)
            r.cv[at, :] = (mask * y).astype(BF16)
            r.dpre[at, :] = d
            r.de[at, :] = (lead3 * d).astype(BF16)
            return (shift + fold(d), cross + fold(d * x))

        shift, cross = strips((b * ipd + i) * CELLS, body, (zero_c, zero_c))
        r.acc[0:8, :] += shift
        r.acc[8:16, :] += cross
        at = rows_of(b, i)
        pltpu.make_async_copy(r.cv.at[at], r.block_out.at[at], r.store.at[0]).start()

    def part_merged(b, i):
        return dot(r.de[rows_of(b, i), :], r.wet[...])

    rs1.done()
    rs2 = Scatter(1, r.stage, r.inward2, r.outward, r.landed2, r.dm)
    for t in range(1, X):

        def far(i, ahead):
            gm.from_pass(t, i)
            outputs(block_of(t, False), i)
            rs2.mate_one(t, i, part_merged)
            outputs(block_of(t, True), i)
            if ahead:
                gm.from_peer(t, i + 2)
            rs2.peer_one(t, i, part_merged)

        loop(ipd - 2, lambda i: far(i, True))
        lax.fori_loop(ipd - 2, ipd, lambda i, carry: (far(i, False), carry)[1], 0)

    def near(i):
        gm.from_mate(i)
        outputs(block_of(0, False), i)
        rs2.mate_one(0, i, part_merged)

    loop(ipd, near)
    loop(ipd, lambda i: outputs(ch, i))
    shift = total(r.acc[0:8, :])
    put(r.c2, 0, shift)
    put(r.c2, cw // LANES, (total(r.acc[8:16, :]) - mean3 * shift) * scale3)
    everyone(r.c2, 6)
    rs2.own(part_merged)

    def turn_other(j):
        b = j // ipd
        b = jnp.where(b < ch, b, b + 1)
        at = b * ipd + j % ipd
        r.mt[:, image(at)] = flip(r.merged[image(at), :])

    loop(images - ipd, turn_other)
    everyone_wait(r.c2, 6)
    drain(r.r2.at[pl.ds(1, CH - 1)], r.row_recv.at[0])
    r.back3[...] = jnp.sum(r.c2[...].reshape(DP, CH, 4, LANES), axis=0)
    sums = r.back3[0]
    shift_grad, gain_grad = get(sums, 0, cw), get(sums, cw // LANES, cw)
    r.third_gain_grad[...] = gain_grad
    r.third_shift_grad[...] = shift_grad
    base3, slant3 = shift_grad * inverse, gain_grad * inverse
    slope3 = lead3 * scale3 * slant3
    flat3 = lead3 * base3 - mean3 * slope3

    r.mix[...] = jnp.zeros((width, width), F32)
    r.offset[...] = jnp.zeros((16, width), F32)

    def mix(q):
        b = (ch + q) % CH
        coefs, part = r.r2[q], r.back3[q]
        base, slant = get(part, 0, cw) * inverse, get(part, per3, cw) * inverse
        slope = get(coefs, 0, cw) * slant
        flat = get(coefs, per3, cw) * base - get(coefs, 2 * per3, cw) * slant
        r.mix[...] += dot((r.wx[b].astype(F32) * slope).astype(BF16), r.wxt[b])
        high = flat.astype(BF16)
        low = (flat - high.astype(F32)).astype(BF16)
        pair = jnp.concatenate([high, low, jnp.zeros((14, cw), BF16)], axis=0)
        r.offset[...] += dot(pair, r.wxt[b])

    loop(CH, mix)
    r.mixb[...] = r.mix[...].astype(BF16)

    offset = total(r.offset[...])
    away = offset + dot(r.merged[block_rows(ch), :], r.mixb[...])
    r.inward[0] = away.astype(BF16).reshape(ipd, CELLS, width)

    r.told[...] = jnp.zeros((16, LANES), F32)

    def finish_merged(i):
        rs2.arrive(i)

        def body(at, k, state):
            here = pl.ds(pl.multiple_of(k * SIDE, SIDE), SIDE)
            there = pl.ds(pl.multiple_of((ch * ipd + i) * CELLS + k * SIDE, SIDE), SIDE)
            away = wide(r.maskf[there, :], width) * r.inward[0, i, here, :].astype(F32)
            value = r.dm[at, :] + rs2.extra(i, here, slice(None)) - away
            r.dm[at, :] = value
            new = [state[0] + fold(value * (r.act2[at, 0:width] - r.act2[at, width:two]))]
            for g in range(2):
                lanes = slice(g * width, (g + 1) * width)
                part = value * r.slope2[at, lanes]
                new += [state[1 + 2 * g] + fold(part), state[2 + 2 * g] + fold(part * r.sp[at, lanes])]
            return tuple(new)

        gap, *parts = strips(i * CELLS, body, (zero8,) * 5, SIDE)
        att = r.att[pl.ds(i, 1), :]
        grad = att[:, 0:width] * att[:, width:two] * total(gap)
        n = width // LANES
        for q in range(n):
            r.told[pl.ds(4 * q + i, 1), :] = grad[:, q * LANES : (q + 1) * LANES]
        for g in range(2):
            for stat in range(2):
                part = total(parts[2 * g + stat]) * att[:, g * width : (g + 1) * width]
                for q in range(n):
                    at = 8 + (2 * stat + g) * n + q
                    r.told[at : at + 1, :] += part[:, q * LANES : (q + 1) * LANES]

    loop(ipd, finish_merged)
    r.r4[0] = r.told[8:16, :]
    row(r.r4, 2)
    r.g4[0] = r.told[0:8, :]
    everyone(r.g4, 3)
    lax.fori_loop(ipd // 2, ipd, lambda i, carry: (gx.send(i), carry)[1], 0)
    row_sum(r.r4, 2, r.c4)
    column(r.c4, 3)

    piece = width // DP
    et = r.es.dtype
    def piece_rows(d):
        return pl.ds(pl.multiple_of(((dp + d) % DP) * piece, piece), piece)

    def grow(b):
        def body(at, k, carry):
            mask = wide(r.maskf[at, :], cw)
            d = lead3 * r.dpre[at, :] - mask * (flat3 + r.ex[at, :] * slope3)
            r.de[at, :] = d.astype(BF16)
            return carry

        for i in range(ipd):
            strips((b * ipd + i) * CELLS, body, 0)
        value = dot(r.mt[:, block_rows(b)], r.de[block_rows(b), :])
        r.eg[...] += value

    r.eg[...] = jnp.zeros((width, cw), F32)
    loop(CH, grow)
    r.es[...] = r.eg[...].astype(et)

    for d in range(1, DP):
        remote(r.es.at[piece_rows(d)], r.ebuf.at[DP - d], r.eg_send.at[0], r.eg_recv.at[0], across(d)).start()

    everyone_wait(r.g5, 4)
    everyone_wait(r.g4, 3)
    up_gap = r.gate_up[:, 0:width] - r.gate_up[:, width:two]

    def gate_back(n, state):
        at = gate_block(n)
        grad_lo, grad_hi = lower_upper(r.g4, n)
        grad = exact_nt(grad_lo, up_gap[:, 0:LANES]) + exact_nt(grad_hi, up_gap[:, LANES:width])
        grad = grad * r.gate_slope[at, :]
        r.grad_down[at, :] = grad
        return state[0] + total(grad), state[1] + total(grad * r.gate_x[at, :])

    gate_shift_all, gate_gain_all = lax.fori_loop(0, gate_blocks, gate_back, (zero1, zero1))
    lead = r.gate_gain[...] * gate_scale

    def gate_norm_back(n, state):
        at = gate_block(n)
        grad = r.grad_down[at, :] - gate_shift_all * every - r.gate_x[at, :] * (gate_gain_all * every)
        grad = jnp.where(valid, lead * grad, 0.0)
        r.grad_down[at, :] = grad
        summary = exact_nt(grad, r.gate_down[...])
        slots = gate_rows // 8

        @pl.when(n == 0)
        def _():
            r.grad_summary[...] = summary[0:8, :]

        slopes = r.g5[pl.ds(n * slots, slots)].astype(F32)
        new = []
        for stat in range(2):
            for p in range(width // LANES):
                part = summary[:, p * LANES : (p + 1) * LANES]
                part = (part + pltpu.roll(part, 4, 0)).reshape(slots, 8, LANES)
                k = stat * (width // LANES) + p
                new.append(state[k] + jnp.sum(part * slopes[:, 8 * k : 8 * k + 8, :], axis=0))
        new.append(state[-1] + total(summary))
        return tuple(new)

    n_half = width // LANES
    zero = jnp.zeros((8, LANES), F32)
    *flats, summed = lax.fori_loop(
        0, gate_blocks, gate_norm_back, (zero,) * (2 * n_half) + (jnp.zeros((1, width), F32),)
    )
    guess = slope_guess()
    column_wait(r.c4, 3)
    told = jnp.sum(r.c4[...], axis=0)

    def second_sum(stat):
        parts = []
        for q in range(2 * n_half):
            flat = flats[stat * n_half + q % n_half]
            flat = total(flat[4 * (q // n_half) : 4 * (q // n_half) + 4, :])
            at = 2 * n_half * stat + q
            lanes = slice(q % n_half * LANES, (q % n_half + 1) * LANES)
            flat = flat + guess[stat][:, q * LANES : (q + 1) * LANES] * summed[:, lanes]
            parts.append(flat + told[at : at + 1, :])
        return jnp.concatenate(parts, axis=1)

    shift_grad2, gain_grad2 = second_sum(0), second_sum(1)
    lead2, base2, slant2 = gain2 * scale2, shift_grad2 * inverse, gain_grad2 * inverse

    def splits_back(i):
        att = r.att[pl.ds(i, 1), :]
        flat = r.grad_summary[pl.ds(i, 1), :] * wide(r.share[pl.ds(i, 1), :], width)

        def body(at, k, carry):
            there = pl.ds(pl.multiple_of((ch * ipd + i) * CELLS + k * STRIP, STRIP), STRIP)
            put_at = pl.ds(pl.multiple_of(SIDE + k * STRIP, SIDE), STRIP)
            mask = r.maskf[there, :]
            for q in range(two // LANES):
                g, p = q // n_half, q % n_half
                lanes = slice(q * LANES, (q + 1) * LANES)
                here = slice(p * LANES, (p + 1) * LANES)
                d = (r.dm[at, here] * att[:, lanes] + flat[:, here]) * r.slope2[at, lanes]
                d = mask * lead2[:, lanes] * (d - base2[:, lanes] - r.sp[at, lanes] * slant2[:, lanes])
                r.act2[at, lanes] = d
                before = jnp.where(not_first, pltpu.roll(d, 1, 0), 0.0)
                after = jnp.where(not_last, pltpu.roll(d, STRIP - 1, 0), 0.0)
                for n, value in enumerate((after, d, before)):
                    start = n * width + p * LANES
                    r.dsh[g, i, put_at, start : start + LANES] = value.astype(BF16)
            return carry

        strips(i * CELLS, body, 0)

    loop(ipd, splits_back)

    drain(r.ebuf.at[pl.ds(1, DP - 1)], r.eg_recv.at[0])
    value = r.eg[piece_rows(0), :]
    for d in range(1, DP):
        value = value + r.ebuf[d].astype(F32)
    r.eo[0] = value.astype(et)
    for d in range(1, DP):
        remote(r.eo.at[0], r.eo.at[DP - d], r.eg_send.at[1], r.eg_recv.at[1], across(d)).start()

    def first_back(n, state):
        there = pl.ds(pl.multiple_of((ch * ipd + 2 * n) * CELLS, 2 * CELLS), 2 * CELLS)
        out = []
        for g in range(2):
            lanes = slice(g * half, (g + 1) * half)
            left = jnp.concatenate(
                [
                    r.dsh[g, pl.ds(2 * n, 2), (2 - k) * SIDE : (2 - k) * SIDE + CELLS, :].reshape(2 * CELLS, 3 * width)
                    for k in range(3)
                ],
                axis=1,
            )
            value = dot(left, r.wt[g]) * r.slope1[two_of(n), lanes]
            r.dh1[there, lanes] = value.astype(BF16)
            out.append((state[g][0] + fold(value), state[g][1] + fold(value * r.red[two_of(n), lanes])))
        return tuple(out)

    zero_h = jnp.zeros((8, half), F32)
    gd = Gather(2, lambda b, i: r.dh1.at[rows_of(b, i)], lambda b: r.dh1.at[block_rows(b)], ipd)
    state = ((zero_h, zero_h), (zero_h, zero_h))
    for n in range(ipd // 2):
        state = first_back(n, state)
        if n == 0:
            loop(2, gd.send)
    for g in range(2):
        r.g6[0, g : g + 1, :] = total(state[g][0])
        r.g6[0, 2 + g : 3 + g, :] = total(state[g][1])
    everyone(r.g6, 5)
    lax.fori_loop(2, ipd, lambda i, carry: (gd.send(i), carry)[1], 0)

    def pass_x(i):
        for t in range(1, X):
            gx.from_peer(t, i)

    loop(ipd, pass_x)

    drain(r.stage, r.rs_core_send.at[1])

    def turn_d(i):
        for g in range(2):
            r.stage[g, i] = r.act2[image(i), g * width : (g + 1) * width].T.astype(BF16)

    loop(ipd, turn_d)
    per = CH // 2
    wide3 = 3 * half
    for k in range(3):
        for g in range(2):
            right = r.act[g, :, k * SIDE : k * SIDE + CELLS, :].reshape(own_rows, wide3)
            value = dot(jnp.concatenate([r.stage[g, i] for i in range(ipd)], axis=1), right)
            if c.split_inside:
                for q in range(per):
                    b = g * per + q
                    r.ss[k, b % 2, b // 2] = value[q * m2 : (q + 1) * m2, :].astype(BF16)
            else:
                r.split_part[g * width : (g + 1) * width, k * wide3 : (k + 1) * wide3] = value
        if c.split_inside:
            remote(r.ss.at[k, 1 - core], r.sin.at[k], r.sg_send.at[0, k], r.sg_recv.at[0, k], mate).start()
    slab = m2 // DP
    Z = DP // 2
    turn, side = dp // 2, dp % 2

    def ring(e):
        return (((turn + e) % Z) * 2 + side, ch)

    other = (dp + 1 - 2 * side, ch)

    def split_cores(k):
        drain(r.sin.at[k], r.sg_recv.at[0, k])
        for t in range(X):
            value = (r.ss[k, core, t].astype(F32) + r.sin[k, t].astype(F32)).astype(BF16)
            value = value.reshape(Z, 2, slab, wide3)
            for p in range(2):
                r.sc[k, p, :, t] = value[:, p]
        remote(r.sc.at[k, 1 - side], r.sp1.at[k], r.sg_send.at[1, k], r.sg_recv.at[1, k], other).start()

    def split_pairs(k):
        drain(r.sp1.at[k], r.sg_recv.at[1, k])
        r.sy[k] = (r.sc[k, side].astype(F32) + r.sp1[k].astype(F32)).astype(BF16)
        for e in range(1, Z):
            remote(
                r.sy.at[k, (turn + e) % Z], r.sz.at[k, Z - e], r.sg_send.at[2, k], r.sg_recv.at[2, k], ring(e)
            ).start()

    def split_chips(k):
        drain(r.sz.at[k, pl.ds(1, Z - 1)], r.sg_recv.at[2, k])
        for t in range(X):
            there = (chip + t) % X
            value = r.sy[k, turn, there].astype(F32)
            for e in range(1, Z):
                value = value + r.sz[k, e, there].astype(F32)
            r.sx[k, t] = value.astype(BF16)
            if t:
                remote(r.sx.at[k, t], r.sxin.at[k, X - t], r.sg_send.at[3, k], r.sg_recv.at[3, k], peer(t)).start()

    def split_out(k):
        drain(r.sxin.at[k, pl.ds(1, X - 1)], r.sg_recv.at[3, k])
        value = r.sx[k, 0].astype(F32)
        for t in range(1, X):
            value = value + r.sxin[k, t].astype(F32)
        r.so[k, 0] = value.astype(BF16)
        for d in range(1, DP):
            remote(r.so.at[k, 0], r.so.at[k, DP - d], r.sg_send.at[4, k], r.sg_recv.at[4, k], across(d)).start()

    def split_step(step, k):
        if c.split_inside:
            step(k)

    for k in range(3):
        split_step(split_cores, k)
    everyone_wait(r.g6, 5)
    sums = jnp.sum(r.g6[...], axis=0)
    shift_grad, gain_grad = get(sums, 0, width), get(sums, 2, width)
    lead1, base1, slant1 = gain1 * scale1, shift_grad * inverse, gain_grad * inverse

    r.rg[...] = jnp.zeros((cw, width), F32)

    def from_x(i):
        gx.from_mate(i)
        for t in range(1, X):
            gx.from_pass(t, i)

    loop(ipd, from_x)
    gx.done()

    def reduced_back(b, i):
        def body(at, k, carry):
            mask = wide(r.maskf[at, :], width)
            d = mask * lead1 * (r.dh1[at, :].astype(F32) - base1 - r.xh1[at, :].astype(F32) * slant1)
            r.xh1[at, :] = d.astype(BF16)
            return carry

        strips((b * ipd + i) * CELLS, body, 0)
        r.rg[...] += dot(r.xt[b * ipd + i], r.xh1[rows_of(b, i), :])

    def input_back(b, i):
        at = rows_of(b, i)
        r.xv[at, :] = (r.dpre[at, :] + dot(r.xh1[at, :], r.wrt[...])).astype(BF16)
        pltpu.make_async_copy(r.xv.at[at], r.inputs_grad.at[at], r.store.at[1]).start()

    loop(ipd, lambda i: reduced_back(ch, i))

    def from_mate(i):
        gd.from_mate(i)
        reduced_back(block_of(0, False), i)

    loop(ipd, from_mate)
    split_step(split_pairs, 0)
    for t in range(1, X):

        def from_peer(i):
            gd.from_peer(t, i)
            reduced_back(block_of(t, True), i)

        loop(ipd, from_peer)
    split_step(split_pairs, 1)
    for t in range(1, X):

        def from_pass(i):
            gd.from_pass(t, i)
            reduced_back(block_of(t, False), i)

        loop(ipd, from_pass)

    if c.reduce_inside:
        r.rs[...] = r.rg[...].T.astype(r.rs.dtype)
        for d in range(1, DP):
            remote(r.rs.at[piece_rows(d)], r.rbuf.at[DP - d], r.rg_send.at[0], r.rg_recv.at[0], across(d)).start()
    else:
        r.reduce_part[...] = r.rg[...].T
    split_step(split_pairs, 2)
    split_step(split_chips, 0)
    loop(ipd, lambda i: input_back(ch, i))
    split_step(split_chips, 1)
    loop(ipd, lambda i: input_back(block_of(0, False), i))
    split_step(split_out, 0)
    split_step(split_chips, 2)
    if c.reduce_inside:
        groups = DP // CH
        goal = dp // groups
        drain(r.rbuf.at[pl.ds(1, DP - 1)], r.rg_recv.at[0])
        value = r.rs[piece_rows(0), :].astype(F32)
        for d in range(1, DP):
            value = value + r.rbuf[d].astype(F32)
        r.rsum[...] = value.astype(r.rsum.dtype)
        slot = r.rall.at[dp % groups, ch]
        for d in range(1, DP):
            remote(r.rsum, slot, r.rg_send.at[1], r.rg_recv.at[1], ((dp + d) % DP, goal)).start()

        @pl.when(goal == ch)
        def _():
            pltpu.make_async_copy(r.rsum, slot, r.rg_recv.at[1]).start()

        @pl.when(goal != ch)
        def _():
            remote(r.rsum, slot, r.rg_send.at[2], r.rg_recv.at[1], (dp, goal)).start()

    split_step(split_out, 1)
    for t in range(1, X):
        loop(ipd, lambda i: input_back(block_of(t, True), i))
    split_step(split_out, 2)
    for t in range(1, X):
        loop(ipd, lambda i: input_back(block_of(t, False), i))
    r.second_gain_grad[...] = exact_nt(gain_grad2, pick2)
    r.second_shift_grad[...] = exact_nt(shift_grad2, pick2)
    r.first_gain_grad[...] = exact_nt(gain_grad, pick1)
    r.first_shift_grad[...] = exact_nt(shift_grad, pick1)
    r.gate_gain_grad[...] = exact_nt(gate_gain_all, pickg)
    r.gate_shift_grad[...] = exact_nt(gate_shift_all, pickg)

    def gate_grads(n, state):
        at = gate_block(n)
        sum_lo, sum_hi = lower_upper(r.g3, n)
        grad_lo, grad_hi = lower_upper(r.g4, n)
        picked = exact_nt(r.grad_down[at, :], pickg)
        down = jnp.concatenate([exact_tn(picked, sum_lo), exact_tn(picked, sum_hi)], axis=1)
        squeezed = r.squeezed[at, :]
        up = jnp.concatenate([exact_tn(squeezed, grad_lo), exact_tn(squeezed, grad_hi)], axis=1)
        bias = jnp.concatenate([total(grad_lo), total(grad_hi)], axis=1)
        return state[0] + down, state[1] + up, state[2] + bias

    down, up, bias = lax.fori_loop(
        0, gate_blocks, gate_grads,
        (jnp.zeros((mg, width), F32), jnp.zeros((inner, width), F32), jnp.zeros((1, width), F32)),
    )
    r.down_grad[...] = down
    r.up_grad[...] = exact_nt(jnp.concatenate([up, -up], axis=1), pick2)
    r.bias_grad[...] = exact_nt(jnp.concatenate([bias, -bias], axis=1), pick2)

    drain(r.eo.at[pl.ds(1, DP - 1)], r.eg_recv.at[1])
    for d in range(DP):
        r.expand_grad[piece_rows(d), :] = r.eo[d].astype(F32)
    if c.reduce_inside:
        drain(r.rall, r.rg_recv.at[1])
        for s in range(groups):
            for q in range(CH):
                r.reduce_grad[s * piece : (s + 1) * piece, q * cw : (q + 1) * cw] = r.rall[s, q].astype(F32)
    if c.split_inside:
        for k in range(3):
            drain(r.so.at[k, pl.ds(1, DP - 1)], r.sg_recv.at[4, k])
            for p in range(3):
                at = slice(p * half, (p + 1) * half)
                block = jnp.concatenate(
                    [r.so[k, (d - dp + DP) % DP, :, at].astype(F32) for d in range(DP)], axis=0
                )
                r.split_grad[3 * k + p] = block.T

    for k, buf in enumerate((r.g1, r.g2, r.g3, r.g4, r.g5, r.g6, r.c2)):
        everyone_done(buf, k)
    column_done(r.c1, 0)
    row_done(r.r1, 1)
    row_done(r.r2, 0)
    row_done(r.r4, 2)
    column_done(r.c4, 3)
    rs2.done(False)
    for gather in (gm, gd) + shares:
        gather.done()
    drain(r.pbuf.at[pl.ds(1, CH - 1)], r.par_send.at[0])
    drain(r.ebuf.at[pl.ds(1, DP - 1)], r.eg_send.at[0])
    drain(r.ebuf.at[pl.ds(1, DP - 1)], r.eg_send.at[1])
    if c.reduce_inside:
        drain(r.rbuf.at[pl.ds(1, DP - 1)], r.rg_send.at[0])
        drain(r.rbuf.at[pl.ds(1, DP - 1)], r.rg_send.at[1])

        @pl.when(goal != ch)
        def _():
            drain(r.rsum, r.rg_send.at[2])

    if c.split_inside:
        for k in range(3):
            drain(r.sin.at[k], r.sg_send.at[0, k])
            drain(r.sp1.at[k], r.sg_send.at[1, k])
            drain(r.sz.at[k, pl.ds(1, Z - 1)], r.sg_send.at[2, k])
            drain(r.sxin.at[k, pl.ds(1, X - 1)], r.sg_send.at[3, k])
            drain(r.so.at[k, pl.ds(1, DP - 1)], r.sg_send.at[4, k])
    drain(r.cv, r.store.at[0])
    drain(r.xv, r.store.at[1])


def hand_over(*refs):
    count = (len(refs) - 1) // 3
    sources, results, places, sems = refs[:count], refs[count : 2 * count], refs[2 * count : -1], refs[-1]
    copies = []
    for source, result, place in zip(sources, results, places):
        rows = source.shape[0]
        parts = 2 if rows >= 1024 else 1
        for p in range(parts):
            at = pl.ds(p * (rows // parts), rows // parts)
            k = len(copies)
            inward = pltpu.make_async_copy(source.at[at], place.at[at], sems.at[k, 0])
            copies.append((inward, pltpu.make_async_copy(place.at[at], result.at[at], sems.at[k, 1])))
            inward.start()
    for inward, outward in copies:
        inward.wait()
        outward.start()
    for inward, outward in copies:
        outward.wait()


ARGS = (
    "inputs", "resolution", "reduce_weight", "first_gain", "first_shift", "split_weight", "second_gain",
    "second_shift", "gate_down", "gate_gain", "gate_shift", "gate_up", "gate_bias", "expand_weight",
    "third_gain", "third_shift", "cotangent",
)


def per_device(*arrays):
    a = dict(zip(ARGS, arrays))
    c = types.SimpleNamespace()
    c.DP, c.CH = lax.axis_size("dp"), lax.axis_size("chan")
    c.X, c.D = c.CH // 2, c.DP * c.CH
    c.images = a["resolution"].shape[0]
    c.ipd = c.images // c.CH
    rows, c.cw = a["inputs"].shape
    c.width = a["reduce_weight"].shape[1]
    c.inner = a["gate_down"].shape[1]
    c.m1, c.m2, c.mg = c.width // c.CH, 2 * c.width // c.CH, c.inner // c.CH
    half, two = c.width // 2, 2 * c.width
    taps = 9 * half
    piece = c.width // c.DP
    piece_type = BF16 if piece % 16 == 0 else F32
    c.reduce_inside = c.DP % c.CH == 0 and piece % 8 == 0
    c.share = taps % (16 * c.DP) == 0 and c.width % (16 * c.DP) == 0
    c.split_inside = c.m2 % (16 * c.DP) == 0 and c.DP % 2 == 0 and c.DP > 2
    own = c.ipd * CELLS
    DP, CH, X, D, ipd, cw, width = c.DP, c.CH, c.X, c.D, c.ipd, c.cw, c.width
    for name in ARGS:
        if a[name].ndim == 1 and name != "resolution":
            a[name] = a[name].reshape(1, -1)
    a["split_weight"] = a["split_weight"].reshape(taps, c.m2)
    sds = jax.ShapeDtypeStruct
    outs = dict(
        block_out=sds((rows, cw), BF16),
        inputs_grad=sds((rows, cw), BF16),
        first_gain_grad=sds((1, c.m1), F32),
        first_shift_grad=sds((1, c.m1), F32),
        second_gain_grad=sds((1, c.m2), F32),
        second_shift_grad=sds((1, c.m2), F32),
        down_grad=sds((c.mg, width), F32),
        gate_gain_grad=sds((1, c.mg), F32),
        gate_shift_grad=sds((1, c.mg), F32),
        up_grad=sds((c.inner, c.m2), F32),
        bias_grad=sds((1, c.m2), F32),
        expand_grad=sds((width, cw), F32),
        third_gain_grad=sds((1, cw), F32),
        third_shift_grad=sds((1, cw), F32),
    )
    if c.reduce_inside:
        outs["reduce_grad"] = sds((c.m1, CH * cw), F32)
    else:
        outs["reduce_part"] = sds((width, cw), F32)
    if c.split_inside:
        outs["split_grad"] = sds((9, half, c.m2), F32)
    else:
        outs["split_part"] = sds((two, taps), F32)
    V = pltpu.VMEM
    dma = lambda *shape: pltpu.SemaphoreType.DMA(shape)
    scratch = dict(
        xv=V((rows, cw), BF16), cv=V((rows, cw), BF16), wr=V((cw, width), BF16), wrt=V((width, cw), BF16),
        wet=V((cw, width), BF16), xt=V((c.images, cw, CELLS), BF16), mt=V((width, rows), BF16),
        maskf=V((rows, LANES), F32), area=V((c.images, LANES), F32), pbuf=V((CH, 8, two), F32),
        red=V((own, width), F32), slope1=V((own, width), F32), xh1=V((rows, width), BF16),
        act=V((2, ipd, TALL, 3 * half), BF16), dsh=V((2, ipd, TALL, 3 * width), BF16),
        wg=V((CH, taps, c.m2), BF16), wx=V((CH, width, cw), BF16), wf=V((2, taps, width), BF16), wt=V((2, 9 * width, half), BF16),
        sp=V((own, two), F32), slope2=V((own, two), F32), act2=V((own, two), F32), share=V((8, LANES), F32),
        gate_x=V((D * 8, LANES), F32), squeezed=V((D * 8, LANES), F32), gate_slope=V((D * 8, LANES), F32),
        grad_down=V((D * 8, LANES), F32), grad_summary=V((8, width), F32), att=V((8, two), F32),
        merged=V((rows, width), BF16), ex=V((rows, cw), F32), acc=V((16, cw), F32),
        dpre=V((rows, cw), F32), de=V((rows, cw), BF16), dm=V((own, width), F32), dh1=V((rows, width), BF16),

        eg=V((width, cw), F32), es=V((width, cw), piece_type), ebuf=V((DP, piece, cw), piece_type),
        eo=V((DP, piece, cw), piece_type), rg=V((cw, width), F32),
        all_send=dma(7), all_recv=dma(7), col_send=dma(4), col_recv=dma(4), row_send=dma(3), row_recv=dma(3),
        rs_core_send=dma(2), rs_core_recv=dma(2, X, ipd), rs_chip_send=dma(2), rs_chip_recv=dma(2, X, ipd),
        ag_core_send=dma(3), ag_core_recv=dma(3, ipd), ag_chip_send=dma(3, X), ag_chip_recv=dma(3, X, ipd),
        ag_pass_send=dma(3, X), ag_pass_recv=dma(3, X, ipd), sh_core_send=dma(2), sh_core_recv=dma(2),
        sh_chip_send=dma(2, X), sh_chip_recv=dma(2, X), sh_col_send=dma(2, X), sh_col_recv=dma(2, X, DP),
        sh_pass_send=dma(2, X), sh_pass_recv=dma(2, X), par_send=dma(1), par_recv=dma(CH),
        eg_send=dma(2), eg_recv=dma(2), rg_send=dma(3), rg_recv=dma(2), sg_send=dma(5, 3), sg_recv=dma(5, 3),
        load=dma(2 + 2 * X), store=dma(2),
    )
    for name, count in (
        ("stage", X), ("inward", X), ("outward", X - 1), ("landed", X - 1), ("inward2", X), ("landed2", X - 1)
    ):
        scratch[name] = V((count, ipd, CELLS, width), BF16)
    for k in range(1, 5):
        scratch[f"g{k}"] = V((D, 8, LANES), F32)
    scratch["r4"] = V((CH, 8, LANES), F32)
    scratch["c4"] = V((DP, 8, LANES), F32)
    scratch["g5"] = V((D, 16 * width // LANES, LANES), BF16)
    scratch["told"] = V((16, LANES), F32)
    scratch["slopes"] = V((16 * width // LANES, LANES), F32)
    scratch["back3"] = V((CH, 4, LANES), F32)
    scratch["sums3"] = V((CH, 4, LANES), F32)
    scratch["c1"] = V((DP, 4, LANES), F32)
    scratch["r1"] = V((CH, 4, LANES), F32)
    scratch["r2"] = V((CH, 8, LANES), F32)
    scratch["mix"] = V((width, width), F32)
    scratch["mixb"] = V((width, width), BF16)
    scratch["offset"] = V((16, width), F32)
    scratch["wxt"] = V((CH, cw, width), BF16)
    scratch["c2"] = V((D, 4, LANES), F32)
    scratch["g6"] = V((D, 4, LANES), F32)
    if c.reduce_inside:
        scratch.update(
            rs=V((width, cw), piece_type), rbuf=V((DP, piece, cw), piece_type), rsum=V((piece, cw), piece_type),
            rall=V((DP // CH, CH, piece, cw), piece_type),
        )
    if c.split_inside:
        slab = c.m2 // DP
        scratch.update(
            ss=V((3, 2, X, c.m2, 3 * half), BF16), sin=V((3, X, c.m2, 3 * half), BF16),
            sc=V((3, 2, c.DP // 2, X, slab, 3 * half), BF16), sp1=V((3, c.DP // 2, X, slab, 3 * half), BF16),
            sy=V((3, c.DP // 2, X, slab, 3 * half), BF16), sz=V((3, c.DP // 2, X, slab, 3 * half), BF16),
            sx=V((3, X, slab, 3 * half), BF16), sxin=V((3, X, slab, 3 * half), BF16),
            so=V((3, c.DP, slab, 3 * half), BF16),
        )
    anywhere = pl.BlockSpec(memory_space=pl.ANY)
    vmem = pl.BlockSpec(memory_space=pltpu.VMEM)
    spec = dict(
        inputs=anywhere, cotangent=anywhere, reduce_weight=anywhere, block_out=anywhere, inputs_grad=anywhere,
        resolution=pl.BlockSpec(memory_space=pltpu.SMEM),
    )
    names = tuple(ARGS) + tuple(outs) + tuple(scratch)
    results = pl.pallas_call(
        functools.partial(kernel, c, names),
        out_shape=tuple(outs.values()),
        in_specs=[spec.get(name, vmem) for name in ARGS],
        out_specs=tuple(spec.get(name, vmem) for name in outs),
        scratch_shapes=list(scratch.values()),
        compiler_params=pltpu.CompilerParams(
            collective_id=0, has_side_effects=True, vmem_limit_bytes=62 * 2**20
        ),
        name="block",
    )(*[a[name] for name in ARGS])
    results = pl.pallas_call(
        hand_over,
        out_shape=tuple(outs.values()),
        in_specs=[anywhere] * len(outs),
        out_specs=tuple(anywhere for _ in outs),
        scratch_shapes=[V(v.shape, v.dtype) for v in outs.values()] + [dma(4 * len(outs), 2)],
        compiler_params=pltpu.CompilerParams(vmem_limit_bytes=62 * 2**20),
        name="results",
    )(*results)
    o = dict(zip(outs, results))
    if not c.reduce_inside:
        place = lax.axis_index("chan")
        part = lax.psum(o["reduce_part"], "dp")
        part = lax.all_gather(part, "chan", axis=1, tiled=True)
        o["reduce_grad"] = lax.dynamic_slice_in_dim(part, place * c.m1, c.m1, 0)
    if not c.split_inside:
        place = lax.axis_index("chan")
        part = lax.psum(o["split_part"], ("dp", "chan"))
        part = lax.dynamic_slice_in_dim(part, place * c.m2, c.m2, 0)
        o["split_grad"] = part.T.reshape(9, half, c.m2)
    flat = lambda name: o[name].reshape(-1)
    return (
        o["block_out"], o["inputs_grad"], o["reduce_grad"].T, flat("first_gain_grad"), flat("first_shift_grad"),
        o["split_grad"], flat("second_gain_grad"), flat("second_shift_grad"), o["down_grad"].T,
        flat("gate_gain_grad"), flat("gate_shift_grad"), o["up_grad"], flat("bias_grad"), o["expand_grad"],
        flat("third_gain_grad"), flat("third_shift_grad"),
    )


def solution(mesh):
    placed = (
        P("dp", "chan"), P("dp"), P(), P("chan"), P("chan"), P(None, None, "chan"), P("chan"), P("chan"),
        P(), P(), P(), P(), P(), P(None, "chan"), P("chan"), P("chan"), P("dp", "chan"),
    )
    return jax.shard_map(
        per_device,
        mesh=mesh,
        in_specs=placed,
        out_specs=(
            P("dp", "chan"), P("dp", "chan"), P(None, "chan"), P("chan"), P("chan"), P(None, None, "chan"),
            P("chan"), P("chan"), P(None, "chan"), P("chan"), P("chan"), P(None, "chan"), P("chan"),
            P(None, "chan"), P("chan"), P("chan"),
        ),
        check_vma=False,
    )
```

```python
import functools
import types

import jax
import jax.numpy as jnp
from jax import lax
from jax.experimental import pallas as pl
from jax.experimental.pallas import tpu as pltpu
from jax.sharding import PartitionSpec as P

SIDE = 16
CELLS = SIDE * SIDE
TALL = CELLS + 2 * SIDE
LANES = 128
EPS = 1e-05
HIGHEST = lax.Precision.HIGHEST
F32 = jnp.float32
BF16 = jnp.bfloat16
MESH = pl.DeviceIdType.MESH
STRIP = 32


def wide(mask, width):
    return mask if width == LANES else jnp.concatenate([mask] * (width // LANES), axis=1)


def fold(values):
    return jnp.sum(values.reshape(values.shape[0] // 8, 8, values.shape[1]), axis=0)


def total(values):
    return jnp.sum(values, axis=0, keepdims=True)


def sigmoid(values):
    return 0.5 * jnp.tanh(0.5 * values) + 0.5


def dot(left, right):
    return jnp.dot(left, right, preferred_element_type=F32)


def exact(left, right):
    return jnp.dot(left, right, precision=HIGHEST, preferred_element_type=F32)


def exact_nt(left, right):
    return lax.dot_general(
        left, right, (((1,), (1,)), ((), ())), precision=HIGHEST, preferred_element_type=F32
    )


def exact_tn(left, right):
    return lax.dot_general(
        left, right, (((0,), (0,)), ((), ())), precision=HIGHEST, preferred_element_type=F32
    )


def flip(values):
    return values.astype(F32).T.astype(values.dtype)


def put(ref, row, vector):
    for part in range(vector.shape[1] // LANES):
        ref[0, row + part : row + part + 1, :] = vector[:, part * LANES : (part + 1) * LANES]


def get(block, row, width):
    parts = [block[row + q : row + q + 1, :] for q in range(width // LANES)]
    return parts[0] if len(parts) == 1 else jnp.concatenate(parts, axis=1)


def kernel(c, names, *refs):
    r = types.SimpleNamespace(**dict(zip(names, refs)))
    DP, CH, X, D, ipd, images = c.DP, c.CH, c.X, c.D, c.ipd, c.images
    width, cw, inner, m1, m2, mg = c.width, c.cw, c.inner, c.m1, c.m2, c.mg
    half, two = width // 2, 2 * width
    own_rows = ipd * CELLS
    taps = 9 * half
    dp = lax.axis_index("dp")
    ch = lax.axis_index("chan")
    core = ch % 2
    chip = ch // 2
    mate = (dp, ch + 1 - 2 * core)
    f0 = ((0, 0), (0, 0))

    def remote(src, dst, send, recv, device):
        return pltpu.make_async_remote_copy(
            src_ref=src, dst_ref=dst, send_sem=send, recv_sem=recv, device_id=device, device_id_type=MESH
        )

    def drain(ref, sem):
        pltpu.make_async_copy(ref, ref, sem).wait()

    def loop(count, body):
        def step(i, carry):
            body(i)
            return carry

        lax.fori_loop(0, count, step, 0)

    def peer(t):
        return (dp, ((chip + t) % X) * 2 + core)

    def across(d):
        return ((dp + d) % DP, ch)

    def block_of(t, same):
        return ((chip + t) % X) * 2 + (core if same else 1 - core)

    def rows_of(b, i):
        return pl.ds(pl.multiple_of((b * ipd + i) * CELLS, CELLS), CELLS)

    def block_rows(b):
        return pl.ds(pl.multiple_of(b * own_rows, own_rows), own_rows)

    def image(i):
        return pl.ds(pl.multiple_of(i * CELLS, CELLS), CELLS)

    def strips(base, body, carry, size=STRIP):
        def step(k, state):
            return body(pl.ds(pl.multiple_of(base + k * size, size), size), k, state)

        return lax.fori_loop(0, CELLS // size, step, carry)

    def everyone(buf, k, message=None):
        message = buf.at[0] if message is None else message

        def one(j, carry):
            d, q = j // CH, j % CH
            slot = ((DP - d) % DP) * CH + (CH - q) % CH
            remote(buf.at[0], buf.at[slot], r.all_send.at[k], r.all_recv.at[k], ((dp + d) % DP, (ch + q) % CH)).start()
            return carry

        lax.fori_loop(1, D, one, 0)

    def everyone_wait(buf, k):
        drain(buf.at[pl.ds(1, D - 1)], r.all_recv.at[k])

    def everyone_wait_on(buf, sem):
        drain(buf.at[pl.ds(1, D - 1)], sem)

    def everyone_done(buf, k):
        drain(buf.at[pl.ds(1, D - 1)], r.all_send.at[k])

    def column(buf, k):
        for d in range(1, DP):
            remote(buf.at[0], buf.at[DP - d], r.col_send.at[k], r.col_recv.at[k], across(d)).start()

    def row(buf, k, source=None):
        for q in range(1, CH):
            src = buf.at[0] if source is None else source.at[(ch + q) % CH]
            remote(src, buf.at[CH - q], r.row_send.at[k], r.row_recv.at[k], (dp, (ch + q) % CH)).start()

    def row_sum(buf, k, column_buf):
        drain(buf.at[pl.ds(1, CH - 1)], r.row_recv.at[k])
        column_buf[0] = jnp.sum(buf[...], axis=0)

    def row_done(buf, k):
        drain(buf.at[pl.ds(1, CH - 1)], r.row_send.at[k])

    def column_wait(buf, k):
        drain(buf.at[pl.ds(1, DP - 1)], r.col_recv.at[k])

    def column_done(buf, k):
        drain(buf.at[pl.ds(1, DP - 1)], r.col_send.at[k])

    class Scatter:
        def __init__(self, k, stage, inward, outward, landed, keep):
            self.k, self.stage, self.inward = k, stage, inward
            self.outward, self.landed, self.keep = outward, landed, keep

        def compute_mate(self, t, part):
            def body(i):
                self.stage[t, i] = part(block_of(t, False), i).astype(BF16)

            loop(ipd, body)

        def send_mate(self, t):
            def body(i):
                remote(
                    self.stage.at[t, i], self.inward.at[t, i],
                    r.rs_core_send.at[self.k], r.rs_core_recv.at[self.k, t, i], mate,
                ).start()

            loop(ipd, body)

        def mate_one(self, t, i, part):
            self.stage[t, i] = part(block_of(t, False), i).astype(BF16)
            remote(
                self.stage.at[t, i], self.inward.at[t, i],
                r.rs_core_send.at[self.k], r.rs_core_recv.at[self.k, t, i], mate,
            ).start()

        def to_mate(self, t, part):
            loop(ipd, lambda i: self.mate_one(t, i, part))

        def peer_one(self, t, i, part):
            value = part(block_of(t, True), i)
            drain(self.inward.at[t, i], r.rs_core_recv.at[self.k, t, i])
            self.outward[t - 1, i] = (value + self.inward[t, i].astype(F32)).astype(BF16)
            remote(
                self.outward.at[t - 1, i], self.landed.at[X - t - 1, i],
                r.rs_chip_send.at[self.k], r.rs_chip_recv.at[self.k, X - t, i], peer(t),
            ).start()

        def to_peer(self, t, part):
            loop(ipd, lambda i: self.peer_one(t, i, part))

        def both(self, t, part):
            self.mate_one(t, 0, part)

            def body(i, carry):
                self.mate_one(t, i, part)
                self.peer_one(t, i - 1, part)
                return carry

            lax.fori_loop(1, ipd, body, 0)
            self.peer_one(t, ipd - 1, part)

        def own(self, part):
            def body(i):
                value = part(ch, i)
                drain(self.inward.at[0, i], r.rs_core_recv.at[self.k, 0, i])
                self.keep[image(i), :] = value + self.inward[0, i].astype(F32)

            loop(ipd, body)

        def arrive(self, i):
            for t in range(1, X):
                drain(self.landed.at[t - 1, i], r.rs_chip_recv.at[self.k, t, i])

        def extra(self, i, at, lanes):
            value = self.landed[0, i, at, lanes].astype(F32)
            for t in range(2, X):
                value = value + self.landed[t - 1, i, at, lanes].astype(F32)
            return value

        def done(self, stage=True):
            if stage:
                drain(self.stage, r.rs_core_send.at[self.k])
            drain(self.outward, r.rs_chip_send.at[self.k])

    class Gather:
        def __init__(self, k, place, whole, pieces):
            self.k, self.place, self.whole, self.pieces = k, place, whole, pieces

        def send(self, i):
            src = self.place(ch, i)
            remote(src, src, r.ag_core_send.at[self.k], r.ag_core_recv.at[self.k, i], mate).start()
            for t in range(1, X):
                remote(src, src, r.ag_chip_send.at[self.k, t], r.ag_chip_recv.at[self.k, X - t, i], peer(t)).start()

        def from_mate(self, i):
            drain(self.place(block_of(0, False), i), r.ag_core_recv.at[self.k, i])

        def from_peer(self, t, i):
            ref = self.place(block_of(t, True), i)
            drain(ref, r.ag_chip_recv.at[self.k, t, i])
            remote(ref, ref, r.ag_pass_send.at[self.k, t], r.ag_pass_recv.at[self.k, t, i], mate).start()

        def from_pass(self, t, i):
            drain(self.place(block_of(t, False), i), r.ag_pass_recv.at[self.k, t, i])

        def done(self):
            drain(self.whole(ch), r.ag_core_send.at[self.k])
            for t in range(1, X):
                drain(self.whole(ch), r.ag_chip_send.at[self.k, t])
                drain(self.whole(block_of(t, True)), r.ag_pass_send.at[self.k, t])

    class Share:
        def __init__(self, k, blocks, rows):
            self.k, self.blocks, self.piece = k, blocks, rows // DP

        def part(self, b, d):
            at = pl.ds(pl.multiple_of(((dp + d) % DP) * self.piece, self.piece), self.piece)
            return self.blocks.at[b, at]

        def send(self):
            own = self.blocks.at[ch]
            remote(own, own, r.sh_core_send.at[self.k], r.sh_core_recv.at[self.k], mate).start()
            for t in range(1, X):
                src = self.part(ch, 0) if c.share else own
                remote(src, src, r.sh_chip_send.at[self.k, t], r.sh_chip_recv.at[self.k, X - t], peer(t)).start()

        def spread(self):
            for t in range(1, X):
                b = block_of(t, True)
                src = self.part(b, 0) if c.share else self.blocks.at[b]
                drain(src, r.sh_chip_recv.at[self.k, t])
                if c.share:
                    for d in range(1, DP):
                        remote(src, src, r.sh_col_send.at[self.k, t], r.sh_col_recv.at[self.k, t, DP - d], across(d)).start()

        def hand(self):
            for t in range(1, X):
                b = block_of(t, True)
                if c.share:
                    for d in range(1, DP):
                        drain(self.part(b, d), r.sh_col_recv.at[self.k, t, d])
                whole = self.blocks.at[b]
                remote(whole, whole, r.sh_pass_send.at[self.k, t], r.sh_pass_recv.at[self.k, t], mate).start()

        def take(self):
            drain(self.blocks.at[block_of(0, False)], r.sh_core_recv.at[self.k])
            for t in range(1, X):
                drain(self.blocks.at[block_of(t, False)], r.sh_pass_recv.at[self.k, t])

        def done(self):
            own = self.blocks.at[ch]
            drain(own, r.sh_core_send.at[self.k])
            for t in range(1, X):
                whole = self.blocks.at[block_of(t, True)]
                drain(self.part(ch, 0) if c.share else own, r.sh_chip_send.at[self.k, t])
                drain(whole, r.sh_pass_send.at[self.k, t])
                if c.share:
                    for d in range(1, DP):
                        drain(self.part(block_of(t, True), 0), r.sh_col_send.at[self.k, t])

    barrier = pltpu.get_barrier_semaphore()

    def greet(j, carry):
        pl.semaphore_signal(
            barrier, inc=1, device_id=((dp + j // CH) % DP, (ch + j % CH) % CH), device_id_type=MESH
        )
        return carry

    lax.fori_loop(1, D, greet, 0)

    load_w = pltpu.make_async_copy(
        r.reduce_weight.at[pl.ds(pl.multiple_of(ch * cw, cw), cw)], r.wr, r.load.at[0]
    )
    load_w.start()
    order = []
    for t in list(range(1, X)) + [0]:
        order += [block_of(t, False), block_of(t, True)]
    loads = []
    for k, b in enumerate(order):
        at = pl.ds(pl.multiple_of(b * own_rows, own_rows), own_rows)
        loads.append(pltpu.make_async_copy(r.inputs.at[at], r.xv.at[at], r.load.at[2 + k]))
        loads[-1].start()
    load_c = pltpu.make_async_copy(r.cotangent, r.cv, r.load.at[1])
    load_c.start()

    row_at = lax.broadcasted_iota(jnp.int32, (CELLS, LANES), 0)
    spot_r = lax.shift_right_logical(row_at, 4)
    spot_c = lax.bitwise_and(row_at, 15)

    def make_mask(j):
        side = 12 + 2 * r.resolution[j]
        mask = jnp.where(jnp.logical_and(spot_r < side, spot_c < side), 1.0, 0.0)
        r.area[pl.ds(j, 1), :] = jnp.full((1, LANES), side * side, jnp.int32).astype(F32)
        r.maskf[image(j), :] = mask

    loop(images, make_mask)

    def part_reduce(b, i):
        at = rows_of(b, i)
        x = r.xv[at, :] * wide(r.maskf[at, :].astype(BF16), cw)
        r.xv[at, :] = x
        return dot(x, r.wr[...])

    r.wg[ch] = r.split_weight[...]
    r.wx[ch] = r.expand_weight[...]
    shares = (Share(0, r.wg, taps), Share(1, r.wx, width))

    load_w.wait()
    rs1 = Scatter(0, r.stage, r.inward, r.outward, r.landed, r.red)
    loads[0].wait()
    rs1.compute_mate(1, part_reduce)
    pl.semaphore_wait(barrier, D - 1)
    rs1.send_mate(1)
    for share in shares:
        share.send()
    for t in range(1, X):
        if t > 1:
            loads[2 * t - 2].wait()
            rs1.to_mate(t, part_reduce)
        loads[2 * t - 1].wait()
        rs1.to_peer(t, part_reduce)
    for share in shares:
        share.spread()
    loads[2 * X - 2].wait()
    rs1.to_mate(0, part_reduce)
    loads[2 * X - 1].wait()
    rs1.own(part_reduce)

    def selector(parts, mine):
        row = lax.broadcasted_iota(jnp.int32, (mine, mine * parts), 0)
        col = lax.broadcasted_iota(jnp.int32, (mine, mine * parts), 1)
        return jnp.where(col == row + ch * mine, 1.0, 0.0)

    pick1 = selector(CH, m1)
    pick2 = selector(CH, m2)
    pickg = selector(CH, mg)
    r.pbuf[0, 0:1, 0:width] = exact(r.first_gain[...], pick1)
    r.pbuf[0, 1:2, 0:width] = exact(r.first_shift[...], pick1)
    r.pbuf[0, 2:3, :] = exact(r.second_gain[...], pick2)
    r.pbuf[0, 3:4, :] = exact(r.second_shift[...], pick2)

    for q in range(1, CH):
        remote(r.pbuf.at[0], r.pbuf.at[CH - q], r.par_send.at[0], r.par_recv.at[CH - q], (dp, (ch + q) % CH)).start()

    pixels = lax.fori_loop(
        0, ipd, lambda i, count: count + r.area[pl.ds(ch * ipd + i, 1), :], jnp.zeros((1, LANES), F32)
    )
    r.g0[0] = jnp.zeros((4, LANES), F32)
    r.g0[0, 0:1, :] = pixels
    everyone(r.g0, 7)

    r.wrt[...] = flip(r.wr[...])
    r.wet[...] = flip(r.expand_weight[...])

    def turn_x(j):
        r.xt[j] = flip(r.xv[image(j), :])

    loop(images, turn_x)
    for g in range(2):
        for i in range(ipd):
            r.act[g, i, 0:SIDE, :] = jnp.zeros((SIDE, 3 * half), BF16)
            r.act[g, i, CELLS + SIDE : TALL, :] = jnp.zeros((SIDE, 3 * half), BF16)
            r.dsh[g, i, 0:SIDE, :] = jnp.zeros((SIDE, 3 * width), BF16)
            r.dsh[g, i, CELLS + SIDE : TALL, :] = jnp.zeros((SIDE, 3 * width), BF16)

    def finish_reduce(i, state):
        rs1.arrive(i)

        def body(at, k, state):
            first, second = state
            value = r.red[at, :] + rs1.extra(i, pl.ds(pl.multiple_of(k * STRIP, STRIP), STRIP), slice(None))
            r.red[at, :] = value
            return (first + fold(value), second + fold(value * value))

        return strips(i * CELLS, body, state)

    zero8 = jnp.zeros((8, width), F32)
    first, second = lax.fori_loop(0, ipd, finish_reduce, (zero8, zero8))

    put(r.g1, 0, total(first))
    put(r.g1, width // LANES, total(second))
    everyone(r.g1, 0)
    for share in shares:
        share.hand()
    everyone_wait(r.g1, 0)
    sums = jnp.sum(r.g1[...], axis=0)
    everyone_wait(r.g0, 7)
    count = jnp.sum(r.g0[...], axis=0)[0:1, 0:1]
    inverse = 1.0 / count
    params = r.pbuf[0]
    for q in range(1, CH):
        drain(r.pbuf.at[q], r.par_recv.at[q])
        params = params + r.pbuf[q]
    gain1, shift1 = params[0:1, 0:width], params[1:2, 0:width]
    gain2, shift2 = params[2:3, :], params[3:4, :]

    def moments(first, second):
        mean = first * inverse
        return mean, lax.rsqrt(second * inverse - mean * mean + EPS)

    mean1, scale1 = moments(get(sums, 0, width), get(sums, width // LANES, width))

    place_x = lambda b, i: r.xh1.at[rows_of(b, i)]
    gx = Gather(0, place_x, lambda b: r.xh1.at[block_rows(b)], ipd)

    strip_c = lax.bitwise_and(lax.broadcasted_iota(jnp.int32, (STRIP, LANES), 0), 15)
    not_first = strip_c != 0
    not_last = strip_c != 15

    def first_act(i):
        def body(at, k, carry):
            there = pl.ds(pl.multiple_of((ch * ipd + i) * CELLS + k * STRIP, STRIP), STRIP)
            put_at = pl.ds(pl.multiple_of(SIDE + k * STRIP, SIDE), STRIP)
            mask = r.maskf[there, :]
            for g in range(2):
                lanes = slice(g * half, (g + 1) * half)
                xh = (r.red[at, lanes] - mean1[:, lanes]) * scale1[:, lanes]
                h = gain1[:, lanes] * xh + shift1[:, lanes]
                s = sigmoid(h)
                y = h * s
                r.red[at, lanes] = xh
                r.xh1[there, lanes] = xh.astype(BF16)
                r.slope1[at, lanes] = mask * (s + y - y * s)
                a = mask * y
                before = jnp.where(not_first, pltpu.roll(a, 1, 0), 0.0)
                after = jnp.where(not_last, pltpu.roll(a, STRIP - 1, 0), 0.0)
                r.act[g, i, put_at, 0:half] = before.astype(BF16)
                r.act[g, i, put_at, half : 2 * half] = a.astype(BF16)
                r.act[g, i, put_at, 2 * half : 3 * half] = after.astype(BF16)
            return carry

        strips(i * CELLS, body, 0)

    loop(ipd, first_act)

    for share in shares:
        share.take()
    for g in range(2):
        for q in range(CH // 2):
            r.wf[g, :, q * m2 : (q + 1) * m2] = r.wg[g * (CH // 2) + q]

    def two_of(n):
        return pl.ds(pl.multiple_of(n * 2 * CELLS, 2 * CELLS), 2 * CELLS)

    def conv(n, state):
        there = pl.ds(pl.multiple_of((ch * ipd + 2 * n) * CELLS, 2 * CELLS), 2 * CELLS)
        out = []
        for g in range(2):
            lanes = slice(g * width, (g + 1) * width)
            left = jnp.concatenate(
                [
                    r.act[g, pl.ds(2 * n, 2), k * SIDE : k * SIDE + CELLS, :].reshape(2 * CELLS, 3 * half)
                    for k in range(3)
                ],
                axis=1,
            )
            value = dot(left, r.wf[g]) * wide(r.maskf[there, :], width)
            r.sp[two_of(n), lanes] = value
            out.append((state[g][0] + fold(value), state[g][1] + fold(value * value)))
        return tuple(out)

    state = lax.fori_loop(0, ipd // 2, conv, ((zero8, zero8), (zero8, zero8)))
    for g in range(2):
        put(r.g2, g * (width // LANES), total(state[g][0]))
        put(r.g2, (2 + g) * (width // LANES), total(state[g][1]))
    everyone(r.g2, 1)
    loop(ipd // 2, gx.send)

    for g in range(2):
        for tap in range(9):
            r.wt[g, tap * width : (tap + 1) * width, :] = flip(r.wf[g, tap * half : (tap + 1) * half, :])

    everyone_wait(r.g2, 1)
    sums = jnp.sum(r.g2[...], axis=0)
    mean2, scale2 = moments(get(sums, 0, two), get(sums, two // LANES, two))

    r.g3[0] = jnp.zeros((8, LANES), F32)

    def second_act(i):
        def body(at, k, state):
            there = pl.ds(pl.multiple_of((ch * ipd + i) * CELLS + k * STRIP, STRIP), STRIP)
            mask = r.maskf[there, :]
            new = []
            for q in range(two // LANES):
                lanes = slice(q * LANES, (q + 1) * LANES)
                xh = (r.sp[at, lanes] - mean2[:, lanes]) * scale2[:, lanes]
                h = gain2[:, lanes] * xh + shift2[:, lanes]
                s = sigmoid(h)
                y = h * s
                r.sp[at, lanes] = xh
                r.slope2[at, lanes] = mask * (s + y - y * s)
                a = mask * y
                r.act2[at, lanes] = a
                new.append(state[q] + fold(a))
            return tuple(new)

        zero = jnp.zeros((8, LANES), F32)
        pooled = strips(i * CELLS, body, (zero,) * (two // LANES))
        share = 1.0 / r.area[pl.ds(ch * ipd + i, 1), :]
        r.share[pl.ds(i, 1), :] = share
        n = width // LANES
        for q in range(n):
            r.g3[0, pl.ds(4 * q + i, 1), :] = total(pooled[q] + pooled[n + q]) * share

    loop(ipd, second_act)
    everyone(r.g3, 2)

    def slope_guess():
        root = 3.0**0.5
        points = []
        for z in (-root, 0.0, root):
            h = shift2 + z * gain2
            s = sigmoid(h)
            points.append(s + h * s - h * s * s)
        low, mid, high = points
        return (low + 4.0 * mid + high) * (1.0 / 6.0), (high - low) * (root / 6.0)

    guess = slope_guess()

    def slope_sums(i):
        share = r.share[pl.ds(i, 1), :]
        zero = jnp.zeros((8, LANES), F32)
        n = width // LANES

        def body(at, k, state):
            new = []
            for q in range(2 * n):
                lanes = slice(q * LANES, (q + 1) * LANES)
                slope = r.slope2[at, lanes]
                new.append((state[q][0] + fold(slope), state[q][1] + fold(slope * r.sp[at, lanes])))
            return tuple(new)

        state = strips(i * CELLS, body, ((zero, zero),) * (2 * n))
        for q in range(2 * n):
            for stat in range(2):
                row_at = (stat * n + q % n) * 8 + 4 * (q // n)
                r.slopes[pl.ds(row_at + i, 1), :] = (
                    total(state[q][stat]) * share - guess[stat][:, q * LANES : (q + 1) * LANES]
                )

    r.slopes[...] = jnp.zeros_like(r.slopes)
    loop(ipd, slope_sums)
    r.g5[0] = r.slopes[...].astype(BF16)

    everyone(r.g5, 4)


    gate_rows = min(D * 8, 2 * LANES)
    gate_blocks = D * 8 // gate_rows
    gate_at = lax.broadcasted_iota(jnp.int32, (gate_rows, LANES), 0)
    valid = lax.bitwise_and(gate_at, 7) < ipd
    every = 1.0 / (D * ipd)

    def gate_block(n):
        return pl.ds(pl.multiple_of(n * gate_rows, gate_rows), gate_rows)

    def lower_upper(buf, n):
        slots = gate_rows // 8
        both = buf[pl.ds(n * slots, slots)].reshape(gate_rows, LANES)
        return jnp.where(valid, both, 0.0), jnp.where(valid, pltpu.roll(both, gate_rows - 4, 0), 0.0)

    def gate_in(n, state):
        sum_lo, sum_hi = lower_upper(r.g3, n)
        pre = exact(sum_lo, r.gate_down[0:LANES, :]) + exact(sum_hi, r.gate_down[LANES:, :])
        r.gate_x[gate_block(n), :] = pre
        return state[0] + total(pre), state[1] + total(pre * pre)

    everyone_wait(r.g3, 2)
    zero1 = jnp.zeros((1, LANES), F32)
    first, second = lax.fori_loop(0, gate_blocks, gate_in, (zero1, zero1))
    gate_mean = first * every
    gate_scale = lax.rsqrt(second * every - gate_mean * gate_mean + EPS)

    def gate_out(n):
        at = gate_block(n)
        x = (r.gate_x[at, :] - gate_mean) * gate_scale
        h = r.gate_gain[...] * x + r.gate_shift[...]
        s = sigmoid(h)
        y = h * s
        r.gate_x[at, :] = x
        r.squeezed[at, :] = y
        r.gate_slope[at, :] = s + y - y * s

    loop(gate_blocks, gate_out)
    logits = exact(r.squeezed[0:8, :], r.gate_up[...]) + r.gate_bias[...]
    top = jnp.maximum(logits[:, :width], logits[:, width:])
    upper = jnp.exp(logits[:, :width] - top)
    lower = jnp.exp(logits[:, width:] - top)
    both = upper + lower
    r.att[:, 0:width] = upper / both
    r.att[:, width:two] = lower / both

    gm = Gather(1, lambda b, i: r.merged.at[rows_of(b, i)], lambda b: r.merged.at[block_rows(b)], ipd)

    def merge(i, state):
        att = r.att[pl.ds(i, 1), :]

        def body(at, k, carry):
            there = pl.ds(pl.multiple_of((ch * ipd + i) * CELLS + k * STRIP, STRIP), STRIP)
            left = (r.act2[at, 0:width] * att[:, 0:width]).astype(BF16)
            right = (r.act2[at, width:two] * att[:, width:two]).astype(BF16)
            both = (left.astype(F32) + right.astype(F32)).astype(BF16)
            r.merged[there, :] = both
            return carry + fold(both.astype(F32))

        return strips(i * CELLS, body, state)

    merged_sum = merge(0, zero8)
    gm.send(0)
    merged_sum = lax.fori_loop(1, ipd, merge, merged_sum)

    def turn_own(j):
        r.mt[:, rows_of(ch, j)] = flip(r.merged[rows_of(ch, j), :])

    loop(ipd, turn_own)

    def halves(value):
        high = value.astype(BF16)
        return high, (value - high.astype(F32)).astype(BF16)

    gram = dot(r.mt[:, block_rows(ch)], r.merged[block_rows(ch), :])
    gram_high, gram_low = halves(gram)
    high, rest = halves(total(merged_sum))
    low, last = halves(total(merged_sum) - high.astype(F32))
    means = jnp.concatenate([high, low, last, jnp.zeros((13, width), BF16)], axis=0)

    def expand_sums(k):
        weight = r.wx[k]
        square = dot(gram_high, weight) + dot(gram_low, weight)
        put(r.sums3.at[pl.ds(k, 1)], 0, total(dot(means, weight)))
        put(r.sums3.at[pl.ds(k, 1)], cw // LANES, total(fold(square * weight.astype(F32))))

    zero_c = jnp.zeros((8, cw), F32)
    loop(CH, expand_sums)
    r.r1[0] = r.sums3[ch]
    row(r.r1, 1, r.sums3)
    lax.fori_loop(1, ipd, lambda i, carry: (gm.send(i), carry)[1], 0)
    load_c.wait()
    r.acc[...] = jnp.zeros((16, cw), F32)
    row_sum(r.r1, 1, r.c1)
    column(r.c1, 0)

    for t in range(1, X):
        loop(2, lambda i: gm.from_peer(t, i))
    def turn_w(k):
        r.wxt[k] = flip(r.wx[k])

    loop(CH, turn_w)
    for p in range(width // LANES):
        at = slice(p * LANES, (p + 1) * LANES)
        r.gapt[at, :] = (r.gate_up[:, at] - r.gate_up[:, width + p * LANES : width + (p + 1) * LANES]).T
        r.downt[:, at] = r.gate_down[at, :].T
    column_wait(r.c1, 0)
    sums = jnp.sum(r.c1[...], axis=0)
    mean3, scale3 = moments(get(sums, 0, cw), get(sums, cw // LANES, cw))
    gain3, shift3 = r.third_gain[...], r.third_shift[...]
    lead3 = gain3 * scale3
    lift3 = shift3 - mean3 * lead3
    per3 = cw // LANES
    put(r.r2, 0, lead3 * scale3)
    put(r.r2, per3, lead3)
    put(r.r2, 2 * per3, lead3 * scale3 * mean3)
    row(r.r2, 0)

    def outputs(b, i):
        r.ex[rows_of(b, i), :] = dot(r.merged[rows_of(b, i), :], r.expand_weight[...])

        def body(at, k, state):
            shift, cross = state
            mask = wide(r.maskf[at, :], cw)
            x = r.ex[at, :]
            h = lead3 * x + lift3 + r.xv[at, :].astype(F32)
            s = sigmoid(h)
            y = h * s
            d = r.cv[at, :].astype(F32) * mask * (s + y - y * s)
            r.cv[at, :] = (mask * y).astype(BF16)
            r.dpre[at, :] = d
            r.de[at, :] = (lead3 * d).astype(BF16)
            return (shift + fold(d), cross + fold(d * x))

        shift, cross = strips((b * ipd + i) * CELLS, body, (zero_c, zero_c))
        r.acc[0:8, :] += shift
        r.acc[8:16, :] += cross
        at = rows_of(b, i)
        pltpu.make_async_copy(r.cv.at[at], r.block_out.at[at], r.store.at[0]).start()

    def part_merged(b, i):
        return dot(r.de[rows_of(b, i), :], r.wet[...])

    rs1.done()
    rs2 = Scatter(1, r.stage, r.inward2, r.outward, r.landed2, r.dm)
    for t in range(1, X):

        def far(i):
            gm.from_pass(t, i)
            outputs(block_of(t, False), i)
            rs2.mate_one(t, i, part_merged)
            if i >= 2:
                rs2.peer_one(t, i - 1, part_merged)
            outputs(block_of(t, True), i)
            if i + 2 < ipd:
                gm.from_peer(t, i + 2)
            if i == 0:
                rs2.peer_one(t, 0, part_merged)

        for i in range(ipd):
            far(i)
        rs2.peer_one(t, ipd - 1, part_merged)

    def near(i):
        gm.from_mate(i)
        outputs(block_of(0, False), i)
        rs2.mate_one(0, i, part_merged)

    loop(ipd, near)
    loop(ipd, lambda i: outputs(ch, i))
    shift = total(r.acc[0:8, :])
    put(r.c2, 0, shift)
    put(r.c2, cw // LANES, (total(r.acc[8:16, :]) - mean3 * shift) * scale3)
    everyone(r.c2, 6)
    rs2.own(part_merged)

    def turn_other(j):
        b = j // ipd
        b = jnp.where(b < ch, b, b + 1)
        at = b * ipd + j % ipd
        r.mt[:, image(at)] = flip(r.merged[image(at), :])

    loop(images - ipd, turn_other)
    everyone_wait(r.c2, 6)
    drain(r.r2.at[pl.ds(1, CH - 1)], r.row_recv.at[0])
    r.back3[...] = jnp.sum(r.c2[...].reshape(DP, CH, 4, LANES), axis=0)
    sums = r.back3[0]
    shift_grad, gain_grad = get(sums, 0, cw), get(sums, cw // LANES, cw)
    r.third_gain_grad[...] = gain_grad
    r.third_shift_grad[...] = shift_grad
    base3, slant3 = shift_grad * inverse, gain_grad * inverse
    slope3 = lead3 * scale3 * slant3
    flat3 = lead3 * base3 - mean3 * slope3

    r.mix[...] = jnp.zeros((width, width), F32)
    r.offset[...] = jnp.zeros((16, width), F32)

    def mix(q):
        b = (ch + q) % CH
        coefs, part = r.r2[q], r.back3[q]
        base, slant = get(part, 0, cw) * inverse, get(part, per3, cw) * inverse
        slope = get(coefs, 0, cw) * slant
        flat = get(coefs, per3, cw) * base - get(coefs, 2 * per3, cw) * slant
        r.mix[...] += dot((r.wx[b].astype(F32) * slope).astype(BF16), r.wxt[b])
        high = flat.astype(BF16)
        low = (flat - high.astype(F32)).astype(BF16)
        pair = jnp.concatenate([high, low, jnp.zeros((14, cw), BF16)], axis=0)
        r.offset[...] += dot(pair, r.wxt[b])

    loop(CH, mix)
    r.mixb[...] = r.mix[...].astype(BF16)

    offset = total(r.offset[...])
    away = offset + dot(r.merged[block_rows(ch), :], r.mixb[...])
    r.inward[0] = away.astype(BF16).reshape(ipd, CELLS, width)

    r.told[...] = jnp.zeros((16, LANES), F32)

    def finish_merged(i):
        rs2.arrive(i)

        def body(at, k, state):
            here = pl.ds(pl.multiple_of(k * SIDE, SIDE), SIDE)
            there = pl.ds(pl.multiple_of((ch * ipd + i) * CELLS + k * SIDE, SIDE), SIDE)
            away = wide(r.maskf[there, :], width) * r.inward[0, i, here, :].astype(F32)
            value = r.dm[at, :] + rs2.extra(i, here, slice(None)) - away
            r.dm[at, :] = value
            new = [state[0] + fold(value * (r.act2[at, 0:width] - r.act2[at, width:two]))]
            for g in range(2):
                lanes = slice(g * width, (g + 1) * width)
                part = value * r.slope2[at, lanes]
                new += [state[1 + 2 * g] + fold(part), state[2 + 2 * g] + fold(part * r.sp[at, lanes])]
            return tuple(new)

        gap, *parts = strips(i * CELLS, body, (zero8,) * 5, SIDE)
        att = r.att[pl.ds(i, 1), :]
        grad = att[:, 0:width] * att[:, width:two] * total(gap)
        n = width // LANES
        for q in range(n):
            r.told[pl.ds(4 * q + i, 1), :] = grad[:, q * LANES : (q + 1) * LANES]
        for g in range(2):
            for stat in range(2):
                part = total(parts[2 * g + stat]) * att[:, g * width : (g + 1) * width]
                for q in range(n):
                    at = 8 + (2 * stat + g) * n + q
                    r.told[at : at + 1, :] += part[:, q * LANES : (q + 1) * LANES]

    loop(ipd, finish_merged)
    r.r4[0] = r.told[8:16, :]
    row(r.r4, 2)
    r.g4[0] = r.told[0:8, :]
    everyone(r.g4, 3)
    lax.fori_loop(ipd // 2, ipd, lambda i, carry: (gx.send(i), carry)[1], 0)
    row_sum(r.r4, 2, r.c4)
    column(r.c4, 3)

    piece = width // DP
    et = r.es.dtype
    def piece_rows(d):
        return pl.ds(pl.multiple_of(((dp + d) % DP) * piece, piece), piece)

    def grow(b):
        def body(at, k, carry):
            mask = wide(r.maskf[at, :], cw)
            d = lead3 * r.dpre[at, :] - mask * (flat3 + r.ex[at, :] * slope3)
            r.de[at, :] = d.astype(BF16)
            return carry

        for i in range(ipd):
            strips((b * ipd + i) * CELLS, body, 0)
        value = dot(r.mt[:, block_rows(b)], r.de[block_rows(b), :])
        r.eg[...] += value

    r.eg[...] = jnp.zeros((width, cw), F32)
    loop(CH, grow)
    r.es[...] = r.eg[...].astype(et)

    for d in range(1, DP):
        remote(r.es.at[piece_rows(d)], r.ebuf.at[DP - d], r.eg_send.at[0], r.eg_recv.at[0], across(d)).start()

    everyone_wait(r.g5, 4)
    everyone_wait(r.g4, 3)

    def gate_back(n, state):
        at = gate_block(n)
        grad_lo, grad_hi = lower_upper(r.g4, n)
        grad = exact(grad_lo, r.gapt[0:LANES, :]) + exact(grad_hi, r.gapt[LANES:width, :])
        grad = grad * r.gate_slope[at, :]
        r.grad_down[at, :] = grad
        return state[0] + total(grad), state[1] + total(grad * r.gate_x[at, :])

    gate_shift_all, gate_gain_all = lax.fori_loop(0, gate_blocks, gate_back, (zero1, zero1))
    lead = r.gate_gain[...] * gate_scale

    def gate_norm_back(n, state):
        at = gate_block(n)
        grad = r.grad_down[at, :] - gate_shift_all * every - r.gate_x[at, :] * (gate_gain_all * every)
        grad = jnp.where(valid, lead * grad, 0.0)
        r.grad_down[at, :] = grad
        summary = exact(grad, r.downt[...])
        slots = gate_rows // 8

        @pl.when(n == 0)
        def _():
            r.grad_summary[...] = summary[0:8, :]

        slopes = r.g5[pl.ds(n * slots, slots)].astype(F32)
        new = []
        for stat in range(2):
            for p in range(width // LANES):
                part = summary[:, p * LANES : (p + 1) * LANES]
                part = (part + pltpu.roll(part, 4, 0)).reshape(slots, 8, LANES)
                k = stat * (width // LANES) + p
                new.append(state[k] + jnp.sum(part * slopes[:, 8 * k : 8 * k + 8, :], axis=0))
        new.append(state[-1] + total(summary))
        return tuple(new)

    n_half = width // LANES
    zero = jnp.zeros((8, LANES), F32)
    *flats, summed = lax.fori_loop(
        0, gate_blocks, gate_norm_back, (zero,) * (2 * n_half) + (jnp.zeros((1, width), F32),)
    )
    guess = slope_guess()
    column_wait(r.c4, 3)
    told = jnp.sum(r.c4[...], axis=0)

    def second_sum(stat):
        parts = []
        for q in range(2 * n_half):
            flat = flats[stat * n_half + q % n_half]
            flat = total(flat[4 * (q // n_half) : 4 * (q // n_half) + 4, :])
            at = 2 * n_half * stat + q
            lanes = slice(q % n_half * LANES, (q % n_half + 1) * LANES)
            flat = flat + guess[stat][:, q * LANES : (q + 1) * LANES] * summed[:, lanes]
            parts.append(flat + told[at : at + 1, :])
        return jnp.concatenate(parts, axis=1)

    shift_grad2, gain_grad2 = second_sum(0), second_sum(1)
    lead2, base2, slant2 = gain2 * scale2, shift_grad2 * inverse, gain_grad2 * inverse

    def splits_back(i):
        att = r.att[pl.ds(i, 1), :]
        flat = r.grad_summary[pl.ds(i, 1), :] * wide(r.share[pl.ds(i, 1), :], width)

        def body(at, k, carry):
            there = pl.ds(pl.multiple_of((ch * ipd + i) * CELLS + k * STRIP, STRIP), STRIP)
            put_at = pl.ds(pl.multiple_of(SIDE + k * STRIP, SIDE), STRIP)
            mask = r.maskf[there, :]
            for q in range(two // LANES):
                g, p = q // n_half, q % n_half
                lanes = slice(q * LANES, (q + 1) * LANES)
                here = slice(p * LANES, (p + 1) * LANES)
                d = (r.dm[at, here] * att[:, lanes] + flat[:, here]) * r.slope2[at, lanes]
                d = mask * lead2[:, lanes] * (d - base2[:, lanes] - r.sp[at, lanes] * slant2[:, lanes])
                r.act2[at, lanes] = d
                before = jnp.where(not_first, pltpu.roll(d, 1, 0), 0.0)
                after = jnp.where(not_last, pltpu.roll(d, STRIP - 1, 0), 0.0)
                for n, value in enumerate((after, d, before)):
                    start = n * width + p * LANES
                    r.dsh[g, i, put_at, start : start + LANES] = value.astype(BF16)
            return carry

        strips(i * CELLS, body, 0)

    loop(ipd, splits_back)

    drain(r.stage, r.rs_core_send.at[1])

    def turn_d(i):
        for g in range(2):
            r.stage[g, i] = r.act2[image(i), g * width : (g + 1) * width].T.astype(BF16)

    loop(ipd, turn_d)
    per = CH // 2
    wide3 = 3 * half
    for k in range(3):
        for g in range(2):
            right = r.act[g, :, k * SIDE : k * SIDE + CELLS, :].reshape(own_rows, wide3)
            value = dot(jnp.concatenate([r.stage[g, i] for i in range(ipd)], axis=1), right)
            if c.split_inside:
                for q in range(per):
                    b = g * per + q
                    r.ss[k, b % 2, b // 2] = value[q * m2 : (q + 1) * m2, :].astype(BF16)
            else:
                r.split_part[g * width : (g + 1) * width, k * wide3 : (k + 1) * wide3] = value
        if c.split_inside:
            remote(r.ss.at[k, 1 - core], r.sin.at[k], r.sg_send.at[0, k], r.sg_recv.at[0, k], mate).start()
    slab = m2 // DP
    Z = DP // 2
    turn, side = dp // 2, dp % 2

    def ring(e):
        return (((turn + e) % Z) * 2 + side, ch)

    other = (dp + 1 - 2 * side, ch)

    def split_cores(k):
        drain(r.sin.at[k], r.sg_recv.at[0, k])
        for t in range(X):
            value = (r.ss[k, core, t].astype(F32) + r.sin[k, t].astype(F32)).astype(BF16)
            value = value.reshape(Z, 2, slab, wide3)
            for p in range(2):
                r.sc[k, p, :, t] = value[:, p]
        remote(r.sc.at[k, 1 - side], r.sp1.at[k], r.sg_send.at[1, k], r.sg_recv.at[1, k], other).start()

    def split_pairs(k):
        drain(r.sp1.at[k], r.sg_recv.at[1, k])
        r.sy[k] = (r.sc[k, side].astype(F32) + r.sp1[k].astype(F32)).astype(BF16)
        for e in range(1, Z):
            remote(
                r.sy.at[k, (turn + e) % Z], r.sz.at[k, Z - e], r.sg_send.at[2, k], r.sg_recv.at[2, k], ring(e)
            ).start()

    def split_chips(k):
        drain(r.sz.at[k, pl.ds(1, Z - 1)], r.sg_recv.at[2, k])
        for t in range(X):
            there = (chip + t) % X
            value = r.sy[k, turn, there].astype(F32)
            for e in range(1, Z):
                value = value + r.sz[k, e, there].astype(F32)
            r.sx[k, t] = value.astype(BF16)
            if t:
                remote(r.sx.at[k, t], r.sxin.at[k, X - t], r.sg_send.at[3, k], r.sg_recv.at[3, k], peer(t)).start()

    def split_out(k):
        drain(r.sxin.at[k, pl.ds(1, X - 1)], r.sg_recv.at[3, k])
        value = r.sx[k, 0].astype(F32)
        for t in range(1, X):
            value = value + r.sxin[k, t].astype(F32)
        r.so[k, 0] = value.astype(BF16)
        for d in range(1, DP):
            remote(r.so.at[k, 0], r.so.at[k, DP - d], r.sg_send.at[4, k], r.sg_recv.at[4, k], across(d)).start()

    def split_step(step, k):
        if c.split_inside:
            step(k)

    def first_back(i, many, state):
        size = many * CELLS
        there = pl.ds(pl.multiple_of((ch * ipd + i) * CELLS, CELLS), size)
        here = slice(i * CELLS, i * CELLS + size)
        out = []
        for g in range(2):
            lanes = slice(g * half, (g + 1) * half)
            left = jnp.concatenate(
                [
                    r.dsh[g, i : i + many, (2 - k) * SIDE : (2 - k) * SIDE + CELLS, :].reshape(size, 3 * width)
                    for k in range(3)
                ],
                axis=1,
            )
            value = dot(left, r.wt[g]) * r.slope1[here, lanes]
            r.dh1[there, lanes] = value.astype(BF16)
            out.append((state[g][0] + fold(value), state[g][1] + fold(value * r.red[here, lanes])))
        return tuple(out)

    zero_h = jnp.zeros((8, half), F32)
    gd = Gather(2, lambda b, i: r.dh1.at[rows_of(b, i)], lambda b: r.dh1.at[block_rows(b)], ipd)
    state = ((zero_h, zero_h), (zero_h, zero_h))
    for i in range(2):
        state = first_back(i, 1, state)
        gd.send(i)
        if i == 0:
            for k in range(3):
                split_step(split_cores, k)
    if ipd > 2:
        state = first_back(2, ipd - 2, state)
    for g in range(2):
        r.g6[0, g : g + 1, :] = total(state[g][0])
        r.g6[0, 2 + g : 3 + g, :] = total(state[g][1])
    everyone(r.g6, 5)
    lax.fori_loop(2, ipd, lambda i, carry: (gd.send(i), carry)[1], 0)

    def pass_x(i):
        for t in range(1, X):
            gx.from_peer(t, i)

    loop(ipd, pass_x)

    drain(r.ebuf.at[pl.ds(1, DP - 1)], r.eg_recv.at[0])
    value = r.eg[piece_rows(0), :]
    for d in range(1, DP):
        value = value + r.ebuf[d].astype(F32)
    r.eo[0] = value.astype(et)
    for d in range(1, DP):
        remote(r.eo.at[0], r.eo.at[DP - d], r.eg_send.at[1], r.eg_recv.at[1], across(d)).start()
    for k in range(3):
        split_step(split_pairs, k)
    everyone_wait(r.g6, 5)
    sums = jnp.sum(r.g6[...], axis=0)
    shift_grad, gain_grad = get(sums, 0, width), get(sums, 2, width)
    lead1, base1, slant1 = gain1 * scale1, shift_grad * inverse, gain_grad * inverse

    r.rg[...] = jnp.zeros((cw, width), F32)

    def from_x(i):
        gx.from_mate(i)
        for t in range(1, X):
            gx.from_pass(t, i)

    loop(ipd, from_x)
    gx.done()

    def reduced_back(b, i):
        def body(at, k, carry):
            mask = wide(r.maskf[at, :], width)
            d = mask * lead1 * (r.dh1[at, :].astype(F32) - base1 - r.xh1[at, :].astype(F32) * slant1)
            r.xh1[at, :] = d.astype(BF16)
            return carry

        strips((b * ipd + i) * CELLS, body, 0)
        r.rg[...] += dot(r.xt[b * ipd + i], r.xh1[rows_of(b, i), :])

    def input_back(b, i):
        at = rows_of(b, i)
        r.xv[at, :] = (r.dpre[at, :] + dot(r.xh1[at, :], r.wrt[...])).astype(BF16)
        pltpu.make_async_copy(r.xv.at[at], r.inputs_grad.at[at], r.store.at[1]).start()

    loop(ipd, lambda i: reduced_back(ch, i))

    def from_mate(i):
        gd.from_mate(i)
        reduced_back(block_of(0, False), i)

    loop(ipd, from_mate)
    split_step(split_chips, 0)
    for t in range(1, X):

        def from_peer(i):
            gd.from_peer(t, i)
            reduced_back(block_of(t, True), i)

        loop(ipd, from_peer)
    split_step(split_chips, 1)
    for t in range(1, X):

        def from_pass(i):
            gd.from_pass(t, i)
            reduced_back(block_of(t, False), i)

        loop(ipd, from_pass)

    split_step(split_chips, 2)
    if c.reduce_inside:
        r.rs[...] = r.rg[...].T.astype(r.rs.dtype)
        for d in range(1, DP):
            remote(r.rs.at[piece_rows(d)], r.rbuf.at[DP - d], r.rg_send.at[0], r.rg_recv.at[0], across(d)).start()
    else:
        r.reduce_part[...] = r.rg[...].T
    split_step(split_out, 0)
    loop(ipd, lambda i: input_back(ch, i))
    split_step(split_out, 1)
    loop(ipd, lambda i: input_back(block_of(0, False), i))
    split_step(split_out, 2)
    if c.reduce_inside:
        groups = DP // CH
        goal = dp // groups
        drain(r.rbuf.at[pl.ds(1, DP - 1)], r.rg_recv.at[0])
        value = r.rs[piece_rows(0), :].astype(F32)
        for d in range(1, DP):
            value = value + r.rbuf[d].astype(F32)
        r.rsum[...] = value.astype(r.rsum.dtype)
        slot = r.rall.at[dp % groups, ch]
        for d in range(1, DP):
            remote(r.rsum, slot, r.rg_send.at[1], r.rg_recv.at[1], ((dp + d) % DP, goal)).start()

        @pl.when(goal == ch)
        def _():
            pltpu.make_async_copy(r.rsum, slot, r.rg_recv.at[1]).start()

        @pl.when(goal != ch)
        def _():
            remote(r.rsum, slot, r.rg_send.at[2], r.rg_recv.at[1], (dp, goal)).start()

    for t in range(1, X):
        loop(ipd, lambda i: input_back(block_of(t, True), i))
    for t in range(1, X):
        loop(ipd, lambda i: input_back(block_of(t, False), i))
    r.second_gain_grad[...] = exact_nt(gain_grad2, pick2)
    r.second_shift_grad[...] = exact_nt(shift_grad2, pick2)
    r.first_gain_grad[...] = exact_nt(gain_grad, pick1)
    r.first_shift_grad[...] = exact_nt(shift_grad, pick1)
    r.gate_gain_grad[...] = exact_nt(gate_gain_all, pickg)
    r.gate_shift_grad[...] = exact_nt(gate_shift_all, pickg)

    def gate_grads(n, state):
        at = gate_block(n)
        sum_lo, sum_hi = lower_upper(r.g3, n)
        grad_lo, grad_hi = lower_upper(r.g4, n)
        picked = exact_nt(r.grad_down[at, :], pickg)
        down = jnp.concatenate([exact_tn(picked, sum_lo), exact_tn(picked, sum_hi)], axis=1)
        squeezed = r.squeezed[at, :]
        up = jnp.concatenate([exact_tn(squeezed, grad_lo), exact_tn(squeezed, grad_hi)], axis=1)
        bias = jnp.concatenate([total(grad_lo), total(grad_hi)], axis=1)
        return state[0] + down, state[1] + up, state[2] + bias

    down, up, bias = lax.fori_loop(
        0, gate_blocks, gate_grads,
        (jnp.zeros((mg, width), F32), jnp.zeros((inner, width), F32), jnp.zeros((1, width), F32)),
    )
    r.down_grad[...] = down
    r.up_grad[...] = exact_nt(jnp.concatenate([up, -up], axis=1), pick2)
    r.bias_grad[...] = exact_nt(jnp.concatenate([bias, -bias], axis=1), pick2)

    drain(r.eo.at[pl.ds(1, DP - 1)], r.eg_recv.at[1])
    for d in range(DP):
        r.expand_grad[piece_rows(d), :] = r.eo[d].astype(F32)
    if c.reduce_inside:
        drain(r.rall, r.rg_recv.at[1])
        for s in range(groups):
            for q in range(CH):
                r.reduce_grad[s * piece : (s + 1) * piece, q * cw : (q + 1) * cw] = r.rall[s, q].astype(F32)
    if c.split_inside:
        for k in range(3):
            drain(r.so.at[k, pl.ds(1, DP - 1)], r.sg_recv.at[4, k])
            for p in range(3):
                at = slice(p * half, (p + 1) * half)
                block = jnp.concatenate(
                    [r.so[k, (d - dp + DP) % DP, :, at].astype(F32) for d in range(DP)], axis=0
                )
                r.split_grad[3 * k + p] = block.T

    for k, buf in enumerate((r.g1, r.g2, r.g3, r.g4, r.g5, r.g6, r.c2, r.g0)):
        everyone_done(buf, k)
    column_done(r.c1, 0)
    row_done(r.r1, 1)
    row_done(r.r2, 0)
    row_done(r.r4, 2)
    column_done(r.c4, 3)
    rs2.done(False)
    for gather in (gm, gd) + shares:
        gather.done()
    drain(r.pbuf.at[pl.ds(1, CH - 1)], r.par_send.at[0])
    drain(r.ebuf.at[pl.ds(1, DP - 1)], r.eg_send.at[0])
    drain(r.ebuf.at[pl.ds(1, DP - 1)], r.eg_send.at[1])
    if c.reduce_inside:
        drain(r.rbuf.at[pl.ds(1, DP - 1)], r.rg_send.at[0])
        drain(r.rbuf.at[pl.ds(1, DP - 1)], r.rg_send.at[1])

        @pl.when(goal != ch)
        def _():
            drain(r.rsum, r.rg_send.at[2])

    if c.split_inside:
        for k in range(3):
            drain(r.sin.at[k], r.sg_send.at[0, k])
            drain(r.sp1.at[k], r.sg_send.at[1, k])
            drain(r.sz.at[k, pl.ds(1, Z - 1)], r.sg_send.at[2, k])
            drain(r.sxin.at[k, pl.ds(1, X - 1)], r.sg_send.at[3, k])
            drain(r.so.at[k, pl.ds(1, DP - 1)], r.sg_send.at[4, k])
    drain(r.cv, r.store.at[0])
    drain(r.xv, r.store.at[1])


def hand_over(*refs):
    count = (len(refs) - 1) // 3
    sources, results, places, sems = refs[:count], refs[count : 2 * count], refs[2 * count : -1], refs[-1]
    copies = []
    for source, result, place in zip(sources, results, places):
        rows = source.shape[0]
        parts = 2 if rows >= 1024 else 1
        for p in range(parts):
            at = pl.ds(p * (rows // parts), rows // parts)
            k = len(copies)
            inward = pltpu.make_async_copy(source.at[at], place.at[at], sems.at[k, 0])
            copies.append((inward, pltpu.make_async_copy(place.at[at], result.at[at], sems.at[k, 1])))
            inward.start()
    for inward, outward in copies:
        inward.wait()
        outward.start()
    for inward, outward in copies:
        outward.wait()


ARGS = (
    "inputs", "resolution", "reduce_weight", "first_gain", "first_shift", "split_weight", "second_gain",
    "second_shift", "gate_down", "gate_gain", "gate_shift", "gate_up", "gate_bias", "expand_weight",
    "third_gain", "third_shift", "cotangent",
)


def per_device(*arrays):
    a = dict(zip(ARGS, arrays))
    c = types.SimpleNamespace()
    c.DP, c.CH = lax.axis_size("dp"), lax.axis_size("chan")
    c.X, c.D = c.CH // 2, c.DP * c.CH
    c.images = a["resolution"].shape[0]
    c.ipd = c.images // c.CH
    rows, c.cw = a["inputs"].shape
    c.width = a["reduce_weight"].shape[1]
    c.inner = a["gate_down"].shape[1]
    c.m1, c.m2, c.mg = c.width // c.CH, 2 * c.width // c.CH, c.inner // c.CH
    half, two = c.width // 2, 2 * c.width
    taps = 9 * half
    piece = c.width // c.DP
    piece_type = BF16 if piece % 16 == 0 else F32
    c.reduce_inside = c.DP % c.CH == 0 and piece % 8 == 0
    c.share = taps % (16 * c.DP) == 0 and c.width % (16 * c.DP) == 0
    c.split_inside = c.m2 % (16 * c.DP) == 0 and c.DP % 2 == 0 and c.DP > 2
    own = c.ipd * CELLS
    DP, CH, X, D, ipd, cw, width = c.DP, c.CH, c.X, c.D, c.ipd, c.cw, c.width
    for name in ARGS:
        if a[name].ndim == 1 and name != "resolution":
            a[name] = a[name].reshape(1, -1)
    a["split_weight"] = a["split_weight"].reshape(taps, c.m2)
    sds = jax.ShapeDtypeStruct
    outs = dict(
        block_out=sds((rows, cw), BF16),
        inputs_grad=sds((rows, cw), BF16),
        first_gain_grad=sds((1, c.m1), F32),
        first_shift_grad=sds((1, c.m1), F32),
        second_gain_grad=sds((1, c.m2), F32),
        second_shift_grad=sds((1, c.m2), F32),
        down_grad=sds((c.mg, width), F32),
        gate_gain_grad=sds((1, c.mg), F32),
        gate_shift_grad=sds((1, c.mg), F32),
        up_grad=sds((c.inner, c.m2), F32),
        bias_grad=sds((1, c.m2), F32),
        expand_grad=sds((width, cw), F32),
        third_gain_grad=sds((1, cw), F32),
        third_shift_grad=sds((1, cw), F32),
    )
    if c.reduce_inside:
        outs["reduce_grad"] = sds((c.m1, CH * cw), F32)
    else:
        outs["reduce_part"] = sds((width, cw), F32)
    if c.split_inside:
        outs["split_grad"] = sds((9, half, c.m2), F32)
    else:
        outs["split_part"] = sds((two, taps), F32)
    V = pltpu.VMEM
    dma = lambda *shape: pltpu.SemaphoreType.DMA(shape)
    scratch = dict(
        xv=V((rows, cw), BF16), cv=V((rows, cw), BF16), wr=V((cw, width), BF16), wrt=V((width, cw), BF16),
        wet=V((cw, width), BF16), xt=V((c.images, cw, CELLS), BF16), mt=V((width, rows), BF16),
        maskf=V((rows, LANES), F32), area=V((c.images, LANES), F32), pbuf=V((CH, 8, two), F32),
        red=V((own, width), F32), slope1=V((own, width), F32), xh1=V((rows, width), BF16),
        act=V((2, ipd, TALL, 3 * half), BF16), dsh=V((2, ipd, TALL, 3 * width), BF16),
        wg=V((CH, taps, c.m2), BF16), wx=V((CH, width, cw), BF16), wf=V((2, taps, width), BF16), wt=V((2, 9 * width, half), BF16),
        sp=V((own, two), F32), slope2=V((own, two), F32), act2=V((own, two), F32), share=V((8, LANES), F32),
        gate_x=V((D * 8, LANES), F32), squeezed=V((D * 8, LANES), F32), gate_slope=V((D * 8, LANES), F32),
        grad_down=V((D * 8, LANES), F32), grad_summary=V((8, width), F32), att=V((8, two), F32),
        merged=V((rows, width), BF16), ex=V((rows, cw), F32), acc=V((16, cw), F32),
        dpre=V((rows, cw), F32), de=V((rows, cw), BF16), dm=V((own, width), F32), dh1=V((rows, width), BF16),

        eg=V((width, cw), F32), es=V((width, cw), piece_type), ebuf=V((DP, piece, cw), piece_type),
        eo=V((DP, piece, cw), piece_type), rg=V((cw, width), F32),
        all_send=dma(8), all_recv=dma(8), col_send=dma(4), col_recv=dma(4), row_send=dma(3), row_recv=dma(3),
        rs_core_send=dma(2), rs_core_recv=dma(2, X, ipd), rs_chip_send=dma(2), rs_chip_recv=dma(2, X, ipd),
        ag_core_send=dma(3), ag_core_recv=dma(3, ipd), ag_chip_send=dma(3, X), ag_chip_recv=dma(3, X, ipd),
        ag_pass_send=dma(3, X), ag_pass_recv=dma(3, X, ipd), sh_core_send=dma(2), sh_core_recv=dma(2),
        sh_chip_send=dma(2, X), sh_chip_recv=dma(2, X), sh_col_send=dma(2, X), sh_col_recv=dma(2, X, DP),
        sh_pass_send=dma(2, X), sh_pass_recv=dma(2, X), par_send=dma(1), par_recv=dma(CH),
        eg_send=dma(2), eg_recv=dma(2), rg_send=dma(3), rg_recv=dma(2), sg_send=dma(5, 3), sg_recv=dma(5, 3),
        load=dma(2 + 2 * X), store=dma(2),
    )
    for name, count in (
        ("stage", X), ("inward", X), ("outward", X - 1), ("landed", X - 1), ("inward2", X), ("landed2", X - 1)
    ):
        scratch[name] = V((count, ipd, CELLS, width), BF16)
    for k in range(2, 5):
        scratch[f"g{k}"] = V((D, 8, LANES), F32)
    scratch["g0"] = V((D, 4, LANES), F32)
    scratch["g1"] = V((D, 4, LANES), F32)
    scratch["r4"] = V((CH, 8, LANES), F32)
    scratch["c4"] = V((DP, 8, LANES), F32)
    scratch["g5"] = V((D, 16 * width // LANES, LANES), BF16)
    scratch["told"] = V((16, LANES), F32)
    scratch["slopes"] = V((16 * width // LANES, LANES), F32)
    scratch["back3"] = V((CH, 4, LANES), F32)
    scratch["sums3"] = V((CH, 4, LANES), F32)
    scratch["c1"] = V((DP, 4, LANES), F32)
    scratch["r1"] = V((CH, 4, LANES), F32)
    scratch["r2"] = V((CH, 8, LANES), F32)
    scratch["mix"] = V((width, width), F32)
    scratch["mixb"] = V((width, width), BF16)
    scratch["offset"] = V((16, width), F32)
    scratch["gapt"] = V((width, LANES), F32)
    scratch["downt"] = V((LANES, width), F32)
    scratch["wxt"] = V((CH, cw, width), BF16)
    scratch["c2"] = V((D, 4, LANES), F32)
    scratch["g6"] = V((D, 4, LANES), F32)
    if c.reduce_inside:
        scratch.update(
            rs=V((width, cw), piece_type), rbuf=V((DP, piece, cw), piece_type), rsum=V((piece, cw), piece_type),
            rall=V((DP // CH, CH, piece, cw), piece_type),
        )
    if c.split_inside:
        slab = c.m2 // DP
        scratch.update(
            ss=V((3, 2, X, c.m2, 3 * half), BF16), sin=V((3, X, c.m2, 3 * half), BF16),
            sc=V((3, 2, c.DP // 2, X, slab, 3 * half), BF16), sp1=V((3, c.DP // 2, X, slab, 3 * half), BF16),
            sy=V((3, c.DP // 2, X, slab, 3 * half), BF16), sz=V((3, c.DP // 2, X, slab, 3 * half), BF16),
            sx=V((3, X, slab, 3 * half), BF16), sxin=V((3, X, slab, 3 * half), BF16),
            so=V((3, c.DP, slab, 3 * half), BF16),
        )
    anywhere = pl.BlockSpec(memory_space=pl.ANY)
    vmem = pl.BlockSpec(memory_space=pltpu.VMEM)
    spec = dict(
        inputs=anywhere, cotangent=anywhere, reduce_weight=anywhere, block_out=anywhere, inputs_grad=anywhere,
        resolution=pl.BlockSpec(memory_space=pltpu.SMEM),
    )
    names = tuple(ARGS) + tuple(outs) + tuple(scratch)
    results = pl.pallas_call(
        functools.partial(kernel, c, names),
        out_shape=tuple(outs.values()),
        in_specs=[spec.get(name, vmem) for name in ARGS],
        out_specs=tuple(spec.get(name, vmem) for name in outs),
        scratch_shapes=list(scratch.values()),
        compiler_params=pltpu.CompilerParams(
            collective_id=0, has_side_effects=True, vmem_limit_bytes=62 * 2**20
        ),
        name="block",
    )(*[a[name] for name in ARGS])
    results = pl.pallas_call(
        hand_over,
        out_shape=tuple(outs.values()),
        in_specs=[anywhere] * len(outs),
        out_specs=tuple(anywhere for _ in outs),
        scratch_shapes=[V(v.shape, v.dtype) for v in outs.values()] + [dma(4 * len(outs), 2)],
        compiler_params=pltpu.CompilerParams(vmem_limit_bytes=62 * 2**20),
        name="results",
    )(*results)
    o = dict(zip(outs, results))
    if not c.reduce_inside:
        place = lax.axis_index("chan")
        part = lax.psum(o["reduce_part"], "dp")
        part = lax.all_gather(part, "chan", axis=1, tiled=True)
        o["reduce_grad"] = lax.dynamic_slice_in_dim(part, place * c.m1, c.m1, 0)
    if not c.split_inside:
        place = lax.axis_index("chan")
        part = lax.psum(o["split_part"], ("dp", "chan"))
        part = lax.dynamic_slice_in_dim(part, place * c.m2, c.m2, 0)
        o["split_grad"] = part.T.reshape(9, half, c.m2)
    flat = lambda name: o[name].reshape(-1)
    return (
        o["block_out"], o["inputs_grad"], o["reduce_grad"].T, flat("first_gain_grad"), flat("first_shift_grad"),
        o["split_grad"], flat("second_gain_grad"), flat("second_shift_grad"), o["down_grad"].T,
        flat("gate_gain_grad"), flat("gate_shift_grad"), o["up_grad"], flat("bias_grad"), o["expand_grad"],
        flat("third_gain_grad"), flat("third_shift_grad"),
    )


def solution(mesh):
    placed = (
        P("dp", "chan"), P("dp"), P(), P("chan"), P("chan"), P(None, None, "chan"), P("chan"), P("chan"),
        P(), P(), P(), P(), P(), P(None, "chan"), P("chan"), P("chan"), P("dp", "chan"),
    )
    return jax.shard_map(
        per_device,
        mesh=mesh,
        in_specs=placed,
        out_specs=(
            P("dp", "chan"), P("dp", "chan"), P(None, "chan"), P("chan"), P("chan"), P(None, None, "chan"),
            P("chan"), P("chan"), P(None, "chan"), P("chan"), P("chan"), P(None, "chan"), P("chan"),
            P(None, "chan"), P("chan"), P("chan"),
        ),
        check_vma=False,
    )
```

```python
import functools
import types

import jax
import jax.numpy as jnp
from jax import lax
from jax.experimental import pallas as pl
from jax.experimental.pallas import tpu as pltpu
from jax.sharding import PartitionSpec as P

SIDE = 16
CELLS = SIDE * SIDE
TALL = CELLS + 2 * SIDE
LANES = 128
EPS = 1e-05
HIGHEST = lax.Precision.HIGHEST
F32 = jnp.float32
BF16 = jnp.bfloat16
MESH = pl.DeviceIdType.MESH
STRIP = 64


def wide(mask, width):
    return mask if width == LANES else jnp.concatenate([mask] * (width // LANES), axis=1)


def fold(values):
    return jnp.sum(values.reshape(values.shape[0] // 8, 8, values.shape[1]), axis=0)


def total(values):
    return jnp.sum(values, axis=0, keepdims=True)


def sigmoid(values):
    return 0.5 * jnp.tanh(0.5 * values) + 0.5


def dot(left, right):
    return jnp.dot(left, right, preferred_element_type=F32)


def exact(left, right):
    return jnp.dot(left, right, precision=HIGHEST, preferred_element_type=F32)


def exact_nt(left, right):
    return lax.dot_general(
        left, right, (((1,), (1,)), ((), ())), precision=HIGHEST, preferred_element_type=F32
    )


def exact_tn(left, right):
    return lax.dot_general(
        left, right, (((0,), (0,)), ((), ())), precision=HIGHEST, preferred_element_type=F32
    )


def flip(values):
    return values.astype(F32).T.astype(values.dtype)


def put(ref, row, vector):
    for part in range(vector.shape[1] // LANES):
        ref[0, row + part : row + part + 1, :] = vector[:, part * LANES : (part + 1) * LANES]


def get(block, row, width):
    parts = [block[row + q : row + q + 1, :] for q in range(width // LANES)]
    return parts[0] if len(parts) == 1 else jnp.concatenate(parts, axis=1)


def kernel(c, names, *refs):
    r = types.SimpleNamespace(**dict(zip(names, refs)))
    DP, CH, X, D, ipd, images = c.DP, c.CH, c.X, c.D, c.ipd, c.images
    width, cw, inner, m1, m2, mg = c.width, c.cw, c.inner, c.m1, c.m2, c.mg
    half, two = width // 2, 2 * width
    own_rows = ipd * CELLS
    taps = 9 * half
    dp = lax.axis_index("dp")
    ch = lax.axis_index("chan")
    core = ch % 2
    chip = ch // 2
    mate = (dp, ch + 1 - 2 * core)
    f0 = ((0, 0), (0, 0))

    def remote(src, dst, send, recv, device):
        return pltpu.make_async_remote_copy(
            src_ref=src, dst_ref=dst, send_sem=send, recv_sem=recv, device_id=device, device_id_type=MESH
        )

    def drain(ref, sem):
        pltpu.make_async_copy(ref, ref, sem).wait()

    def loop(count, body):
        def step(i, carry):
            body(i)
            return carry

        lax.fori_loop(0, count, step, 0)

    def peer(t):
        return (dp, ((chip + t) % X) * 2 + core)

    def across(d):
        return ((dp + d) % DP, ch)

    def block_of(t, same):
        return ((chip + t) % X) * 2 + (core if same else 1 - core)

    def rows_of(b, i):
        return pl.ds(pl.multiple_of((b * ipd + i) * CELLS, CELLS), CELLS)

    def block_rows(b):
        return pl.ds(pl.multiple_of(b * own_rows, own_rows), own_rows)

    def image(i):
        return pl.ds(pl.multiple_of(i * CELLS, CELLS), CELLS)

    def strips(base, body, carry, size=STRIP):
        def step(k, state):
            return body(pl.ds(pl.multiple_of(base + k * size, size), size), k, state)

        return lax.fori_loop(0, CELLS // size, step, carry)

    def everyone(buf, k, message=None):
        message = buf.at[0] if message is None else message

        def one(j, carry):
            d, q = j // CH, j % CH
            slot = ((DP - d) % DP) * CH + (CH - q) % CH
            remote(buf.at[0], buf.at[slot], r.all_send.at[k], r.all_recv.at[k], ((dp + d) % DP, (ch + q) % CH)).start()
            return carry

        lax.fori_loop(1, D, one, 0)

    def everyone_wait(buf, k):
        drain(buf.at[pl.ds(1, D - 1)], r.all_recv.at[k])

    def everyone_wait_on(buf, sem):
        drain(buf.at[pl.ds(1, D - 1)], sem)

    def everyone_done(buf, k):
        drain(buf.at[pl.ds(1, D - 1)], r.all_send.at[k])

    def column(buf, k):
        for d in range(1, DP):
            remote(buf.at[0], buf.at[DP - d], r.col_send.at[k], r.col_recv.at[k], across(d)).start()

    def row(buf, k, source=None):
        for q in range(1, CH):
            src = buf.at[0] if source is None else source.at[(ch + q) % CH]
            remote(src, buf.at[CH - q], r.row_send.at[k], r.row_recv.at[k], (dp, (ch + q) % CH)).start()

    def row_sum(buf, k, column_buf):
        drain(buf.at[pl.ds(1, CH - 1)], r.row_recv.at[k])
        column_buf[0] = jnp.sum(buf[...], axis=0)

    def row_done(buf, k):
        drain(buf.at[pl.ds(1, CH - 1)], r.row_send.at[k])

    def column_wait(buf, k):
        drain(buf.at[pl.ds(1, DP - 1)], r.col_recv.at[k])

    def column_done(buf, k):
        drain(buf.at[pl.ds(1, DP - 1)], r.col_send.at[k])

    class Scatter:
        def __init__(self, k, stage, inward, outward, landed, keep):
            self.k, self.stage, self.inward = k, stage, inward
            self.outward, self.landed, self.keep = outward, landed, keep

        def compute_mate(self, t, part):
            def body(i):
                self.stage[t, i] = part(block_of(t, False), i).astype(BF16)

            loop(ipd, body)

        def send_mate(self, t):
            def body(i):
                remote(
                    self.stage.at[t, i], self.inward.at[t, i],
                    r.rs_core_send.at[self.k], r.rs_core_recv.at[self.k, t, i], mate,
                ).start()

            loop(ipd, body)

        def mate_one(self, t, i, part):
            self.stage[t, i] = part(block_of(t, False), i).astype(BF16)
            remote(
                self.stage.at[t, i], self.inward.at[t, i],
                r.rs_core_send.at[self.k], r.rs_core_recv.at[self.k, t, i], mate,
            ).start()

        def to_mate(self, t, part):
            loop(ipd, lambda i: self.mate_one(t, i, part))

        def peer_one(self, t, i, part):
            value = part(block_of(t, True), i)
            drain(self.inward.at[t, i], r.rs_core_recv.at[self.k, t, i])
            self.outward[t - 1, i] = (value + self.inward[t, i].astype(F32)).astype(BF16)
            remote(
                self.outward.at[t - 1, i], self.landed.at[X - t - 1, i],
                r.rs_chip_send.at[self.k], r.rs_chip_recv.at[self.k, X - t, i], peer(t),
            ).start()

        def to_peer(self, t, part):
            loop(ipd, lambda i: self.peer_one(t, i, part))

        def both(self, t, part):
            self.mate_one(t, 0, part)

            def body(i, carry):
                self.mate_one(t, i, part)
                self.peer_one(t, i - 1, part)
                return carry

            lax.fori_loop(1, ipd, body, 0)
            self.peer_one(t, ipd - 1, part)

        def own(self, part):
            def body(i):
                value = part(ch, i)
                drain(self.inward.at[0, i], r.rs_core_recv.at[self.k, 0, i])
                self.keep[image(i), :] = value + self.inward[0, i].astype(F32)

            loop(ipd, body)

        def arrive(self, i):
            for t in range(1, X):
                drain(self.landed.at[t - 1, i], r.rs_chip_recv.at[self.k, t, i])

        def extra(self, i, at, lanes):
            value = self.landed[0, i, at, lanes].astype(F32)
            for t in range(2, X):
                value = value + self.landed[t - 1, i, at, lanes].astype(F32)
            return value

        def done(self, stage=True):
            if stage:
                drain(self.stage, r.rs_core_send.at[self.k])
            drain(self.outward, r.rs_chip_send.at[self.k])

    class Gather:
        def __init__(self, k, place, whole, pieces):
            self.k, self.place, self.whole, self.pieces = k, place, whole, pieces

        def send(self, i):
            src = self.place(ch, i)
            remote(src, src, r.ag_core_send.at[self.k], r.ag_core_recv.at[self.k, i], mate).start()
            for t in range(1, X):
                remote(src, src, r.ag_chip_send.at[self.k, t], r.ag_chip_recv.at[self.k, X - t, i], peer(t)).start()

        def from_mate(self, i):
            drain(self.place(block_of(0, False), i), r.ag_core_recv.at[self.k, i])

        def from_peer(self, t, i):
            ref = self.place(block_of(t, True), i)
            drain(ref, r.ag_chip_recv.at[self.k, t, i])
            remote(ref, ref, r.ag_pass_send.at[self.k, t], r.ag_pass_recv.at[self.k, t, i], mate).start()

        def from_pass(self, t, i):
            drain(self.place(block_of(t, False), i), r.ag_pass_recv.at[self.k, t, i])

        def done(self):
            drain(self.whole(ch), r.ag_core_send.at[self.k])
            for t in range(1, X):
                drain(self.whole(ch), r.ag_chip_send.at[self.k, t])
                drain(self.whole(block_of(t, True)), r.ag_pass_send.at[self.k, t])

    class Share:
        def __init__(self, k, blocks, rows):
            self.k, self.blocks, self.piece = k, blocks, rows // DP

        def part(self, b, d):
            at = pl.ds(pl.multiple_of(((dp + d) % DP) * self.piece, self.piece), self.piece)
            return self.blocks.at[b, at]

        def send(self):
            own = self.blocks.at[ch]
            remote(own, own, r.sh_core_send.at[self.k], r.sh_core_recv.at[self.k], mate).start()
            for t in range(1, X):
                src = self.part(ch, 0) if c.share else own
                remote(src, src, r.sh_chip_send.at[self.k, t], r.sh_chip_recv.at[self.k, X - t], peer(t)).start()

        def spread(self):
            for t in range(1, X):
                b = block_of(t, True)
                src = self.part(b, 0) if c.share else self.blocks.at[b]
                drain(src, r.sh_chip_recv.at[self.k, t])
                if c.share:
                    for d in range(1, DP):
                        remote(src, src, r.sh_col_send.at[self.k, t], r.sh_col_recv.at[self.k, t, DP - d], across(d)).start()

        def hand(self):
            for t in range(1, X):
                b = block_of(t, True)
                if c.share:
                    for d in range(1, DP):
                        drain(self.part(b, d), r.sh_col_recv.at[self.k, t, d])
                whole = self.blocks.at[b]
                remote(whole, whole, r.sh_pass_send.at[self.k, t], r.sh_pass_recv.at[self.k, t], mate).start()

        def take(self):
            drain(self.blocks.at[block_of(0, False)], r.sh_core_recv.at[self.k])
            for t in range(1, X):
                drain(self.blocks.at[block_of(t, False)], r.sh_pass_recv.at[self.k, t])

        def done(self):
            own = self.blocks.at[ch]
            drain(own, r.sh_core_send.at[self.k])
            for t in range(1, X):
                whole = self.blocks.at[block_of(t, True)]
                drain(self.part(ch, 0) if c.share else own, r.sh_chip_send.at[self.k, t])
                drain(whole, r.sh_pass_send.at[self.k, t])
                if c.share:
                    for d in range(1, DP):
                        drain(self.part(block_of(t, True), 0), r.sh_col_send.at[self.k, t])

    barrier = pltpu.get_barrier_semaphore()

    def greet(j, carry):
        pl.semaphore_signal(
            barrier, inc=1, device_id=((dp + j // CH) % DP, (ch + j % CH) % CH), device_id_type=MESH
        )
        return carry

    lax.fori_loop(1, D, greet, 0)

    load_w = pltpu.make_async_copy(
        r.reduce_weight.at[pl.ds(pl.multiple_of(ch * cw, cw), cw)], r.wr, r.load.at[0]
    )
    load_w.start()
    order = []
    for t in list(range(1, X)) + [0]:
        order += [block_of(t, False), block_of(t, True)]
    loads = []
    for k, b in enumerate(order):
        at = pl.ds(pl.multiple_of(b * own_rows, own_rows), own_rows)
        loads.append(pltpu.make_async_copy(r.inputs.at[at], r.xv.at[at], r.load.at[2 + k]))
        loads[-1].start()
    load_c = pltpu.make_async_copy(r.cotangent, r.cv, r.load.at[1])
    load_c.start()

    row_at = lax.broadcasted_iota(jnp.int32, (CELLS, LANES), 0)
    spot_r = lax.shift_right_logical(row_at, 4)
    spot_c = lax.bitwise_and(row_at, 15)

    def make_mask(j):
        side = 12 + 2 * r.resolution[j]
        mask = jnp.where(jnp.logical_and(spot_r < side, spot_c < side), 1.0, 0.0)
        r.area[pl.ds(j, 1), :] = jnp.full((1, LANES), side * side, jnp.int32).astype(F32)
        r.maskf[image(j), :] = mask

    loop(images, make_mask)

    def part_reduce(b, i):
        at = rows_of(b, i)
        x = r.xv[at, :] * wide(r.maskf[at, :].astype(BF16), cw)
        r.xv[at, :] = x
        return dot(x, r.wr[...])

    r.wg[ch] = r.split_weight[...]
    r.wx[ch] = r.expand_weight[...]
    shares = (Share(0, r.wg, taps), Share(1, r.wx, width))

    load_w.wait()
    rs1 = Scatter(0, r.stage, r.inward, r.outward, r.landed, r.red)
    loads[0].wait()
    rs1.compute_mate(1, part_reduce)
    pl.semaphore_wait(barrier, D - 1)
    rs1.send_mate(1)
    for share in shares:
        share.send()
    for t in range(1, X):
        if t > 1:
            loads[2 * t - 2].wait()
            rs1.to_mate(t, part_reduce)
        loads[2 * t - 1].wait()
        rs1.to_peer(t, part_reduce)
    for share in shares:
        share.spread()
    loads[2 * X - 2].wait()
    rs1.to_mate(0, part_reduce)
    loads[2 * X - 1].wait()
    rs1.own(part_reduce)

    def selector(parts, mine):
        row = lax.broadcasted_iota(jnp.int32, (mine, mine * parts), 0)
        col = lax.broadcasted_iota(jnp.int32, (mine, mine * parts), 1)
        return jnp.where(col == row + ch * mine, 1.0, 0.0)

    pick1 = selector(CH, m1)
    pick2 = selector(CH, m2)
    pickg = selector(CH, mg)
    r.pbuf[0, 0:1, 0:width] = exact(r.first_gain[...], pick1)
    r.pbuf[0, 1:2, 0:width] = exact(r.first_shift[...], pick1)
    r.pbuf[0, 2:3, :] = exact(r.second_gain[...], pick2)
    r.pbuf[0, 3:4, :] = exact(r.second_shift[...], pick2)

    for q in range(1, CH):
        remote(r.pbuf.at[0], r.pbuf.at[CH - q], r.par_send.at[0], r.par_recv.at[CH - q], (dp, (ch + q) % CH)).start()

    pixels = lax.fori_loop(
        0, ipd, lambda i, count: count + r.area[pl.ds(ch * ipd + i, 1), :], jnp.zeros((1, LANES), F32)
    )
    r.g0[0] = jnp.zeros((4, LANES), F32)
    r.g0[0, 0:1, :] = pixels
    everyone(r.g0, 7)

    r.wrt[...] = flip(r.wr[...])
    r.wet[...] = flip(r.expand_weight[...])

    def turn_x(j):
        r.xt[j] = flip(r.xv[image(j), :])

    loop(images, turn_x)
    for g in range(2):
        for i in range(ipd):
            r.act[g, i, 0:SIDE, :] = jnp.zeros((SIDE, 3 * half), BF16)
            r.act[g, i, CELLS + SIDE : TALL, :] = jnp.zeros((SIDE, 3 * half), BF16)
            r.dsh[g, i, 0:SIDE, :] = jnp.zeros((SIDE, 3 * width), BF16)
            r.dsh[g, i, CELLS + SIDE : TALL, :] = jnp.zeros((SIDE, 3 * width), BF16)

    def finish_reduce(i, state):
        rs1.arrive(i)

        def body(at, k, state):
            first, second = state
            value = r.red[at, :] + rs1.extra(i, pl.ds(pl.multiple_of(k * STRIP, STRIP), STRIP), slice(None))
            r.red[at, :] = value
            return (first + fold(value), second + fold(value * value))

        return strips(i * CELLS, body, state)

    zero8 = jnp.zeros((8, width), F32)
    first, second = lax.fori_loop(0, ipd, finish_reduce, (zero8, zero8))

    put(r.g1, 0, total(first))
    put(r.g1, width // LANES, total(second))
    everyone(r.g1, 0)
    for share in shares:
        share.hand()
    everyone_wait(r.g1, 0)
    sums = jnp.sum(r.g1[...], axis=0)
    everyone_wait(r.g0, 7)
    count = jnp.sum(r.g0[...], axis=0)[0:1, 0:1]
    inverse = 1.0 / count
    params = r.pbuf[0]
    for q in range(1, CH):
        drain(r.pbuf.at[q], r.par_recv.at[q])
        params = params + r.pbuf[q]
    gain1, shift1 = params[0:1, 0:width], params[1:2, 0:width]
    gain2, shift2 = params[2:3, :], params[3:4, :]

    def moments(first, second):
        mean = first * inverse
        return mean, lax.rsqrt(second * inverse - mean * mean + EPS)

    mean1, scale1 = moments(get(sums, 0, width), get(sums, width // LANES, width))

    place_x = lambda b, i: r.xh1.at[rows_of(b, i)]
    gx = Gather(0, place_x, lambda b: r.xh1.at[block_rows(b)], ipd)

    strip_c = lax.bitwise_and(lax.broadcasted_iota(jnp.int32, (STRIP, LANES), 0), 15)
    not_first = strip_c != 0
    not_last = strip_c != 15

    def first_act(i):
        def body(at, k, carry):
            there = pl.ds(pl.multiple_of((ch * ipd + i) * CELLS + k * STRIP, STRIP), STRIP)
            put_at = pl.ds(pl.multiple_of(SIDE + k * STRIP, SIDE), STRIP)
            mask = r.maskf[there, :]
            for g in range(2):
                lanes = slice(g * half, (g + 1) * half)
                xh = (r.red[at, lanes] - mean1[:, lanes]) * scale1[:, lanes]
                h = gain1[:, lanes] * xh + shift1[:, lanes]
                s = sigmoid(h)
                y = h * s
                r.red[at, lanes] = xh
                r.xh1[there, lanes] = xh.astype(BF16)
                r.slope1[at, lanes] = mask * (s + y - y * s)
                a = mask * y
                before = jnp.where(not_first, pltpu.roll(a, 1, 0), 0.0)
                after = jnp.where(not_last, pltpu.roll(a, STRIP - 1, 0), 0.0)
                r.act[g, i, put_at, 0:half] = before.astype(BF16)
                r.act[g, i, put_at, half : 2 * half] = a.astype(BF16)
                r.act[g, i, put_at, 2 * half : 3 * half] = after.astype(BF16)
            return carry

        strips(i * CELLS, body, 0)

    loop(ipd, first_act)

    for share in shares:
        share.take()
    for g in range(2):
        for q in range(CH // 2):
            r.wf[g, :, q * m2 : (q + 1) * m2] = r.wg[g * (CH // 2) + q]

    def two_of(n):
        return pl.ds(pl.multiple_of(n * 2 * CELLS, 2 * CELLS), 2 * CELLS)

    def conv(n, state):
        there = pl.ds(pl.multiple_of((ch * ipd + 2 * n) * CELLS, 2 * CELLS), 2 * CELLS)
        out = []
        for g in range(2):
            lanes = slice(g * width, (g + 1) * width)
            left = jnp.concatenate(
                [
                    r.act[g, pl.ds(2 * n, 2), k * SIDE : k * SIDE + CELLS, :].reshape(2 * CELLS, 3 * half)
                    for k in range(3)
                ],
                axis=1,
            )
            value = dot(left, r.wf[g]) * wide(r.maskf[there, :], width)
            r.sp[two_of(n), lanes] = value
            out.append((state[g][0] + fold(value), state[g][1] + fold(value * value)))
        return tuple(out)

    state = lax.fori_loop(0, ipd // 2, conv, ((zero8, zero8), (zero8, zero8)))
    for g in range(2):
        put(r.g2, g * (width // LANES), total(state[g][0]))
        put(r.g2, (2 + g) * (width // LANES), total(state[g][1]))
    everyone(r.g2, 1)
    loop(ipd // 2, gx.send)

    for g in range(2):
        for tap in range(9):
            r.wt[g, tap * width : (tap + 1) * width, :] = flip(r.wf[g, tap * half : (tap + 1) * half, :])

    everyone_wait(r.g2, 1)
    sums = jnp.sum(r.g2[...], axis=0)
    mean2, scale2 = moments(get(sums, 0, two), get(sums, two // LANES, two))

    r.g3[0] = jnp.zeros((8, LANES), F32)

    def second_act(i):
        def body(at, k, state):
            there = pl.ds(pl.multiple_of((ch * ipd + i) * CELLS + k * STRIP, STRIP), STRIP)
            mask = r.maskf[there, :]
            new = []
            for q in range(two // LANES):
                lanes = slice(q * LANES, (q + 1) * LANES)
                xh = (r.sp[at, lanes] - mean2[:, lanes]) * scale2[:, lanes]
                h = gain2[:, lanes] * xh + shift2[:, lanes]
                s = sigmoid(h)
                y = h * s
                r.sp[at, lanes] = xh
                r.slope2[at, lanes] = mask * (s + y - y * s)
                a = mask * y
                r.act2[at, lanes] = a
                new.append(state[q] + fold(a))
            return tuple(new)

        zero = jnp.zeros((8, LANES), F32)
        pooled = strips(i * CELLS, body, (zero,) * (two // LANES))
        share = 1.0 / r.area[pl.ds(ch * ipd + i, 1), :]
        r.share[pl.ds(i, 1), :] = share
        n = width // LANES
        for q in range(n):
            r.g3[0, pl.ds(4 * q + i, 1), :] = total(pooled[q] + pooled[n + q]) * share

    loop(ipd, second_act)
    everyone(r.g3, 2)

    def slope_guess():
        root = 3.0**0.5
        points = []
        for z in (-root, 0.0, root):
            h = shift2 + z * gain2
            s = sigmoid(h)
            points.append(s + h * s - h * s * s)
        low, mid, high = points
        return (low + 4.0 * mid + high) * (1.0 / 6.0), (high - low) * (root / 6.0)

    guess = slope_guess()

    def slope_sums(i):
        share = r.share[pl.ds(i, 1), :]
        zero = jnp.zeros((8, LANES), F32)
        n = width // LANES

        def body(at, k, state):
            new = []
            for q in range(2 * n):
                lanes = slice(q * LANES, (q + 1) * LANES)
                slope = r.slope2[at, lanes]
                new.append((state[q][0] + fold(slope), state[q][1] + fold(slope * r.sp[at, lanes])))
            return tuple(new)

        state = strips(i * CELLS, body, ((zero, zero),) * (2 * n))
        for q in range(2 * n):
            for stat in range(2):
                row_at = (stat * n + q % n) * 8 + 4 * (q // n)
                r.slopes[pl.ds(row_at + i, 1), :] = (
                    total(state[q][stat]) * share - guess[stat][:, q * LANES : (q + 1) * LANES]
                )

    r.slopes[...] = jnp.zeros_like(r.slopes)
    loop(ipd, slope_sums)
    r.g5[0] = r.slopes[...].astype(BF16)

    everyone(r.g5, 4)


    gate_rows = min(D * 8, 2 * LANES)
    gate_blocks = D * 8 // gate_rows
    gate_at = lax.broadcasted_iota(jnp.int32, (gate_rows, LANES), 0)
    valid = lax.bitwise_and(gate_at, 7) < ipd
    every = 1.0 / (D * ipd)

    def gate_block(n):
        return pl.ds(pl.multiple_of(n * gate_rows, gate_rows), gate_rows)

    def lower_upper(buf, n):
        slots = gate_rows // 8
        both = buf[pl.ds(n * slots, slots)].reshape(gate_rows, LANES)
        return jnp.where(valid, both, 0.0), jnp.where(valid, pltpu.roll(both, gate_rows - 4, 0), 0.0)

    def gate_in(n, state):
        sum_lo, sum_hi = lower_upper(r.g3, n)
        pre = exact(sum_lo, r.gate_down[0:LANES, :]) + exact(sum_hi, r.gate_down[LANES:, :])
        r.gate_x[gate_block(n), :] = pre
        return state[0] + total(pre), state[1] + total(pre * pre)

    everyone_wait(r.g3, 2)
    zero1 = jnp.zeros((1, LANES), F32)
    first, second = lax.fori_loop(0, gate_blocks, gate_in, (zero1, zero1))
    gate_mean = first * every
    gate_scale = lax.rsqrt(second * every - gate_mean * gate_mean + EPS)

    def gate_out(n):
        at = gate_block(n)
        x = (r.gate_x[at, :] - gate_mean) * gate_scale
        h = r.gate_gain[...] * x + r.gate_shift[...]
        s = sigmoid(h)
        y = h * s
        r.gate_x[at, :] = x
        r.squeezed[at, :] = y
        r.gate_slope[at, :] = s + y - y * s

    loop(gate_blocks, gate_out)
    logits = exact(r.squeezed[0:8, :], r.gate_up[...]) + r.gate_bias[...]
    top = jnp.maximum(logits[:, :width], logits[:, width:])
    upper = jnp.exp(logits[:, :width] - top)
    lower = jnp.exp(logits[:, width:] - top)
    both = upper + lower
    r.att[:, 0:width] = upper / both
    r.att[:, width:two] = lower / both

    gm = Gather(1, lambda b, i: r.merged.at[rows_of(b, i)], lambda b: r.merged.at[block_rows(b)], ipd)

    def merge(i, state):
        att = r.att[pl.ds(i, 1), :]

        def body(at, k, carry):
            there = pl.ds(pl.multiple_of((ch * ipd + i) * CELLS + k * STRIP, STRIP), STRIP)
            left = (r.act2[at, 0:width] * att[:, 0:width]).astype(BF16)
            right = (r.act2[at, width:two] * att[:, width:two]).astype(BF16)
            both = (left.astype(F32) + right.astype(F32)).astype(BF16)
            r.merged[there, :] = both
            return carry + fold(both.astype(F32))

        return strips(i * CELLS, body, state)

    merged_sum = merge(0, zero8)
    gm.send(0)
    merged_sum = lax.fori_loop(1, ipd, merge, merged_sum)

    def turn_own(j):
        r.mt[:, rows_of(ch, j)] = flip(r.merged[rows_of(ch, j), :])

    loop(ipd, turn_own)

    def halves(value):
        high = value.astype(BF16)
        return high, (value - high.astype(F32)).astype(BF16)

    gram = dot(r.mt[:, block_rows(ch)], r.merged[block_rows(ch), :])
    gram_high, gram_low = halves(gram)
    high, rest = halves(total(merged_sum))
    low, last = halves(total(merged_sum) - high.astype(F32))
    means = jnp.concatenate([high, low, last, jnp.zeros((13, width), BF16)], axis=0)

    def expand_sums(k):
        weight = r.wx[k]
        square = dot(gram_high, weight) + dot(gram_low, weight)
        put(r.sums3.at[pl.ds(k, 1)], 0, total(dot(means, weight)))
        put(r.sums3.at[pl.ds(k, 1)], cw // LANES, total(fold(square * weight.astype(F32))))

    zero_c = jnp.zeros((8, cw), F32)
    loop(CH, expand_sums)
    r.r1[0] = r.sums3[ch]
    row(r.r1, 1, r.sums3)
    lax.fori_loop(1, ipd, lambda i, carry: (gm.send(i), carry)[1], 0)
    load_c.wait()
    r.acc[...] = jnp.zeros((16, cw), F32)
    row_sum(r.r1, 1, r.c1)
    column(r.c1, 0)

    for t in range(1, X):
        loop(2, lambda i: gm.from_peer(t, i))
    def turn_w(k):
        r.wxt[k] = flip(r.wx[k])

    loop(CH, turn_w)
    for p in range(width // LANES):
        at = slice(p * LANES, (p + 1) * LANES)
        r.gapt[at, :] = (r.gate_up[:, at] - r.gate_up[:, width + p * LANES : width + (p + 1) * LANES]).T
        r.downt[:, at] = r.gate_down[at, :].T
    column_wait(r.c1, 0)
    sums = jnp.sum(r.c1[...], axis=0)
    mean3, scale3 = moments(get(sums, 0, cw), get(sums, cw // LANES, cw))
    gain3, shift3 = r.third_gain[...], r.third_shift[...]
    lead3 = gain3 * scale3
    lift3 = shift3 - mean3 * lead3
    per3 = cw // LANES
    put(r.r2, 0, lead3 * scale3)
    put(r.r2, per3, lead3)
    put(r.r2, 2 * per3, lead3 * scale3 * mean3)
    row(r.r2, 0)

    def outputs(b, i):
        r.ex[rows_of(b, i), :] = dot(r.merged[rows_of(b, i), :], r.expand_weight[...])

        def body(at, k, state):
            shift, cross = state
            mask = wide(r.maskf[at, :], cw)
            x = r.ex[at, :]
            h = lead3 * x + lift3 + r.xv[at, :].astype(F32)
            s = sigmoid(h)
            y = h * s
            d = r.cv[at, :].astype(F32) * mask * (s + y - y * s)
            r.cv[at, :] = (mask * y).astype(BF16)
            r.dpre[at, :] = d
            r.de[at, :] = (lead3 * d).astype(BF16)
            return (shift + fold(d), cross + fold(d * x))

        shift, cross = strips((b * ipd + i) * CELLS, body, (zero_c, zero_c))
        r.acc[0:8, :] += shift
        r.acc[8:16, :] += cross
        at = rows_of(b, i)
        pltpu.make_async_copy(r.cv.at[at], r.block_out.at[at], r.store.at[0]).start()

    def part_merged(b, i):
        return dot(r.de[rows_of(b, i), :], r.wet[...])

    rs1.done()
    rs2 = Scatter(1, r.stage, r.inward2, r.outward, r.landed2, r.dm)
    for t in range(1, X):

        def far(i):
            gm.from_pass(t, i)
            outputs(block_of(t, False), i)
            rs2.mate_one(t, i, part_merged)
            if i >= 2:
                rs2.peer_one(t, i - 1, part_merged)
            outputs(block_of(t, True), i)
            if i + 2 < ipd:
                gm.from_peer(t, i + 2)
            if i == 0:
                rs2.peer_one(t, 0, part_merged)

        for i in range(ipd):
            far(i)
        rs2.peer_one(t, ipd - 1, part_merged)

    def near(i):
        gm.from_mate(i)
        outputs(block_of(0, False), i)
        rs2.mate_one(0, i, part_merged)

    loop(ipd, near)
    loop(ipd, lambda i: outputs(ch, i))
    shift = total(r.acc[0:8, :])
    put(r.c2, 0, shift)
    put(r.c2, cw // LANES, (total(r.acc[8:16, :]) - mean3 * shift) * scale3)
    everyone(r.c2, 6)
    rs2.own(part_merged)

    def turn_other(j):
        b = j // ipd
        b = jnp.where(b < ch, b, b + 1)
        at = b * ipd + j % ipd
        r.mt[:, image(at)] = flip(r.merged[image(at), :])

    loop(images - ipd, turn_other)
    everyone_wait(r.c2, 6)
    drain(r.r2.at[pl.ds(1, CH - 1)], r.row_recv.at[0])
    r.back3[...] = jnp.sum(r.c2[...].reshape(DP, CH, 4, LANES), axis=0)
    sums = r.back3[0]
    shift_grad, gain_grad = get(sums, 0, cw), get(sums, cw // LANES, cw)
    r.third_gain_grad[...] = gain_grad
    r.third_shift_grad[...] = shift_grad
    base3, slant3 = shift_grad * inverse, gain_grad * inverse
    slope3 = lead3 * scale3 * slant3
    flat3 = lead3 * base3 - mean3 * slope3

    r.mix[...] = jnp.zeros((width, width), F32)
    r.offset[...] = jnp.zeros((16, width), F32)

    def mix(q):
        b = (ch + q) % CH
        coefs, part = r.r2[q], r.back3[q]
        base, slant = get(part, 0, cw) * inverse, get(part, per3, cw) * inverse
        slope = get(coefs, 0, cw) * slant
        flat = get(coefs, per3, cw) * base - get(coefs, 2 * per3, cw) * slant
        r.mix[...] += dot((r.wx[b].astype(F32) * slope).astype(BF16), r.wxt[b])
        high = flat.astype(BF16)
        low = (flat - high.astype(F32)).astype(BF16)
        pair = jnp.concatenate([high, low, jnp.zeros((14, cw), BF16)], axis=0)
        r.offset[...] += dot(pair, r.wxt[b])

    loop(CH, mix)
    r.mixb[...] = r.mix[...].astype(BF16)

    offset = total(r.offset[...])
    away = offset + dot(r.merged[block_rows(ch), :], r.mixb[...])
    r.inward[0] = away.astype(BF16).reshape(ipd, CELLS, width)

    r.told[...] = jnp.zeros((16, LANES), F32)

    def finish_merged(i):
        rs2.arrive(i)

        def body(at, k, state):
            here = pl.ds(pl.multiple_of(k * SIDE, SIDE), SIDE)
            there = pl.ds(pl.multiple_of((ch * ipd + i) * CELLS + k * SIDE, SIDE), SIDE)
            away = wide(r.maskf[there, :], width) * r.inward[0, i, here, :].astype(F32)
            value = r.dm[at, :] + rs2.extra(i, here, slice(None)) - away
            r.dm[at, :] = value
            new = [state[0] + fold(value * (r.act2[at, 0:width] - r.act2[at, width:two]))]
            for g in range(2):
                lanes = slice(g * width, (g + 1) * width)
                part = value * r.slope2[at, lanes]
                new += [state[1 + 2 * g] + fold(part), state[2 + 2 * g] + fold(part * r.sp[at, lanes])]
            return tuple(new)

        gap, *parts = strips(i * CELLS, body, (zero8,) * 5, SIDE)
        att = r.att[pl.ds(i, 1), :]
        grad = att[:, 0:width] * att[:, width:two] * total(gap)
        n = width // LANES
        for q in range(n):
            r.told[pl.ds(4 * q + i, 1), :] = grad[:, q * LANES : (q + 1) * LANES]
        for g in range(2):
            for stat in range(2):
                part = total(parts[2 * g + stat]) * att[:, g * width : (g + 1) * width]
                for q in range(n):
                    at = 8 + (2 * stat + g) * n + q
                    r.told[at : at + 1, :] += part[:, q * LANES : (q + 1) * LANES]

    loop(ipd, finish_merged)
    r.r4[0] = r.told[8:16, :]
    row(r.r4, 2)
    r.g4[0] = r.told[0:8, :]
    everyone(r.g4, 3)
    lax.fori_loop(ipd // 2, ipd, lambda i, carry: (gx.send(i), carry)[1], 0)
    row_sum(r.r4, 2, r.c4)
    column(r.c4, 3)

    piece = width // DP
    et = r.es.dtype
    def piece_rows(d):
        return pl.ds(pl.multiple_of(((dp + d) % DP) * piece, piece), piece)

    def grow(b):
        def body(at, k, carry):
            mask = wide(r.maskf[at, :], cw)
            d = lead3 * r.dpre[at, :] - mask * (flat3 + r.ex[at, :] * slope3)
            r.de[at, :] = d.astype(BF16)
            return carry

        for i in range(ipd):
            strips((b * ipd + i) * CELLS, body, 0)
        value = dot(r.mt[:, block_rows(b)], r.de[block_rows(b), :])
        r.eg[...] += value

    r.eg[...] = jnp.zeros((width, cw), F32)
    loop(CH, grow)
    r.es[...] = r.eg[...].astype(et)

    for d in range(1, DP):
        remote(r.es.at[piece_rows(d)], r.ebuf.at[DP - d], r.eg_send.at[0], r.eg_recv.at[0], across(d)).start()

    everyone_wait(r.g5, 4)
    everyone_wait(r.g4, 3)

    def gate_back(n, state):
        at = gate_block(n)
        grad_lo, grad_hi = lower_upper(r.g4, n)
        grad = exact(grad_lo, r.gapt[0:LANES, :]) + exact(grad_hi, r.gapt[LANES:width, :])
        grad = grad * r.gate_slope[at, :]
        r.grad_down[at, :] = grad
        return state[0] + total(grad), state[1] + total(grad * r.gate_x[at, :])

    gate_shift_all, gate_gain_all = lax.fori_loop(0, gate_blocks, gate_back, (zero1, zero1))
    lead = r.gate_gain[...] * gate_scale

    def gate_norm_back(n, state):
        at = gate_block(n)
        grad = r.grad_down[at, :] - gate_shift_all * every - r.gate_x[at, :] * (gate_gain_all * every)
        grad = jnp.where(valid, lead * grad, 0.0)
        r.grad_down[at, :] = grad
        summary = exact(grad, r.downt[...])
        slots = gate_rows // 8

        @pl.when(n == 0)
        def _():
            r.grad_summary[...] = summary[0:8, :]

        slopes = r.g5[pl.ds(n * slots, slots)].astype(F32)
        new = []
        for stat in range(2):
            for p in range(width // LANES):
                part = summary[:, p * LANES : (p + 1) * LANES]
                part = (part + pltpu.roll(part, 4, 0)).reshape(slots, 8, LANES)
                k = stat * (width // LANES) + p
                new.append(state[k] + jnp.sum(part * slopes[:, 8 * k : 8 * k + 8, :], axis=0))
        new.append(state[-1] + total(summary))
        return tuple(new)

    n_half = width // LANES
    zero = jnp.zeros((8, LANES), F32)
    *flats, summed = lax.fori_loop(
        0, gate_blocks, gate_norm_back, (zero,) * (2 * n_half) + (jnp.zeros((1, width), F32),)
    )
    guess = slope_guess()
    column_wait(r.c4, 3)
    told = jnp.sum(r.c4[...], axis=0)

    def second_sum(stat):
        parts = []
        for q in range(2 * n_half):
            flat = flats[stat * n_half + q % n_half]
            flat = total(flat[4 * (q // n_half) : 4 * (q // n_half) + 4, :])
            at = 2 * n_half * stat + q
            lanes = slice(q % n_half * LANES, (q % n_half + 1) * LANES)
            flat = flat + guess[stat][:, q * LANES : (q + 1) * LANES] * summed[:, lanes]
            parts.append(flat + told[at : at + 1, :])
        return jnp.concatenate(parts, axis=1)

    shift_grad2, gain_grad2 = second_sum(0), second_sum(1)
    lead2, base2, slant2 = gain2 * scale2, shift_grad2 * inverse, gain_grad2 * inverse

    def splits_back(i):
        att = r.att[pl.ds(i, 1), :]
        flat = r.grad_summary[pl.ds(i, 1), :] * wide(r.share[pl.ds(i, 1), :], width)

        def body(at, k, carry):
            there = pl.ds(pl.multiple_of((ch * ipd + i) * CELLS + k * STRIP, STRIP), STRIP)
            put_at = pl.ds(pl.multiple_of(SIDE + k * STRIP, SIDE), STRIP)
            mask = r.maskf[there, :]
            for q in range(two // LANES):
                g, p = q // n_half, q % n_half
                lanes = slice(q * LANES, (q + 1) * LANES)
                here = slice(p * LANES, (p + 1) * LANES)
                d = (r.dm[at, here] * att[:, lanes] + flat[:, here]) * r.slope2[at, lanes]
                d = mask * lead2[:, lanes] * (d - base2[:, lanes] - r.sp[at, lanes] * slant2[:, lanes])
                r.act2[at, lanes] = d
                before = jnp.where(not_first, pltpu.roll(d, 1, 0), 0.0)
                after = jnp.where(not_last, pltpu.roll(d, STRIP - 1, 0), 0.0)
                for n, value in enumerate((after, d, before)):
                    start = n * width + p * LANES
                    r.dsh[g, i, put_at, start : start + LANES] = value.astype(BF16)
            return carry

        strips(i * CELLS, body, 0)

    loop(ipd, splits_back)

    drain(r.stage, r.rs_core_send.at[1])

    def turn_d(i):
        for g in range(2):
            r.stage[g, i] = r.act2[image(i), g * width : (g + 1) * width].T.astype(BF16)

    loop(ipd, turn_d)
    per = CH // 2
    wide3 = 3 * half
    for k in range(3):
        for g in range(2):
            right = r.act[g, :, k * SIDE : k * SIDE + CELLS, :].reshape(own_rows, wide3)
            value = dot(jnp.concatenate([r.stage[g, i] for i in range(ipd)], axis=1), right)
            if c.split_inside:
                for q in range(per):
                    b = g * per + q
                    r.ss[k, b % 2, b // 2] = value[q * m2 : (q + 1) * m2, :].astype(BF16)
            else:
                r.split_part[g * width : (g + 1) * width, k * wide3 : (k + 1) * wide3] = value
        if c.split_inside:
            remote(r.ss.at[k, 1 - core], r.sin.at[k], r.sg_send.at[0, k], r.sg_recv.at[0, k], mate).start()
    slab = m2 // DP
    Z = DP // 2
    turn, side = dp // 2, dp % 2

    def ring(e):
        return (((turn + e) % Z) * 2 + side, ch)

    other = (dp + 1 - 2 * side, ch)

    def split_cores(k):
        drain(r.sin.at[k], r.sg_recv.at[0, k])
        for t in range(X):
            value = (r.ss[k, core, t].astype(F32) + r.sin[k, t].astype(F32)).astype(BF16)
            value = value.reshape(Z, 2, slab, wide3)
            for p in range(2):
                r.sc[k, p, :, t] = value[:, p]
        remote(r.sc.at[k, 1 - side], r.sp1.at[k], r.sg_send.at[1, k], r.sg_recv.at[1, k], other).start()

    def split_pairs(k):
        drain(r.sp1.at[k], r.sg_recv.at[1, k])
        r.sy[k] = (r.sc[k, side].astype(F32) + r.sp1[k].astype(F32)).astype(BF16)
        for e in range(1, Z):
            remote(
                r.sy.at[k, (turn + e) % Z], r.sz.at[k, Z - e], r.sg_send.at[2, k], r.sg_recv.at[2, k], ring(e)
            ).start()

    def split_chips(k):
        drain(r.sz.at[k, pl.ds(1, Z - 1)], r.sg_recv.at[2, k])
        for t in range(X):
            there = (chip + t) % X
            value = r.sy[k, turn, there].astype(F32)
            for e in range(1, Z):
                value = value + r.sz[k, e, there].astype(F32)
            r.sx[k, t] = value.astype(BF16)
            if t:
                remote(r.sx.at[k, t], r.sxin.at[k, X - t], r.sg_send.at[3, k], r.sg_recv.at[3, k], peer(t)).start()

    def split_out(k):
        drain(r.sxin.at[k, pl.ds(1, X - 1)], r.sg_recv.at[3, k])
        value = r.sx[k, 0].astype(F32)
        for t in range(1, X):
            value = value + r.sxin[k, t].astype(F32)
        r.so[k, 0] = value.astype(BF16)
        for d in range(1, DP):
            remote(r.so.at[k, 0], r.so.at[k, DP - d], r.sg_send.at[4, k], r.sg_recv.at[4, k], across(d)).start()

    def split_step(step, k):
        if c.split_inside:
            step(k)

    def first_back(i, many, state):
        size = many * CELLS
        there = pl.ds(pl.multiple_of((ch * ipd + i) * CELLS, CELLS), size)
        here = slice(i * CELLS, i * CELLS + size)
        out = []
        for g in range(2):
            lanes = slice(g * half, (g + 1) * half)
            left = jnp.concatenate(
                [
                    r.dsh[g, i : i + many, (2 - k) * SIDE : (2 - k) * SIDE + CELLS, :].reshape(size, 3 * width)
                    for k in range(3)
                ],
                axis=1,
            )
            value = dot(left, r.wt[g]) * r.slope1[here, lanes]
            r.dh1[there, lanes] = value.astype(BF16)
            out.append((state[g][0] + fold(value), state[g][1] + fold(value * r.red[here, lanes])))
        return tuple(out)

    zero_h = jnp.zeros((8, half), F32)
    gd = Gather(2, lambda b, i: r.dh1.at[rows_of(b, i)], lambda b: r.dh1.at[block_rows(b)], ipd)
    state = ((zero_h, zero_h), (zero_h, zero_h))
    for i in range(2):
        state = first_back(i, 1, state)
        gd.send(i)
        if i == 0:
            for k in range(3):
                split_step(split_cores, k)
    if ipd > 2:
        state = first_back(2, ipd - 2, state)
    for g in range(2):
        r.g6[0, g : g + 1, :] = total(state[g][0])
        r.g6[0, 2 + g : 3 + g, :] = total(state[g][1])
    everyone(r.g6, 5)
    lax.fori_loop(2, ipd, lambda i, carry: (gd.send(i), carry)[1], 0)

    def pass_x(i):
        for t in range(1, X):
            gx.from_peer(t, i)

    loop(ipd, pass_x)

    drain(r.ebuf.at[pl.ds(1, DP - 1)], r.eg_recv.at[0])
    value = r.eg[piece_rows(0), :]
    for d in range(1, DP):
        value = value + r.ebuf[d].astype(F32)
    r.eo[0] = value.astype(et)
    for d in range(1, DP):
        remote(r.eo.at[0], r.eo.at[DP - d], r.eg_send.at[1], r.eg_recv.at[1], across(d)).start()
    for k in range(3):
        split_step(split_pairs, k)
    everyone_wait(r.g6, 5)
    sums = jnp.sum(r.g6[...], axis=0)
    shift_grad, gain_grad = get(sums, 0, width), get(sums, 2, width)
    lead1, base1, slant1 = gain1 * scale1, shift_grad * inverse, gain_grad * inverse

    r.rg[...] = jnp.zeros((cw, width), F32)

    def from_x(i):
        gx.from_mate(i)
        for t in range(1, X):
            gx.from_pass(t, i)

    loop(ipd, from_x)
    gx.done()

    def reduced_back(b, i):
        def body(at, k, carry):
            mask = wide(r.maskf[at, :], width)
            d = mask * lead1 * (r.dh1[at, :].astype(F32) - base1 - r.xh1[at, :].astype(F32) * slant1)
            r.xh1[at, :] = d.astype(BF16)
            return carry

        strips((b * ipd + i) * CELLS, body, 0)
        r.rg[...] += dot(r.xt[b * ipd + i], r.xh1[rows_of(b, i), :])

    def input_back(b, i):
        at = rows_of(b, i)
        r.xv[at, :] = (r.dpre[at, :] + dot(r.xh1[at, :], r.wrt[...])).astype(BF16)
        pltpu.make_async_copy(r.xv.at[at], r.inputs_grad.at[at], r.store.at[1]).start()

    loop(ipd, lambda i: reduced_back(ch, i))

    def from_mate(i):
        gd.from_mate(i)
        reduced_back(block_of(0, False), i)

    loop(ipd, from_mate)
    split_step(split_chips, 0)
    for t in range(1, X):

        def from_peer(i):
            gd.from_peer(t, i)
            reduced_back(block_of(t, True), i)

        loop(ipd, from_peer)
    split_step(split_chips, 1)
    for t in range(1, X):

        def from_pass(i):
            gd.from_pass(t, i)
            reduced_back(block_of(t, False), i)

        loop(ipd, from_pass)

    split_step(split_chips, 2)
    if c.reduce_inside:
        r.rs[...] = r.rg[...].T.astype(r.rs.dtype)
        for d in range(1, DP):
            remote(r.rs.at[piece_rows(d)], r.rbuf.at[DP - d], r.rg_send.at[0], r.rg_recv.at[0], across(d)).start()
    else:
        r.reduce_part[...] = r.rg[...].T
    split_step(split_out, 0)
    loop(ipd, lambda i: input_back(ch, i))
    split_step(split_out, 1)
    loop(ipd, lambda i: input_back(block_of(0, False), i))
    split_step(split_out, 2)
    if c.reduce_inside:
        groups = DP // CH
        goal = dp // groups
        drain(r.rbuf.at[pl.ds(1, DP - 1)], r.rg_recv.at[0])
        value = r.rs[piece_rows(0), :].astype(F32)
        for d in range(1, DP):
            value = value + r.rbuf[d].astype(F32)
        r.rsum[...] = value.astype(r.rsum.dtype)
        slot = r.rall.at[dp % groups, ch]
        for d in range(1, DP):
            remote(r.rsum, slot, r.rg_send.at[1], r.rg_recv.at[1], ((dp + d) % DP, goal)).start()

        @pl.when(goal == ch)
        def _():
            pltpu.make_async_copy(r.rsum, slot, r.rg_recv.at[1]).start()

        @pl.when(goal != ch)
        def _():
            remote(r.rsum, slot, r.rg_send.at[2], r.rg_recv.at[1], (dp, goal)).start()

    for t in range(1, X):
        loop(ipd, lambda i: input_back(block_of(t, True), i))
    for t in range(1, X):
        loop(ipd, lambda i: input_back(block_of(t, False), i))
    r.second_gain_grad[...] = exact_nt(gain_grad2, pick2)
    r.second_shift_grad[...] = exact_nt(shift_grad2, pick2)
    r.first_gain_grad[...] = exact_nt(gain_grad, pick1)
    r.first_shift_grad[...] = exact_nt(shift_grad, pick1)
    r.gate_gain_grad[...] = exact_nt(gate_gain_all, pickg)
    r.gate_shift_grad[...] = exact_nt(gate_shift_all, pickg)

    def gate_grads(n, state):
        at = gate_block(n)
        sum_lo, sum_hi = lower_upper(r.g3, n)
        grad_lo, grad_hi = lower_upper(r.g4, n)
        picked = exact_nt(r.grad_down[at, :], pickg)
        down = jnp.concatenate([exact_tn(picked, sum_lo), exact_tn(picked, sum_hi)], axis=1)
        squeezed = r.squeezed[at, :]
        up = jnp.concatenate([exact_tn(squeezed, grad_lo), exact_tn(squeezed, grad_hi)], axis=1)
        bias = jnp.concatenate([total(grad_lo), total(grad_hi)], axis=1)
        return state[0] + down, state[1] + up, state[2] + bias

    down, up, bias = lax.fori_loop(
        0, gate_blocks, gate_grads,
        (jnp.zeros((mg, width), F32), jnp.zeros((inner, width), F32), jnp.zeros((1, width), F32)),
    )
    r.down_grad[...] = down
    r.up_grad[...] = exact_nt(jnp.concatenate([up, -up], axis=1), pick2)
    r.bias_grad[...] = exact_nt(jnp.concatenate([bias, -bias], axis=1), pick2)

    drain(r.eo.at[pl.ds(1, DP - 1)], r.eg_recv.at[1])
    for d in range(DP):
        r.expand_grad[piece_rows(d), :] = r.eo[d].astype(F32)
    if c.reduce_inside:
        drain(r.rall, r.rg_recv.at[1])
        for s in range(groups):
            for q in range(CH):
                r.reduce_grad[s * piece : (s + 1) * piece, q * cw : (q + 1) * cw] = r.rall[s, q].astype(F32)
    if c.split_inside:
        for k in range(3):
            drain(r.so.at[k, pl.ds(1, DP - 1)], r.sg_recv.at[4, k])
            for p in range(3):
                at = slice(p * half, (p + 1) * half)
                block = jnp.concatenate(
                    [r.so[k, (d - dp + DP) % DP, :, at].astype(F32) for d in range(DP)], axis=0
                )
                r.split_grad[3 * k + p] = block.T

    for k, buf in enumerate((r.g1, r.g2, r.g3, r.g4, r.g5, r.g6, r.c2, r.g0)):
        everyone_done(buf, k)
    column_done(r.c1, 0)
    row_done(r.r1, 1)
    row_done(r.r2, 0)
    row_done(r.r4, 2)
    column_done(r.c4, 3)
    rs2.done(False)
    for gather in (gm, gd) + shares:
        gather.done()
    drain(r.pbuf.at[pl.ds(1, CH - 1)], r.par_send.at[0])
    drain(r.ebuf.at[pl.ds(1, DP - 1)], r.eg_send.at[0])
    drain(r.ebuf.at[pl.ds(1, DP - 1)], r.eg_send.at[1])
    if c.reduce_inside:
        drain(r.rbuf.at[pl.ds(1, DP - 1)], r.rg_send.at[0])
        drain(r.rbuf.at[pl.ds(1, DP - 1)], r.rg_send.at[1])

        @pl.when(goal != ch)
        def _():
            drain(r.rsum, r.rg_send.at[2])

    if c.split_inside:
        for k in range(3):
            drain(r.sin.at[k], r.sg_send.at[0, k])
            drain(r.sp1.at[k], r.sg_send.at[1, k])
            drain(r.sz.at[k, pl.ds(1, Z - 1)], r.sg_send.at[2, k])
            drain(r.sxin.at[k, pl.ds(1, X - 1)], r.sg_send.at[3, k])
            drain(r.so.at[k, pl.ds(1, DP - 1)], r.sg_send.at[4, k])
    drain(r.cv, r.store.at[0])
    drain(r.xv, r.store.at[1])


def hand_over(*refs):
    count = (len(refs) - 1) // 3
    sources, results, places, sems = refs[:count], refs[count : 2 * count], refs[2 * count : -1], refs[-1]
    copies = []
    for source, result, place in zip(sources, results, places):
        rows = source.shape[0]
        parts = 2 if rows >= 1024 else 1
        for p in range(parts):
            at = pl.ds(p * (rows // parts), rows // parts)
            k = len(copies)
            inward = pltpu.make_async_copy(source.at[at], place.at[at], sems.at[k, 0])
            copies.append((inward, pltpu.make_async_copy(place.at[at], result.at[at], sems.at[k, 1])))
            inward.start()
    for inward, outward in copies:
        inward.wait()
        outward.start()
    for inward, outward in copies:
        outward.wait()


ARGS = (
    "inputs", "resolution", "reduce_weight", "first_gain", "first_shift", "split_weight", "second_gain",
    "second_shift", "gate_down", "gate_gain", "gate_shift", "gate_up", "gate_bias", "expand_weight",
    "third_gain", "third_shift", "cotangent",
)


def per_device(*arrays):
    a = dict(zip(ARGS, arrays))
    c = types.SimpleNamespace()
    c.DP, c.CH = lax.axis_size("dp"), lax.axis_size("chan")
    c.X, c.D = c.CH // 2, c.DP * c.CH
    c.images = a["resolution"].shape[0]
    c.ipd = c.images // c.CH
    rows, c.cw = a["inputs"].shape
    c.width = a["reduce_weight"].shape[1]
    c.inner = a["gate_down"].shape[1]
    c.m1, c.m2, c.mg = c.width // c.CH, 2 * c.width // c.CH, c.inner // c.CH
    half, two = c.width // 2, 2 * c.width
    taps = 9 * half
    piece = c.width // c.DP
    piece_type = BF16 if piece % 16 == 0 else F32
    c.reduce_inside = c.DP % c.CH == 0 and piece % 8 == 0
    c.share = taps % (16 * c.DP) == 0 and c.width % (16 * c.DP) == 0
    c.split_inside = c.m2 % (16 * c.DP) == 0 and c.DP % 2 == 0 and c.DP > 2
    own = c.ipd * CELLS
    DP, CH, X, D, ipd, cw, width = c.DP, c.CH, c.X, c.D, c.ipd, c.cw, c.width
    for name in ARGS:
        if a[name].ndim == 1 and name != "resolution":
            a[name] = a[name].reshape(1, -1)
    a["split_weight"] = a["split_weight"].reshape(taps, c.m2)
    sds = jax.ShapeDtypeStruct
    outs = dict(
        block_out=sds((rows, cw), BF16),
        inputs_grad=sds((rows, cw), BF16),
        first_gain_grad=sds((1, c.m1), F32),
        first_shift_grad=sds((1, c.m1), F32),
        second_gain_grad=sds((1, c.m2), F32),
        second_shift_grad=sds((1, c.m2), F32),
        down_grad=sds((c.mg, width), F32),
        gate_gain_grad=sds((1, c.mg), F32),
        gate_shift_grad=sds((1, c.mg), F32),
        up_grad=sds((c.inner, c.m2), F32),
        bias_grad=sds((1, c.m2), F32),
        expand_grad=sds((width, cw), F32),
        third_gain_grad=sds((1, cw), F32),
        third_shift_grad=sds((1, cw), F32),
    )
    if c.reduce_inside:
        outs["reduce_grad"] = sds((c.m1, CH * cw), F32)
    else:
        outs["reduce_part"] = sds((width, cw), F32)
    if c.split_inside:
        outs["split_grad"] = sds((9, half, c.m2), F32)
    else:
        outs["split_part"] = sds((two, taps), F32)
    V = pltpu.VMEM
    dma = lambda *shape: pltpu.SemaphoreType.DMA(shape)
    scratch = dict(
        xv=V((rows, cw), BF16), cv=V((rows, cw), BF16), wr=V((cw, width), BF16), wrt=V((width, cw), BF16),
        wet=V((cw, width), BF16), xt=V((c.images, cw, CELLS), BF16), mt=V((width, rows), BF16),
        maskf=V((rows, LANES), F32), area=V((c.images, LANES), F32), pbuf=V((CH, 8, two), F32),
        red=V((own, width), F32), slope1=V((own, width), F32), xh1=V((rows, width), BF16),
        act=V((2, ipd, TALL, 3 * half), BF16), dsh=V((2, ipd, TALL, 3 * width), BF16),
        wg=V((CH, taps, c.m2), BF16), wx=V((CH, width, cw), BF16), wf=V((2, taps, width), BF16), wt=V((2, 9 * width, half), BF16),
        sp=V((own, two), F32), slope2=V((own, two), F32), act2=V((own, two), F32), share=V((8, LANES), F32),
        gate_x=V((D * 8, LANES), F32), squeezed=V((D * 8, LANES), F32), gate_slope=V((D * 8, LANES), F32),
        grad_down=V((D * 8, LANES), F32), grad_summary=V((8, width), F32), att=V((8, two), F32),
        merged=V((rows, width), BF16), ex=V((rows, cw), F32), acc=V((16, cw), F32),
        dpre=V((rows, cw), F32), de=V((rows, cw), BF16), dm=V((own, width), F32), dh1=V((rows, width), BF16),

        eg=V((width, cw), F32), es=V((width, cw), piece_type), ebuf=V((DP, piece, cw), piece_type),
        eo=V((DP, piece, cw), piece_type), rg=V((cw, width), F32),
        all_send=dma(8), all_recv=dma(8), col_send=dma(4), col_recv=dma(4), row_send=dma(3), row_recv=dma(3),
        rs_core_send=dma(2), rs_core_recv=dma(2, X, ipd), rs_chip_send=dma(2), rs_chip_recv=dma(2, X, ipd),
        ag_core_send=dma(3), ag_core_recv=dma(3, ipd), ag_chip_send=dma(3, X), ag_chip_recv=dma(3, X, ipd),
        ag_pass_send=dma(3, X), ag_pass_recv=dma(3, X, ipd), sh_core_send=dma(2), sh_core_recv=dma(2),
        sh_chip_send=dma(2, X), sh_chip_recv=dma(2, X), sh_col_send=dma(2, X), sh_col_recv=dma(2, X, DP),
        sh_pass_send=dma(2, X), sh_pass_recv=dma(2, X), par_send=dma(1), par_recv=dma(CH),
        eg_send=dma(2), eg_recv=dma(2), rg_send=dma(3), rg_recv=dma(2), sg_send=dma(5, 3), sg_recv=dma(5, 3),
        load=dma(2 + 2 * X), store=dma(2),
    )
    for name, count in (
        ("stage", X), ("inward", X), ("outward", X - 1), ("landed", X - 1), ("inward2", X), ("landed2", X - 1)
    ):
        scratch[name] = V((count, ipd, CELLS, width), BF16)
    for k in range(2, 5):
        scratch[f"g{k}"] = V((D, 8, LANES), F32)
    scratch["g0"] = V((D, 4, LANES), F32)
    scratch["g1"] = V((D, 4, LANES), F32)
    scratch["r4"] = V((CH, 8, LANES), F32)
    scratch["c4"] = V((DP, 8, LANES), F32)
    scratch["g5"] = V((D, 16 * width // LANES, LANES), BF16)
    scratch["told"] = V((16, LANES), F32)
    scratch["slopes"] = V((16 * width // LANES, LANES), F32)
    scratch["back3"] = V((CH, 4, LANES), F32)
    scratch["sums3"] = V((CH, 4, LANES), F32)
    scratch["c1"] = V((DP, 4, LANES), F32)
    scratch["r1"] = V((CH, 4, LANES), F32)
    scratch["r2"] = V((CH, 8, LANES), F32)
    scratch["mix"] = V((width, width), F32)
    scratch["mixb"] = V((width, width), BF16)
    scratch["offset"] = V((16, width), F32)
    scratch["gapt"] = V((width, LANES), F32)
    scratch["downt"] = V((LANES, width), F32)
    scratch["wxt"] = V((CH, cw, width), BF16)
    scratch["c2"] = V((D, 4, LANES), F32)
    scratch["g6"] = V((D, 4, LANES), F32)
    if c.reduce_inside:
        scratch.update(
            rs=V((width, cw), piece_type), rbuf=V((DP, piece, cw), piece_type), rsum=V((piece, cw), piece_type),
            rall=V((DP // CH, CH, piece, cw), piece_type),
        )
    if c.split_inside:
        slab = c.m2 // DP
        scratch.update(
            ss=V((3, 2, X, c.m2, 3 * half), BF16), sin=V((3, X, c.m2, 3 * half), BF16),
            sc=V((3, 2, c.DP // 2, X, slab, 3 * half), BF16), sp1=V((3, c.DP // 2, X, slab, 3 * half), BF16),
            sy=V((3, c.DP // 2, X, slab, 3 * half), BF16), sz=V((3, c.DP // 2, X, slab, 3 * half), BF16),
            sx=V((3, X, slab, 3 * half), BF16), sxin=V((3, X, slab, 3 * half), BF16),
            so=V((3, c.DP, slab, 3 * half), BF16),
        )
    anywhere = pl.BlockSpec(memory_space=pl.ANY)
    vmem = pl.BlockSpec(memory_space=pltpu.VMEM)
    spec = dict(
        inputs=anywhere, cotangent=anywhere, reduce_weight=anywhere, block_out=anywhere, inputs_grad=anywhere,
        resolution=pl.BlockSpec(memory_space=pltpu.SMEM),
    )
    names = tuple(ARGS) + tuple(outs) + tuple(scratch)
    results = pl.pallas_call(
        functools.partial(kernel, c, names),
        out_shape=tuple(outs.values()),
        in_specs=[spec.get(name, vmem) for name in ARGS],
        out_specs=tuple(spec.get(name, vmem) for name in outs),
        scratch_shapes=list(scratch.values()),
        compiler_params=pltpu.CompilerParams(
            collective_id=0, has_side_effects=True, vmem_limit_bytes=62 * 2**20
        ),
        name="block",
    )(*[a[name] for name in ARGS])
    results = pl.pallas_call(
        hand_over,
        out_shape=tuple(outs.values()),
        in_specs=[anywhere] * len(outs),
        out_specs=tuple(anywhere for _ in outs),
        scratch_shapes=[V(v.shape, v.dtype) for v in outs.values()] + [dma(4 * len(outs), 2)],
        compiler_params=pltpu.CompilerParams(vmem_limit_bytes=62 * 2**20),
        name="results",
    )(*results)
    o = dict(zip(outs, results))
    if not c.reduce_inside:
        place = lax.axis_index("chan")
        part = lax.psum(o["reduce_part"], "dp")
        part = lax.all_gather(part, "chan", axis=1, tiled=True)
        o["reduce_grad"] = lax.dynamic_slice_in_dim(part, place * c.m1, c.m1, 0)
    if not c.split_inside:
        place = lax.axis_index("chan")
        part = lax.psum(o["split_part"], ("dp", "chan"))
        part = lax.dynamic_slice_in_dim(part, place * c.m2, c.m2, 0)
        o["split_grad"] = part.T.reshape(9, half, c.m2)
    flat = lambda name: o[name].reshape(-1)
    return (
        o["block_out"], o["inputs_grad"], o["reduce_grad"].T, flat("first_gain_grad"), flat("first_shift_grad"),
        o["split_grad"], flat("second_gain_grad"), flat("second_shift_grad"), o["down_grad"].T,
        flat("gate_gain_grad"), flat("gate_shift_grad"), o["up_grad"], flat("bias_grad"), o["expand_grad"],
        flat("third_gain_grad"), flat("third_shift_grad"),
    )


def solution(mesh):
    placed = (
        P("dp", "chan"), P("dp"), P(), P("chan"), P("chan"), P(None, None, "chan"), P("chan"), P("chan"),
        P(), P(), P(), P(), P(), P(None, "chan"), P("chan"), P("chan"), P("dp", "chan"),
    )
    return jax.shard_map(
        per_device,
        mesh=mesh,
        in_specs=placed,
        out_specs=(
            P("dp", "chan"), P("dp", "chan"), P(None, "chan"), P("chan"), P("chan"), P(None, None, "chan"),
            P("chan"), P("chan"), P(None, "chan"), P("chan"), P("chan"), P(None, "chan"), P("chan"),
            P(None, "chan"), P("chan"), P("chan"),
        ),
        check_vma=False,
    )
```
